128 devices in a mesh: pairs: 32 (over z, x, core), grp: 4 (over y).
Axes of the slice: x: 4, y: 4, z: 4, core: 2. Of those that a mesh axis runs over, the one named last changes fastest.
Arguments:
- coefficients: bfloat16 [512, 512, 128], P('pairs', 'grp'), may hold values from -0.4140625 to 0.4140625
- domain: int32 [512, 512], P('pairs', 'grp'), may hold values from 0 to 767, as said below
- coupling_owner: int32 [512, 8], P('pairs'), may hold values from 0 to 31, all different within a row; in each aligned block of 16 rows (0 to 15, 16 to 31, ...) at most 5 rows name the same one
- coupling_slot: int32 [512, 8], P('pairs'), may hold values from 0 to 15
- coupling_fock: float32 [512, 8], P('pairs'), may hold values from -0.5 to 0.5
- exchange_integrals: float32 [512, 128, 128], P('pairs'), may hold values from -6 to 6
- pno_energy: float32 [512, 128], P('pairs'), may hold values from 0.3 to 3
- pair_shift: float32 [512], P('pairs'), may hold values from 0.4 to 2
- amplitudes_start: float32 [512, 128, 128], P('pairs'), may hold values from -1.8 to 1.8
Outputs:
- amplitudes: float32 [512, 128, 128], P('pairs')
The draws below stay inside these ranges and needn't reach their ends.
Inputs may be any that keep to these rules, and one draw needn't show every extreme that they name: `coupling_owner`: each row names different indices. Among the 16 rows of one index of pairs no value is named more than 5 times, a bound that some block reaches. `domain`: for each pair and each g from 0 to 3, the entries g * 128 to (g + 1) * 128 - 1 are distinct numbers from g * 192 to (g + 1) * 192 - 1.
All inputs are finite; a program needn't handle non-finite values.
Results may differ from the reference program's by a relative error of at most 0.0025.
Values may be sent and summed in bfloat16 or wider, within the bound.
No kernel may reach another device: no remote copies, remote signals or barrier semaphores. Data moves between devices by JAX's collectives and lax.ppermute only.
A program may use at most 128 MiB of HBM per device.

```python
import math
import jax
import jax.numpy as jnp
import numpy as np
from jax import lax

NPNO = 128
DOM = 512
NB = 192
NCPL = 8
ITERS = 2
PAIRS_DEV = 16
NPAIRS = 512
DOMB = 128
MOST = 5
N_PAIRS = 32


def draw_domain(key, part):
    block_count = DOM // DOMB
    pair_keys = jax.random.split(key, NPAIRS * block_count)
    chosen = jax.vmap(lambda item_key: jax.random.permutation(item_key, NB)[:DOMB])(pair_keys)
    chosen = chosen.reshape(NPAIRS, block_count, DOMB).astype(jnp.int32)
    offsets = (jnp.arange(block_count, dtype=jnp.int32) * NB)[None, :, None]
    return (chosen + offsets).reshape(NPAIRS, DOM).astype(jnp.int32)


def touch_ends(entries, key, least, high):
    index_at = [jax.random.randint(jax.random.fold_in(key, axis), (), 0, length) for axis, length in enumerate(entries.shape)]
    longest = entries.shape.index(max(entries.shape))
    next_to = index_at[:longest] + [(index_at[longest] + 1) % entries.shape[longest]] + index_at[longest + 1:]
    return entries.at[tuple(index_at)].set(least).at[tuple(next_to)].set(high)


def steps_of(own_key, extent, pieces, smallest, high):
    level, own = 1.0, jax.random.fold_in(own_key, 6)
    for axis_at, blocks in pieces:
        steps = jnp.exp(jax.random.uniform(jax.random.fold_in(own, axis_at), (blocks,), jnp.float32, smallest / len(pieces), high / len(pieces)))
        level = level * jnp.repeat(steps, extent[axis_at] // blocks).reshape([-1 if axis == axis_at else 1 for axis in range(len(extent))])
    return level


def shared_out(rng, own, number, rows, amount, top, limit, skew):
    order = jax.random.permutation(rng, amount)
    packed, ordinary = shares(amount, rows * top, limit, skew, True), shares(amount, rows * top, limit, skew, False)
    places = jnp.arange(amount)

    def named(tallies, turn):
        used = int((tallies > 0).sum())
        fixed = max(1, used // 4)
        shifted = fixed + (places - fixed + turn * (used - fixed)) % max(1, amount - fixed)
        return jnp.zeros((amount,), jnp.int32).at[order[jnp.where(places < fixed, places, shifted)]].set(jnp.asarray(tallies, jnp.int32))

    tallies = jnp.where(number % 4 == 0, named(packed, number // 4), named(ordinary, number - number // 4 - 1))
    mixed = jax.random.permutation(jax.random.fold_in(own, 3), amount)
    donor, taker = mixed[0:amount // 2 * 2:2], mixed[1:amount // 2 * 2:2]
    room = jnp.minimum(tallies[donor] - 1, limit - tallies[taker]) // 2
    room = jnp.where((donor == order[0]) | (taker == order[0]) | (tallies[taker] == 0), 0, jnp.maximum(room, 0))
    shifted = jax.random.randint(jax.random.fold_in(own, 4), (amount // 2,), 0, 1 << 20) % (room + 1)
    tallies = tallies.at[donor].add(-shifted).at[taker].add(shifted)
    labels = jnp.searchsorted(jnp.cumsum(tallies), jnp.arange(rows * top), side="right").astype(jnp.int32)
    table = labels.reshape(top, rows).T
    table = table[jax.random.permutation(jax.random.fold_in(own, 1), rows)]
    turn = jax.random.randint(jax.random.fold_in(own, 2), (rows, 1), 0, top)
    return jnp.take_along_axis(table, (jnp.arange(top)[None, :] + turn) % top, axis=1)


def shares(count, total, reach, skew, full):
    weights = [(1 << 20) // math.isqrt(standing ** skew) + 1 for standing in range(1, count + 1)]
    largest = reach if full else min(reach, max(-(-total // count), total * weights[0] // sum(weights)))
    least = 1 if total - largest >= count - 1 else 0
    holding, spare = [largest] + [least] * (count - 1), total - largest - least * (count - 1)
    while spare > 0:
        candidates = [i for i in range(1, count) if holding[i] < largest] or [i for i in range(1, count) if holding[i] < reach]
        mass, budget = sum([weights[i] for i in candidates]), spare
        for i in candidates:
            more = min(reach - holding[i], max(1, budget * weights[i] // mass), spare)
            holding[i] = holding[i] + more
            spare = spare - more
    return np.array(holding)


def gaussian(own_key, dims, spread, reach, pieces=(), kind=jnp.bfloat16):
    loudness = steps_of(own_key, dims, pieces, -0.22, 0.18) if pieces else 1.0
    drawn = jax.random.normal(own_key, dims, jnp.float32) * spread * loudness
    return jnp.minimum(jnp.maximum(drawn, -reach), reach).astype(kind)


def setup_inputs(seed: int = 0) -> dict:
    seeds = jax.random.split(jax.random.key(seed), 10)
    coefficients = gaussian(seeds[0], (NPAIRS, DOM, NPNO), ((NPNO * DOM * DOMB / NB) ** -0.25), 0.4140625, ((0, 32), (1, 4)))
    domain = draw_domain(jax.random.fold_in(seeds[9], 71), 0)
    coupling_owner_keys = jax.random.split(jax.random.fold_in(seeds[2], 1), NPAIRS // PAIRS_DEV)
    coupling_owner_turns = jax.random.permutation(jax.random.fold_in(seeds[2], 3), NPAIRS // PAIRS_DEV)
    coupling_owner = jax.vmap(lambda own, number: shared_out(jax.random.fold_in(seeds[2], 2), own, number, PAIRS_DEV, N_PAIRS, NCPL, MOST, 2))(coupling_owner_keys, coupling_owner_turns).reshape((NPAIRS, NCPL))
    coupling_slot = touch_ends(jax.random.randint(seeds[3], (NPAIRS, NCPL), 0, PAIRS_DEV), jax.random.fold_in(seeds[3], 1), 0, PAIRS_DEV - 1).astype(jnp.int32)
    coupling_fock = jnp.clip(jax.random.uniform(seeds[4], (NPAIRS, NCPL), jnp.float32, -0.5, 0.5) * steps_of(seeds[4], (NPAIRS, NCPL), ((0, 32),), -0.4, 0.0), -0.5, 0.5)
    exchange_integrals = gaussian(seeds[5], (NPAIRS, NPNO, NPNO), 1.0, 6.0, ((0, 32),), jnp.float32)
    pno_energy = jnp.clip(jnp.exp(math.log(3.0) - 2.3025851 * jax.random.uniform(seeds[6], (NPAIRS, NPNO), jnp.float32) ** steps_of(seeds[6], (NPAIRS, NPNO), ((0, 32),), -0.2, 0.2)), 0.3, 3.0)
    pair_shift = jnp.clip(jnp.exp(math.log(2.0) - 1.609438 * jax.random.uniform(seeds[7], (NPAIRS,), jnp.float32) ** steps_of(seeds[7], (NPAIRS,), ((0, 32),), -0.2, 0.2)), 0.4, 2.0)
    amplitudes_start = gaussian(seeds[8], (NPAIRS, NPNO, NPNO), 0.3, 1.8, ((0, 32),), jnp.float32)
    return {"coefficients": coefficients, "domain": domain, "coupling_owner": coupling_owner, "coupling_slot": coupling_slot, "coupling_fock": coupling_fock, "exchange_integrals": exchange_integrals, "pno_energy": pno_energy, "pair_shift": pair_shift, "amplitudes_start": amplitudes_start}


def reference(coefficients, domain, coupling_owner, coupling_slot, coupling_fock, exchange_integrals, pno_energy, pair_shift, amplitudes_start):
    pair_count = coefficients.shape[0]
    total_functions = NB * (DOM // DOMB)
    source = (PAIRS_DEV * coupling_owner + coupling_slot).astype(jnp.int32)
    wide = coefficients.astype(jnp.float32)
    expanded = jnp.zeros((pair_count, total_functions, NPNO), jnp.float32)
    expanded = expanded.at[jnp.arange(pair_count, dtype=jnp.int32)[:, None], domain].set(wide)

    def intersection_one(operand):
        coef_target, dom_target, src = operand
        picked_rows = expanded[src][:, dom_target, :]
        product = jnp.einsum("ra,krc->kac", coef_target, picked_rows, precision=lax.Precision.HIGHEST)
        return product.astype(jnp.bfloat16)

    intersection = lax.map(intersection_one, (wide, domain, source))
    denominator = pno_energy[:, :, None] + pno_energy[:, None, :] + pair_shift[:, None, None]
    amplitudes = amplitudes_start
    for iteration in range(ITERS):
        sendable = amplitudes.astype(jnp.bfloat16)

        def couple(operand):
            intersection_target, src, fock_target = operand
            source_amp = sendable[src].astype(jnp.float32)
            intersection_wide = intersection_target.astype(jnp.float32)
            half_proj = jnp.einsum("kac,kcd->kad", intersection_wide, source_amp, precision=lax.Precision.HIGHEST)
            half_proj = lax.optimization_barrier(half_proj.astype(jnp.bfloat16)).astype(jnp.float32)
            projected = jnp.einsum("kad,kbd->kab", half_proj, intersection_wide, precision=lax.Precision.HIGHEST)
            return jnp.sum(fock_target[:, None, None] * projected, axis=0)

        coupled = lax.map(couple, (intersection, source, coupling_fock))
        amplitudes = -(exchange_integrals + coupled) / denominator
    return amplitudes
```

```python
import jax
import jax.numpy as jnp
from jax import lax
from jax.experimental import pallas as pl
from jax.experimental.pallas import tpu as pltpu
from jax.sharding import Mesh, PartitionSpec as P

NB = 192
RANGES = 4
PAIRS = 16
PNO = 128
LINKS = 40
UNROLL = 4
HALF_ROWS = 8 * PNO + 2 * PNO + 16
BF16 = jnp.bfloat16
F32 = jnp.float32
SPLIT = ("z", "x", "core")


def one_hot(row):
    functions = lax.broadcasted_iota(jnp.int32, (NB, PNO), 0).astype(F32)
    return jnp.where(functions == row, 1.0, 0.0).astype(BF16)


def expand_kernel(place, own, other, out, dom):
    for core, ref in enumerate((own, other)):
        for d in range(RANGES):
            dom[core, d] = ref[d, PAIRS * PNO :, :].astype(F32)

    def body(i, carry):
        for core, ref in enumerate((own, other)):
            for d in range(RANGES):
                hot = one_hot(dom[core, d, pl.ds(i, 1), :])
                rows = ref[d, pl.ds(pl.multiple_of(i * PNO, PNO), PNO), :]
                full = jnp.dot(hot, rows, preferred_element_type=F32)
                out[core * PAIRS + i, place[d]] = full.T.astype(BF16)
        return carry

    lax.fori_loop(0, PAIRS, body, 0)


def project(inter, amp, weight):
    half = jnp.dot(inter, amp, preferred_element_type=F32).astype(BF16)
    whole = lax.dot_general(half, inter, (((1,), (1,)), ((), ())), preferred_element_type=F32)
    return weight * whole


def first_kernel(info, fock, *refs):
    a_refs, b_refs, wide = refs[0:4], refs[4:8], refs[8]
    inter, own, other = refs[9:12]
    source, amp, expanded, dom_raw, dom, acc, sem, amp_sem, wide_sem, dom_sem = refs[12:]

    for q in range(4):
        pltpu.make_async_copy(
            wide.at[pl.ds(8 * q, 8)], expanded.at[pl.ds(8 * q, 8)], wide_sem.at[q]
        ).start()
    for r in range(4):
        pltpu.make_async_copy(
            a_refs[r].at[:, pl.ds(10 * PNO, 16)], dom_raw.at[0, r], dom_sem.at[r]
        ).start()
        pltpu.make_async_copy(
            b_refs[r].at[:, pl.ds(10 * PNO, 16)], dom_raw.at[1, r], dom_sem.at[4 + r]
        ).start()

    def fetch(j, carry):
        rx, slot, rz = info[1, j], info[2, j], info[3, j]
        row = pl.multiple_of(lax.rem(slot, 8) * PNO, PNO)
        amp_row = pl.multiple_of(8 * PNO + lax.rem(slot, 2) * PNO, PNO)
        amp_high = lax.rem(slot, 4) >= 2

        @pl.when(slot < 8)
        def _():
            for r in range(4):
                pltpu.make_async_copy(
                    a_refs[r].at[rx, pl.ds(row, PNO)], source.at[j, r], sem.at[j]
                ).start()

        for r in range(4):

            @pl.when((slot >= 8) & (rx == r))
            def _():
                pltpu.make_async_copy(
                    b_refs[r].at[:, pl.ds(row, PNO)], source.at[j], sem.at[j]
                ).start()

            @pl.when(jnp.logical_not(amp_high) & (rz == r))
            def _():
                pltpu.make_async_copy(
                    a_refs[r].at[rx, pl.ds(amp_row, PNO)], amp.at[j], amp_sem.at[j]
                ).start()

            @pl.when(amp_high & (rx == r))
            def _():
                pltpu.make_async_copy(
                    b_refs[r].at[rz, pl.ds(amp_row, PNO)], amp.at[j], amp_sem.at[j]
                ).start()

        return carry

    lax.fori_loop(0, LINKS, fetch, 0)
    acc[...] = jnp.zeros_like(acc)
    for r in range(4):
        for h in range(2):
            pltpu.make_async_copy(
                dom_raw.at[h, r], dom_raw.at[h, r], dom_sem.at[4 * h + r]
            ).wait()
    for r in range(4):
        for x in range(4):
            dom[r, x, 0:8] = dom_raw[0, r, x].astype(F32)[0:8]
            dom[r, x, 8:16] = dom_raw[1, x, r].astype(F32)[0:8]
    for q in range(4):
        pltpu.make_async_copy(
            wide.at[pl.ds(8 * q, 8)], expanded.at[pl.ds(8 * q, 8)], wide_sem.at[q]
        ).wait()

    def body(step, carry):
        for u in range(UNROLL):
            j = step * UNROLL + u
            pltpu.make_async_copy(source.at[j], source.at[j], sem.at[j]).wait()
            pltpu.make_async_copy(amp.at[j], amp.at[j], amp_sem.at[j]).wait()
        for u in range(UNROLL):
            j = step * UNROLL + u
            target, rx, slot = info[0, j], info[1, j], info[2, j]
            parts = []
            for r in range(4):
                hot = one_hot(dom[r, rx, pl.ds(slot, 1), :])
                part = jnp.dot(expanded[target, r], hot, preferred_element_type=F32)
                parts.append(part.astype(BF16))
            picked = jnp.concatenate(parts, axis=1)
            rows = source[j].reshape(4 * PNO, PNO)
            block = jnp.dot(picked, rows, preferred_element_type=F32).astype(BF16)
            inter[j] = block
            acc[target] = acc[target] + project(block, amp[j], fock[0, j])
        return carry

    lax.fori_loop(0, LINKS // UNROLL, body, 0)
    own[...] = acc[0:PAIRS]
    other[...] = acc[PAIRS:]


def next_kernel(info, fock, inter, *refs):
    c_refs = refs[0:4]
    own, other = refs[4:6]
    amp, acc, amp_sem = refs[6:]

    def fetch(j, carry):
        rx, slot, rz = info[1, j], info[2, j], info[3, j]
        row = pl.multiple_of(lax.rem(slot, 4) * PNO, PNO)
        for r in range(4):

            @pl.when(rz == r)
            def _():
                pltpu.make_async_copy(
                    c_refs[r].at[rx, pl.ds(row, PNO)], amp.at[j], amp_sem.at[j]
                ).start()

        return carry

    lax.fori_loop(0, LINKS, fetch, 0)
    acc[...] = jnp.zeros_like(acc)

    def body(step, carry):
        for u in range(UNROLL):
            j = step * UNROLL + u
            pltpu.make_async_copy(amp.at[j], amp.at[j], amp_sem.at[j]).wait()
        for u in range(UNROLL):
            j = step * UNROLL + u
            target = info[0, j]
            acc[target] = acc[target] + project(inter[j], amp[j], fock[0, j])
        return carry

    lax.fori_loop(0, LINKS // UNROLL, body, 0)
    own[...] = acc[0:PAIRS]
    other[...] = acc[PAIRS:]


VM = pl.BlockSpec(memory_space=pltpu.VMEM)
SM = pl.BlockSpec(memory_space=pltpu.SMEM)
HB = pl.BlockSpec(memory_space=pl.ANY)
PARAMS = pltpu.CompilerParams(vmem_limit_bytes=48 * 1024 * 1024)
BLOCK = jax.ShapeDtypeStruct((PAIRS, PNO, PNO), F32)


def shifted(value, axis, rel):
    return lax.ppermute(value, axis, [((i + rel) % 4, i) for i in range(4)])


def ring(value, axis):
    plus, minus = shifted(value, axis, 1), shifted(value, axis, 3)
    return [value, plus, shifted(value, axis, 2), minus]


def swap_core(value):
    return lax.ppermute(value, "core", [(0, 1), (1, 0)])


def to_class_plane(value):
    moves = []
    for z in range(4):
        for core in range(2):
            for y in range(4):
                moves.append(
                    ((z * 2 + core) * 4 + y, (y * 2 + core) * 4 + (z + 2 * core) % 4)
                )
    return lax.ppermute(value, ("z", "core", "grp"), moves)


def reduce_core_y(own, other, y):
    total = own + swap_core(other)
    pieces = [lax.dynamic_slice_in_dim(total, 4 * ((y + d) % 4), 4, 0) for d in range(4)]
    result = pieces[0]
    for d in (1, 3, 2):
        result = result + shifted(pieces[d], "grp", 4 - d)
    return result


def on_device(
    coefficients,
    domain,
    coupling_owner,
    coupling_slot,
    coupling_fock,
    exchange_integrals,
    pno_energy,
    pair_shift,
    amplitudes_start,
):
    z, x, core, y = [lax.axis_index(name) for name in ("z", "x", "core", "grp")]
    flat = coefficients.reshape(PAIRS * PNO, PNO)
    local = (domain - y * NB).astype(BF16)
    none = jnp.zeros((8, PNO), BF16)
    start = lax.dynamic_slice_in_dim(amplitudes_start, 4 * y, 4, 0).astype(BF16)
    start = start.reshape(4 * PNO, PNO)
    half_a = jnp.concatenate([flat[: 8 * PNO], start[: 2 * PNO], local[:8], none])
    half_b = jnp.concatenate([flat[8 * PNO :], start[2 * PNO :], local[8:], none])
    half_a = to_class_plane(half_a)
    half_b = to_class_plane(half_b)
    a_refs = ring(jnp.stack(ring(half_a, "x")), "z")
    b_refs = ring(jnp.stack(ring(half_b, "z")), "x")

    targets = jnp.stack(ring(jnp.concatenate([flat, local]), "grp"))
    other_targets = swap_core(targets)
    place = ((y - z + jnp.arange(4, dtype=jnp.int32)) % 4).astype(jnp.int32)
    expanded = pl.pallas_call(
        expand_kernel,
        out_shape=jax.ShapeDtypeStruct((2 * PAIRS, RANGES, PNO, NB), BF16),
        in_specs=[SM, VM, VM],
        out_specs=VM,
        scratch_shapes=[pltpu.VMEM((2, RANGES, PAIRS, PNO), F32)],
        compiler_params=PARAMS,
        name="expand_targets",
    )(place, targets, other_targets)

    table = jnp.stack(
        [(coupling_owner * PAIRS + coupling_slot).astype(F32), coupling_fock]
    )
    table = jnp.concatenate([table, swap_core(table)], axis=1).reshape(2, -1)
    named = table[0].astype(jnp.int32)
    slots, owners = named % PAIRS, named // PAIRS
    mine = (owners % 2 == core) & (owners // 8 == (y + 2 * core) % 4)
    order = jnp.cumsum(mine.astype(jnp.int32)) - 1
    hit = mine[None, :] & (order[None, :] == jnp.arange(LINKS, dtype=jnp.int32)[:, None])
    target_of = jnp.arange(2 * PAIRS * 8, dtype=jnp.int32) // 8
    columns = jnp.stack(
        [target_of, ((owners // 2) % 4 - x) % 4, slots, (slots // 4 - z) % 4]
    )
    info = jnp.sum(jnp.where(hit[None], columns[:, None, :], 0), axis=2).astype(jnp.int32)
    fock = jnp.sum(jnp.where(hit, table[1][None, :], 0.0), axis=1)[None, :]

    inter, own, other = pl.pallas_call(
        first_kernel,
        out_shape=(jax.ShapeDtypeStruct((LINKS, PNO, PNO), BF16), BLOCK, BLOCK),
        in_specs=[SM, SM] + [HB] * 9,
        out_specs=(VM, VM, VM),
        scratch_shapes=[
            pltpu.VMEM((LINKS, RANGES, PNO, PNO), BF16),
            pltpu.VMEM((LINKS, PNO, PNO), BF16),
            pltpu.VMEM((2 * PAIRS, RANGES, PNO, NB), BF16),
            pltpu.VMEM((2, 4, 4, 16, PNO), BF16),
            pltpu.VMEM((4, 4, PAIRS, PNO), F32),
            pltpu.VMEM((2 * PAIRS, PNO, PNO), F32),
            pltpu.SemaphoreType.DMA((LINKS,)),
            pltpu.SemaphoreType.DMA((LINKS,)),
            pltpu.SemaphoreType.DMA((4,)),
            pltpu.SemaphoreType.DMA((8,)),
        ],
        compiler_params=PARAMS,
        name="intersect_and_project",
    )(info, fock, *a_refs, *b_refs, expanded)

    energy = lax.dynamic_slice_in_dim(pno_energy, 4 * y, 4, 0)
    shift = lax.dynamic_slice_in_dim(pair_shift, 4 * y, 4, 0)
    exchange = lax.dynamic_slice_in_dim(exchange_integrals, 4 * y, 4, 0)
    denominator = energy[:, :, None] + energy[:, None, :] + shift[:, None, None]

    amplitudes = -(exchange + reduce_core_y(own, other, y)) / denominator
    sent = to_class_plane(amplitudes.astype(BF16).reshape(4 * PNO, PNO))
    c_refs = ring(jnp.stack(ring(sent, "x")), "z")
    own, other = pl.pallas_call(
        next_kernel,
        out_shape=(BLOCK, BLOCK),
        in_specs=[SM, SM, VM] + [HB] * 4,
        out_specs=(VM, VM),
        scratch_shapes=[
            pltpu.VMEM((LINKS, PNO, PNO), BF16),
            pltpu.VMEM((2 * PAIRS, PNO, PNO), F32),
            pltpu.SemaphoreType.DMA((LINKS,)),
        ],
        compiler_params=PARAMS,
        name="project",
    )(info, fock, inter, *c_refs)
    amplitudes = -(exchange + reduce_core_y(own, other, y)) / denominator
    gathered = ring(amplitudes, "grp")
    result = jnp.zeros_like(exchange_integrals)
    for d in range(4):
        result = lax.dynamic_update_slice_in_dim(result, gathered[d], 4 * ((y + d) % 4), 0)
    return result


def solution(mesh):
    fine = Mesh(mesh.devices.reshape(4, 4, 2, 4), ("z", "x", "core", "grp"))
    placed = (
        P(SPLIT, "grp", None),
        P(SPLIT, "grp"),
        P(SPLIT, None),
        P(SPLIT, None),
        P(SPLIT, None),
        P(SPLIT, None, None),
        P(SPLIT, None),
        P(SPLIT),
        P(SPLIT, None, None),
    )
    return jax.shard_map(
        on_device, mesh=fine, in_specs=placed, out_specs=P(SPLIT, None, None), check_vma=False
    )
```

```python
import jax
import jax.numpy as jnp
from jax import lax
from jax.experimental import pallas as pl
from jax.experimental.pallas import tpu as pltpu
from jax.sharding import Mesh, PartitionSpec as P

NB = 192
RANGES = 4
PAIRS = 16
PNO = 128
LINKS = 40
UNROLL = 8
HALF = 8 * PNO
BF16 = jnp.bfloat16
F32 = jnp.float32
SPLIT = ("z", "x", "core")
TARGET, REL_X, SLOT, REL_Z, ABS_X = range(5)


def one_hot(row):
    functions = lax.broadcasted_iota(jnp.int32, (NB, PNO), 0).astype(F32)
    return jnp.where(functions == row, 1.0, 0.0).astype(BF16)


def pick_kernel(info, place, own, other, domains, picked, expanded, dom, source_dom):
    for core, ref in enumerate((own, other)):
        for d in range(RANGES):
            dom[core, d] = ref[d, PAIRS * PNO :, :].astype(F32)
    for i in range(RANGES):
        for r in range(RANGES):
            source_dom[i, r] = domains[place[8], i, r].astype(F32)

    def expand(i, carry):
        for core, ref in enumerate((own, other)):
            for r in range(RANGES):
                d = place[4 + r]
                hot = one_hot(dom[core, d, pl.ds(i, 1), :])
                rows = ref[d, pl.ds(pl.multiple_of(i * PNO, PNO), PNO), :]
                full = jnp.dot(hot, rows, preferred_element_type=F32)
                expanded[core * PAIRS + i, r] = full.T.astype(BF16)
        return carry

    lax.fori_loop(0, PAIRS, expand, 0)

    def pick(step, carry):
        for u in range(4):
            j = step * 4 + u
            for r in range(RANGES):
                row = source_dom[info[ABS_X, j], place[r], pl.ds(info[SLOT, j], 1), :]
                part = jnp.dot(
                    expanded[info[TARGET, j], r], one_hot(row), preferred_element_type=F32
                )
                picked[j, :, r * PNO : (r + 1) * PNO] = part.astype(BF16)
        return carry

    lax.fori_loop(0, LINKS // 4, pick, 0)


def fetch_amplitudes(info, j, a_refs, b_refs, first, amp):
    rx, slot, rz = info[REL_X, j], info[SLOT, j], info[REL_Z, j]
    rows = pl.ds(pl.multiple_of(first + lax.rem(slot, 2) * PNO, PNO), PNO)
    high = lax.rem(slot, 4) >= 2
    for r in range(4):

        @pl.when(jnp.logical_not(high) & (rz == r))
        def _():
            amp[j] = a_refs[r][rx, rows, :]

        @pl.when(high & (rx == r))
        def _():
            amp[j] = b_refs[r][rz, rows, :]


def project(inter, amp, weight):
    half = jnp.dot(inter, amp, preferred_element_type=F32).astype(BF16)
    whole = lax.dot_general(half, inter, (((1,), (1,)), ((), ())), preferred_element_type=F32)
    return weight * whole


def first_kernel(info, fock, *refs):
    a_refs, b_refs, picked = refs[0:4], refs[4:8], refs[8]
    inter, own, other = refs[9:12]
    source, amp, acc = refs[12:]

    def fetch(j, carry):
        rx, slot = info[REL_X, j], info[SLOT, j]
        rows = pl.ds(pl.multiple_of(lax.rem(slot, 8) * PNO, PNO), PNO)

        @pl.when(slot < 8)
        def _():
            for r in range(4):
                source[j, r] = a_refs[r][rx, rows, :]

        for x in range(4):

            @pl.when((slot >= 8) & (rx == x))
            def _():
                for r in range(4):
                    source[j, r] = b_refs[x][r, rows, :]

        fetch_amplitudes(info, j, a_refs, b_refs, HALF, amp)
        return carry

    lax.fori_loop(0, LINKS, fetch, 0)
    acc[...] = jnp.zeros_like(acc)

    def body(step, carry):
        for u in range(UNROLL):
            j = step * UNROLL + u
            rows = source[j].reshape(RANGES * PNO, PNO)
            block = jnp.dot(picked[j], rows, preferred_element_type=F32).astype(BF16)
            inter[j] = block
            target = info[TARGET, j]
            acc[target] = acc[target] + project(block, amp[j], fock[0, j])
        return carry

    lax.fori_loop(0, LINKS // UNROLL, body, 0)
    own[...] = acc[0:PAIRS]
    other[...] = acc[PAIRS:].astype(other.dtype)


def next_kernel(info, fock, inter, *refs):
    a_refs, b_refs = refs[0:4], refs[4:8]
    own, other = refs[8:10]
    amp, acc = refs[10:]

    def fetch(j, carry):
        fetch_amplitudes(info, j, a_refs, b_refs, 0, amp)
        return carry

    lax.fori_loop(0, LINKS, fetch, 0)
    acc[...] = jnp.zeros_like(acc)

    def body(step, carry):
        for u in range(UNROLL):
            j = step * UNROLL + u
            target = info[TARGET, j]
            acc[target] = acc[target] + project(inter[j], amp[j], fock[0, j])
        return carry

    lax.fori_loop(0, LINKS // UNROLL, body, 0)
    own[...] = acc[0:PAIRS]
    other[...] = acc[PAIRS:].astype(other.dtype)


VM = pl.BlockSpec(memory_space=pltpu.VMEM)
SM = pl.BlockSpec(memory_space=pltpu.SMEM)


def params(mib):
    return pltpu.CompilerParams(vmem_limit_bytes=mib * 1024 * 1024)


BLOCK = jax.ShapeDtypeStruct((PAIRS, PNO, PNO), F32)


def shifted(value, axis, rel):
    return lax.ppermute(value, axis, [((i + rel) % 4, i) for i in range(4)])


def ring(value, axis):
    plus, minus = shifted(value, axis, 1), shifted(value, axis, 3)
    return [value, plus, shifted(value, axis, 2), minus]


def swap_core(value):
    return lax.ppermute(value, "core", [(0, 1), (1, 0)])


def to_class_plane(value):
    moves = []
    for z in range(4):
        for core in range(2):
            for y in range(4):
                moves.append(
                    ((z * 2 + core) * 4 + y, (y * 2 + core) * 4 + (z + 2 * core) % 4)
                )
    return lax.ppermute(value, ("z", "core", "grp"), moves)


def plane_gather(half_a, half_b):
    a, b = lax.optimization_barrier(
        (jnp.stack(ring(half_a, "x")), jnp.stack(ring(half_b, "z")))
    )
    return ring(a, "z"), ring(b, "x")


def reduce_core_y(own, other, y):
    total = own + swap_core(other)
    pieces = [lax.dynamic_slice_in_dim(total, 4 * ((y + d) % 4), 4, 0) for d in range(4)]
    result = pieces[0]
    for d in (1, 3, 2):
        result = result + shifted(pieces[d], "grp", 4 - d)
    return result


def on_device(
    coefficients,
    domain,
    coupling_owner,
    coupling_slot,
    coupling_fock,
    exchange_integrals,
    pno_energy,
    pair_shift,
    amplitudes_start,
):
    z, x, core, y = [lax.axis_index(name) for name in ("z", "x", "core", "grp")]
    class_z = (y + 2 * core) % 4
    flat = coefficients.reshape(PAIRS * PNO, PNO)
    local = (domain - y * NB).astype(BF16)
    start = lax.dynamic_slice_in_dim(amplitudes_start, 4 * y, 4, 0).astype(BF16)
    start = start.reshape(4 * PNO, PNO)
    domains = lax.all_gather(local, ("z", "x", "grp")).reshape(4, 4, RANGES, PAIRS, PNO)
    half_a = to_class_plane(jnp.concatenate([flat[:HALF], start[: 2 * PNO]]))
    half_b = to_class_plane(jnp.concatenate([flat[HALF:], start[2 * PNO :]]))

    table = jnp.stack(
        [(coupling_owner * PAIRS + coupling_slot).astype(F32), coupling_fock]
    )
    table = jnp.concatenate([table, swap_core(table)], axis=1).reshape(2, -1)
    named = table[0].astype(jnp.int32)
    slots, owners = named % PAIRS, named // PAIRS
    owner_x = (owners // 2) % 4
    mine = (owners % 2 == core) & (owners // 8 == class_z)
    order = jnp.cumsum(mine.astype(jnp.int32)) - 1
    hit = mine[None, :] & (order[None, :] == jnp.arange(LINKS, dtype=jnp.int32)[:, None])
    target_of = jnp.arange(2 * PAIRS * 8, dtype=jnp.int32) // 8
    columns = jnp.stack(
        [target_of, (owner_x - x) % 4, slots, (slots // 4 - z) % 4, owner_x]
    )
    info = jnp.sum(jnp.where(hit[None], columns[:, None, :], 0), axis=2).astype(jnp.int32)
    fock = jnp.sum(jnp.where(hit, table[1][None, :], 0.0), axis=1)[None, :]

    own_targets = jnp.concatenate([flat, local])
    half_a, half_b, own_targets = lax.optimization_barrier((half_a, half_b, own_targets))
    targets = jnp.stack(ring(own_targets, "grp"))
    a_refs, b_refs = plane_gather(half_a, half_b)
    other_targets = swap_core(targets)
    ranges = (z + jnp.arange(4, dtype=jnp.int32)) % 4
    place = jnp.concatenate([ranges, (ranges - y) % 4, class_z[None]]).astype(jnp.int32)
    picked = pl.pallas_call(
        pick_kernel,
        out_shape=jax.ShapeDtypeStruct((LINKS, PNO, RANGES * PNO), BF16),
        in_specs=[SM, SM, VM, VM, VM],
        out_specs=VM,
        scratch_shapes=[
            pltpu.VMEM((2 * PAIRS, RANGES, PNO, NB), BF16),
            pltpu.VMEM((2, RANGES, PAIRS, PNO), F32),
            pltpu.VMEM((4, RANGES, PAIRS, PNO), F32),
        ],
        compiler_params=params(24),
        name="pick_targets",
    )(info, place, targets, other_targets, domains)

    inter, own, other = pl.pallas_call(
        first_kernel,
        out_shape=(jax.ShapeDtypeStruct((LINKS, PNO, PNO), BF16), BLOCK, BLOCK),
        in_specs=[SM, SM] + [VM] * 9,
        out_specs=(VM, VM, VM),
        scratch_shapes=[
            pltpu.VMEM((LINKS, RANGES, PNO, PNO), BF16),
            pltpu.VMEM((LINKS, PNO, PNO), BF16),
            pltpu.VMEM((2 * PAIRS, PNO, PNO), F32),
        ],
        compiler_params=params(36),
        name="intersect_and_project",
    )(info, fock, *a_refs, *b_refs, picked)

    energy = lax.dynamic_slice_in_dim(pno_energy, 4 * y, 4, 0)
    shift = lax.dynamic_slice_in_dim(pair_shift, 4 * y, 4, 0)
    exchange = lax.dynamic_slice_in_dim(exchange_integrals, 4 * y, 4, 0)
    denominator = energy[:, :, None] + energy[:, None, :] + shift[:, None, None]

    amplitudes = -(exchange + reduce_core_y(own, other, y)) / denominator
    sent = to_class_plane(amplitudes.astype(BF16).reshape(4 * PNO, PNO))
    a_refs, b_refs = plane_gather(sent[: 2 * PNO], sent[2 * PNO :])
    own, other = pl.pallas_call(
        next_kernel,
        out_shape=(BLOCK, BLOCK),
        in_specs=[SM, SM] + [VM] * 9,
        out_specs=(VM, VM),
        scratch_shapes=[
            pltpu.VMEM((LINKS, PNO, PNO), BF16),
            pltpu.VMEM((2 * PAIRS, PNO, PNO), F32),
        ],
        compiler_params=params(20),
        name="project",
    )(info, fock, inter, *a_refs, *b_refs)
    amplitudes = -(exchange + reduce_core_y(own, other, y)) / denominator
    gathered = ring(amplitudes, "grp")
    result = jnp.zeros_like(exchange_integrals)
    for d in range(4):
        result = lax.dynamic_update_slice_in_dim(result, gathered[d], 4 * ((y + d) % 4), 0)
    return result


def solution(mesh):
    fine = Mesh(mesh.devices.reshape(4, 4, 2, 4), ("z", "x", "core", "grp"))
    placed = (
        P(SPLIT, "grp", None),
        P(SPLIT, "grp"),
        P(SPLIT, None),
        P(SPLIT, None),
        P(SPLIT, None),
        P(SPLIT, None, None),
        P(SPLIT, None),
        P(SPLIT),
        P(SPLIT, None, None),
    )
    return jax.shard_map(
        on_device, mesh=fine, in_specs=placed, out_specs=P(SPLIT, None, None), check_vma=False
    )
```

```python
import jax
import jax.numpy as jnp
from jax import lax
from jax.experimental import pallas as pl
from jax.experimental.pallas import tpu as pltpu
from jax.sharding import Mesh, PartitionSpec as P

NB = 192
RANGES = 4
PAIRS = 16
PNO = 128
LINKS = 40
UNROLL = 8
ORBITALS = 4 * PNO
COLOUR = ORBITALS + PNO
EVEN = [(0, 1), (1, 0), (2, 3), (3, 2)]
ODD = [(1, 2), (2, 1), (3, 0), (0, 3)]
STEPS = (
    (("x", EVEN), ("z", EVEN), ("x", ODD), ("z", ODD)),
    (("z", EVEN), ("x", EVEN), ("z", ODD), ("x", ODD)),
    (("x", ODD), ("z", ODD), ("x", EVEN), ("z", EVEN)),
    (("z", ODD), ("x", ODD), ("z", EVEN), ("x", EVEN)),
)
BF16 = jnp.bfloat16
F32 = jnp.float32
SPLIT = ("z", "x", "core")
TARGET, SLOT, ABS_X, REL_X, REL_Z, X_EVEN, X_ODD, AMP_LIST, AMP_AT = range(9)


def one_hot(row):
    functions = lax.broadcasted_iota(jnp.int32, (NB, PNO), 0).astype(F32)
    return jnp.where(functions == row, 1.0, 0.0).astype(BF16)


def pick_kernel(info, place, targets, domains, picked, expanded, dom, source_dom):
    for i in range(2 * RANGES):
        dom[i] = targets[i, PAIRS * PNO :, :].astype(F32)
    for r in range(RANGES):
        for i in range(4):
            source_dom[r, i] = domains[r, i].astype(F32)

    def expand(i, carry):
        for block in range(2):
            for r in range(RANGES):
                d = place[4 + 4 * block + r]
                hot = one_hot(dom[d, pl.ds(i, 1), :])
                rows = targets[d, pl.ds(pl.multiple_of(i * PNO, PNO), PNO), :]
                full = jnp.dot(hot, rows, preferred_element_type=F32)
                expanded[block * PAIRS + i, r] = full.T.astype(BF16)
        return carry

    lax.fori_loop(0, PAIRS, expand, 0)

    def pick(step, carry):
        for u in range(4):
            j = step * 4 + u
            for r in range(RANGES):
                row = source_dom[place[r], info[ABS_X, j], pl.ds(info[SLOT, j], 1), :]
                part = jnp.dot(
                    expanded[info[TARGET, j], r], one_hot(row), preferred_element_type=F32
                )
                picked[j, :, r * PNO : (r + 1) * PNO] = part.astype(BF16)
        return carry

    lax.fori_loop(0, LINKS // 4, pick, 0)


def fetch_amplitudes(info, j, a_refs, b_refs, amp):
    rx, slot, rz = info[REL_X, j], info[SLOT, j], info[REL_Z, j]
    rows = pl.ds(pl.multiple_of(lax.rem(slot, 2) * PNO, PNO), PNO)
    high = lax.rem(slot, 4) >= 2
    for r in range(4):

        @pl.when(jnp.logical_not(high) & (rz == r))
        def _():
            amp[j] = a_refs[r][rx, rows, :]

        @pl.when(high & (rx == r))
        def _():
            amp[j] = b_refs[r][rz, rows, :]


def project(inter, amp, weight):
    half = jnp.dot(inter, amp, preferred_element_type=F32).astype(BF16)
    whole = lax.dot_general(half, inter, (((1,), (1,)), ((), ())), preferred_element_type=F32)
    return weight * whole


def first_kernel(info, fock, *refs):
    lists, picked = refs[0:8], refs[8]
    inter, own, other = refs[9:12]
    source, amp, acc, sem, amp_sem = refs[12:]

    def fetch(j, carry):
        slot, even, odd = info[SLOT, j], info[X_EVEN, j], info[X_ODD, j]
        colour = lax.div(slot, 4)
        rows = pl.ds(pl.multiple_of(lax.rem(slot, 4) * PNO, PNO), PNO)

        def copy(src, dst):
            pltpu.make_async_copy(src, dst, sem.at[j]).start()

        @pl.when(colour == 0)
        def _():
            for bit in range(2):
                copy(lists[bit].at[odd, :, even, rows], source.at[j, bit])

        @pl.when(colour == 2)
        def _():
            for bit in range(2):
                copy(lists[4 + bit].at[even, :, odd, rows], source.at[j, :, bit])

        for last in range(2):

            @pl.when((colour == 1) & (odd == last))
            def _():
                copy(lists[2 + last].at[:, even, :, rows], source.at[j])

            @pl.when((colour == 3) & (even == last))
            def _():
                for bit in range(2):
                    copy(lists[6 + last].at[bit, odd, :, rows], source.at[j, :, bit])

        at = info[AMP_AT, j]
        for i in range(8):

            @pl.when(info[AMP_LIST, j] == i)
            def _():
                pltpu.make_async_copy(
                    lists[i].at[
                        lax.div(at, 4), lax.rem(lax.div(at, 2), 2), lax.rem(at, 2),
                        pl.ds(ORBITALS, PNO),
                    ],
                    amp.at[j],
                    amp_sem.at[j],
                ).start()

        return carry

    lax.fori_loop(0, LINKS, fetch, 0)
    acc[...] = jnp.zeros_like(acc)

    def body(step, carry):
        for u in range(UNROLL):
            j = step * UNROLL + u
            pltpu.make_async_copy(source.at[j], source.at[j], sem.at[j]).wait()
            pltpu.make_async_copy(amp.at[j], amp.at[j], amp_sem.at[j]).wait()
        for u in range(UNROLL):
            j = step * UNROLL + u
            rows = source[j].reshape(RANGES * PNO, PNO)
            block = jnp.dot(picked[j], rows, preferred_element_type=F32).astype(BF16)
            inter[j] = block
            target = info[TARGET, j]
            acc[target] = acc[target] + project(block, amp[j], fock[0, j])
        return carry

    lax.fori_loop(0, LINKS // UNROLL, body, 0)
    own[...] = acc[0:PAIRS]
    other[...] = acc[PAIRS:].astype(other.dtype)


def next_kernel(info, fock, inter, *refs):
    a_refs, b_refs = refs[0:4], refs[4:8]
    own, other = refs[8:10]
    amp, acc = refs[10:]

    def fetch(j, carry):
        fetch_amplitudes(info, j, a_refs, b_refs, amp)
        return carry

    lax.fori_loop(0, LINKS, fetch, 0)
    acc[...] = jnp.zeros_like(acc)

    def body(step, carry):
        for u in range(UNROLL):
            j = step * UNROLL + u
            target = info[TARGET, j]
            acc[target] = acc[target] + project(inter[j], amp[j], fock[0, j])
        return carry

    lax.fori_loop(0, LINKS // UNROLL, body, 0)
    own[...] = acc[0:PAIRS]
    other[...] = acc[PAIRS:].astype(other.dtype)


VM = pl.BlockSpec(memory_space=pltpu.VMEM)
SM = pl.BlockSpec(memory_space=pltpu.SMEM)
HB = pl.BlockSpec(memory_space=pl.ANY)


def params(mib):
    return pltpu.CompilerParams(vmem_limit_bytes=mib * 1024 * 1024)


BLOCK = jax.ShapeDtypeStruct((PAIRS, PNO, PNO), F32)


def shifted(value, axis, rel):
    return lax.ppermute(value, axis, [((i + rel) % 4, i) for i in range(4)])


def ring(value, axis):
    plus, minus = shifted(value, axis, 1), shifted(value, axis, 3)
    return [value, plus, shifted(value, axis, 2), minus]


def swap_core(value):
    return lax.ppermute(value, "core", [(0, 1), (1, 0)])


def to_class_plane(value):
    moves = []
    for z in range(4):
        for core in range(2):
            for y in range(4):
                moves.append(
                    ((z * 2 + core) * 4 + y, (y * 2 + core) * 4 + (z + 2 * core) % 4)
                )
    return lax.ppermute(value, ("z", "core", "grp"), moves)


def ways(rel, here):
    lean = 1 + 2 * (here % 2)
    even = (rel == 2) | (rel == lean)
    odd = (rel == 2) | (rel == 4 - lean)
    return even.astype(jnp.int32), odd.astype(jnp.int32)


def plane_gather(half_a, half_b):
    a, b = lax.optimization_barrier(
        (jnp.stack(ring(half_a, "x")), jnp.stack(ring(half_b, "z")))
    )
    return ring(a, "z"), ring(b, "x")


def reduce_core_y(own, other, y):
    total = own + swap_core(other)
    pieces = [lax.dynamic_slice_in_dim(total, 4 * ((y + d) % 4), 4, 0) for d in range(4)]
    result = pieces[0]
    for d in (1, 3, 2):
        result = result + shifted(pieces[d], "grp", 4 - d)
    return result


def on_device(
    coefficients,
    domain,
    coupling_owner,
    coupling_slot,
    coupling_fock,
    exchange_integrals,
    pno_energy,
    pair_shift,
    amplitudes_start,
):
    z, x, core, y = [lax.axis_index(name) for name in ("z", "x", "core", "grp")]
    class_z = (y + 2 * core) % 4
    flat = coefficients.reshape(PAIRS * PNO, PNO)
    local = (domain - y * NB).astype(BF16)
    start = lax.dynamic_slice_in_dim(amplitudes_start, 4 * y, 4, 0).astype(BF16)
    start = start.reshape(4 * PNO, PNO)
    own_targets = jnp.concatenate([flat, local])
    targets = lax.all_gather(own_targets, ("core", "grp"))
    colours = [
        to_class_plane(
            jnp.concatenate(
                [flat[k * ORBITALS : (k + 1) * ORBITALS], start[k * PNO : (k + 1) * PNO]]
            )
        )[None]
        for k in range(4)
    ]
    local = to_class_plane(local)

    table = jnp.stack(
        [(coupling_owner * PAIRS + coupling_slot).astype(F32), coupling_fock]
    )
    table = jnp.concatenate([table, swap_core(table)], axis=1).reshape(2, -1)
    named = table[0].astype(jnp.int32)
    slots, owners = named % PAIRS, named // PAIRS
    owner_x = (owners // 2) % 4
    mine = (owners % 2 == core) & (owners // 8 == class_z)
    order = jnp.cumsum(mine.astype(jnp.int32)) - 1
    hit = mine[None, :] & (order[None, :] == jnp.arange(LINKS, dtype=jnp.int32)[:, None])
    target_of = jnp.arange(2 * PAIRS * 8, dtype=jnp.int32) // 8
    x_even, x_odd = ways((owner_x - x) % 4, x)
    z_even, z_odd = ways((slots // 4 - z) % 4, z)
    bits = (
        (x_even, z_even, x_odd, z_odd),
        (z_even, x_even, z_odd, x_odd),
        (x_odd, z_odd, x_even, z_even),
        (z_odd, x_odd, z_even, x_even),
    )
    amp_list, amp_at = jnp.zeros_like(slots), jnp.zeros_like(slots)
    for k in range(4):
        b = bits[k]
        amp_list = jnp.where(slots % 4 == k, 2 * k + b[3], amp_list)
        amp_at = jnp.where(slots % 4 == k, b[0] + 2 * b[1] + 4 * b[2], amp_at)
    columns = jnp.stack(
        [
            target_of, slots, owner_x, (owner_x - x) % 4, (slots // 4 - z) % 4,
            x_even, x_odd, amp_list, amp_at,
        ]
    )
    info = jnp.sum(jnp.where(hit[None], columns[:, None, :], 0), axis=2).astype(jnp.int32)
    fock = jnp.sum(jnp.where(hit, table[1][None, :], 0.0), axis=1)[None, :]

    for step in range(4):
        got = [lax.ppermute(colours[k], *STEPS[k][step]) for k in range(4)]
        if step == 3:
            break
        colours = [jnp.concatenate([colours[k], got[k]]) for k in range(4)]
        if step == 1:
            *colours, local = lax.optimization_barrier((*colours, local))
            everywhere = jnp.broadcast_to(local[None], (16, PAIRS, PNO))
            domains = lax.all_to_all(everywhere, ("z", "x"), 0, 0, tiled=True)
        elif step == 2:
            *colours, domains = lax.optimization_barrier((*colours, domains))
        else:
            colours = list(lax.optimization_barrier(tuple(colours)))
    lists = []
    for k in range(4):
        lists.append(colours[k].reshape(2, 2, 2, COLOUR, PNO))
        lists.append(got[k].reshape(2, 2, 2, COLOUR, PNO))

    lean = 1 - 2 * (z % 2)
    ranges = jnp.stack([z, z + lean, z - lean, z + 2]) % 4
    place = jnp.concatenate([ranges, 4 * core + ranges, 4 * (1 - core) + ranges])
    picked = pl.pallas_call(
        pick_kernel,
        out_shape=jax.ShapeDtypeStruct((LINKS, PNO, RANGES * PNO), BF16),
        in_specs=[SM, SM, VM, VM],
        out_specs=VM,
        scratch_shapes=[
            pltpu.VMEM((2 * PAIRS, RANGES, PNO, NB), BF16),
            pltpu.VMEM((2 * RANGES, PAIRS, PNO), F32),
            pltpu.VMEM((RANGES, 4, PAIRS, PNO), F32),
        ],
        compiler_params=params(24),
        name="pick_targets",
    )(info, place.astype(jnp.int32), targets, domains.reshape(RANGES, 4, PAIRS, PNO))

    inter, own, other = pl.pallas_call(
        first_kernel,
        out_shape=(jax.ShapeDtypeStruct((LINKS, PNO, PNO), BF16), BLOCK, BLOCK),
        in_specs=[SM, SM] + [HB] * 8 + [VM],
        out_specs=(VM, VM, VM),
        scratch_shapes=[
            pltpu.VMEM((LINKS, 2, 2, PNO, PNO), BF16),
            pltpu.VMEM((LINKS, PNO, PNO), BF16),
            pltpu.VMEM((2 * PAIRS, PNO, PNO), F32),
            pltpu.SemaphoreType.DMA((LINKS,)),
            pltpu.SemaphoreType.DMA((LINKS,)),
        ],
        compiler_params=params(26),
        name="intersect_and_project",
    )(info, fock, *lists, picked)

    energy = lax.dynamic_slice_in_dim(pno_energy, 4 * y, 4, 0)
    shift = lax.dynamic_slice_in_dim(pair_shift, 4 * y, 4, 0)
    exchange = lax.dynamic_slice_in_dim(exchange_integrals, 4 * y, 4, 0)
    denominator = energy[:, :, None] + energy[:, None, :] + shift[:, None, None]

    amplitudes = -(exchange + reduce_core_y(own, other, y)) / denominator
    sent = to_class_plane(amplitudes.astype(BF16).reshape(4 * PNO, PNO))
    a_refs, b_refs = plane_gather(sent[: 2 * PNO], sent[2 * PNO :])
    own, other = pl.pallas_call(
        next_kernel,
        out_shape=(BLOCK, BLOCK),
        in_specs=[SM, SM] + [VM] * 9,
        out_specs=(VM, VM),
        scratch_shapes=[
            pltpu.VMEM((LINKS, PNO, PNO), BF16),
            pltpu.VMEM((2 * PAIRS, PNO, PNO), F32),
        ],
        compiler_params=params(20),
        name="project",
    )(info, fock, inter, *a_refs, *b_refs)
    amplitudes = -(exchange + reduce_core_y(own, other, y)) / denominator
    gathered = ring(amplitudes, "grp")
    result = jnp.zeros_like(exchange_integrals)
    for d in range(4):
        result = lax.dynamic_update_slice_in_dim(result, gathered[d], 4 * ((y + d) % 4), 0)
    return result


def solution(mesh):
    fine = Mesh(mesh.devices.reshape(4, 4, 2, 4), ("z", "x", "core", "grp"))
    placed = (
        P(SPLIT, "grp", None),
        P(SPLIT, "grp"),
        P(SPLIT, None),
        P(SPLIT, None),
        P(SPLIT, None),
        P(SPLIT, None, None),
        P(SPLIT, None),
        P(SPLIT),
        P(SPLIT, None, None),
    )
    return jax.shard_map(
        on_device, mesh=fine, in_specs=placed, out_specs=P(SPLIT, None, None), check_vma=False
    )
```

```python
import jax
import jax.numpy as jnp
from jax import lax
from jax.experimental import pallas as pl
from jax.experimental.pallas import tpu as pltpu
from jax.sharding import Mesh, PartitionSpec as P

NB = 192
RANGES = 4
PAIRS = 16
PNO = 128
LINKS = 40
UNROLL = 8
ORBITALS = 4 * PNO
COLOUR = ORBITALS + PNO
EVEN = [(0, 1), (1, 0), (2, 3), (3, 2)]
ODD = [(1, 2), (2, 1), (3, 0), (0, 3)]
STEPS = (
    (("x", EVEN), ("z", EVEN), ("x", ODD), ("z", ODD)),
    (("z", EVEN), ("x", EVEN), ("z", ODD), ("x", ODD)),
    (("x", ODD), ("z", ODD), ("x", EVEN), ("z", EVEN)),
    (("z", ODD), ("x", ODD), ("z", EVEN), ("x", EVEN)),
)
BF16 = jnp.bfloat16
F32 = jnp.float32
SPLIT = ("z", "x", "core")
TARGET, SLOT, ABS_X, REL_X, REL_Z, X_EVEN, X_ODD, AMP_LIST, AMP_AT = range(9)


def one_hot(row):
    functions = lax.broadcasted_iota(jnp.int32, (NB, PNO), 0).astype(F32)
    return jnp.where(functions == row, 1.0, 0.0).astype(BF16)


def pick_kernel(info, place, targets, domains, picked, expanded, dom, source_dom):
    for i in range(2 * RANGES):
        dom[i] = targets[i, PAIRS * PNO :, :].astype(F32)
    for r in range(RANGES):
        for i in range(4):
            source_dom[r, i] = domains[r, i].astype(F32)

    def expand(i, carry):
        for block in range(2):
            for r in range(RANGES):
                d = place[4 + 4 * block + r]
                hot = one_hot(dom[d, pl.ds(i, 1), :])
                rows = targets[d, pl.ds(pl.multiple_of(i * PNO, PNO), PNO), :]
                full = jnp.dot(hot, rows, preferred_element_type=F32)
                expanded[block * PAIRS + i, r] = full.T.astype(BF16)
        return carry

    lax.fori_loop(0, PAIRS, expand, 0)

    def pick(step, carry):
        for u in range(4):
            j = step * 4 + u
            for r in range(RANGES):
                row = source_dom[place[r], info[ABS_X, j], pl.ds(info[SLOT, j], 1), :]
                part = jnp.dot(
                    expanded[info[TARGET, j], r], one_hot(row), preferred_element_type=F32
                )
                picked[j, :, r * PNO : (r + 1) * PNO] = part.astype(BF16)
        return carry

    lax.fori_loop(0, LINKS // 4, pick, 0)


def fetch_amplitudes(info, j, a_refs, b_refs, amp):
    rx, slot, rz = info[REL_X, j], info[SLOT, j], info[REL_Z, j]
    rows = pl.ds(pl.multiple_of(lax.rem(slot, 2) * PNO, PNO), PNO)
    high = lax.rem(slot, 4) >= 2
    for r in range(4):

        @pl.when(jnp.logical_not(high) & (rz == r))
        def _():
            amp[j] = a_refs[r][rx, rows, :]

        @pl.when(high & (rx == r))
        def _():
            amp[j] = b_refs[r][rz, rows, :]


def project(inter, amp, weight):
    half = jnp.dot(inter, amp, preferred_element_type=F32).astype(BF16)
    whole = lax.dot_general(half, inter, (((1,), (1,)), ((), ())), preferred_element_type=F32)
    return weight * whole


def first_kernel(info, fock, *refs):
    lists, picked = refs[0:8], refs[8]
    inter, own, other = refs[9:12]
    source, amp, acc, sem, amp_sem = refs[12:]

    def fetch(j, carry):
        slot, even, odd = info[SLOT, j], info[X_EVEN, j], info[X_ODD, j]
        colour = lax.div(slot, 4)
        rows = pl.ds(pl.multiple_of(lax.rem(slot, 4) * PNO, PNO), PNO)

        def copy(src, dst):
            pltpu.make_async_copy(src, dst, sem.at[j]).start()

        @pl.when(colour == 0)
        def _():
            for bit in range(2):
                copy(lists[bit].at[odd, :, even, rows], source.at[j, bit])

        @pl.when(colour == 2)
        def _():
            for bit in range(2):
                copy(lists[4 + bit].at[even, :, odd, rows], source.at[j, :, bit])

        for last in range(2):

            @pl.when((colour == 1) & (odd == last))
            def _():
                copy(lists[2 + last].at[:, even, :, rows], source.at[j])

            @pl.when((colour == 3) & (even == last))
            def _():
                for bit in range(2):
                    copy(lists[6 + last].at[bit, odd, :, rows], source.at[j, :, bit])

        at = info[AMP_AT, j]
        for i in range(8):

            @pl.when(info[AMP_LIST, j] == i)
            def _():
                pltpu.make_async_copy(
                    lists[i].at[
                        lax.div(at, 4), lax.rem(lax.div(at, 2), 2), lax.rem(at, 2),
                        pl.ds(ORBITALS, PNO),
                    ],
                    amp.at[j],
                    amp_sem.at[j],
                ).start()

        return carry

    lax.fori_loop(0, LINKS, fetch, 0)
    acc[...] = jnp.zeros_like(acc)

    def body(step, carry):
        for u in range(UNROLL):
            j = step * UNROLL + u
            pltpu.make_async_copy(source.at[j], source.at[j], sem.at[j]).wait()
            pltpu.make_async_copy(amp.at[j], amp.at[j], amp_sem.at[j]).wait()
        for u in range(UNROLL):
            j = step * UNROLL + u
            rows = source[j].reshape(RANGES * PNO, PNO)
            block = jnp.dot(picked[j], rows, preferred_element_type=F32).astype(BF16)
            inter[j] = block
            target = info[TARGET, j]
            acc[target] = acc[target] + project(block, amp[j], fock[0, j])
        return carry

    lax.fori_loop(0, LINKS // UNROLL, body, 0)
    own[...] = acc[0:PAIRS]
    other[...] = acc[PAIRS:].astype(other.dtype)


def next_kernel(info, fock, inter, *refs):
    a_refs, b_refs = refs[0:4], refs[4:8]
    own, other = refs[8:10]
    amp, acc = refs[10:]

    def fetch(j, carry):
        fetch_amplitudes(info, j, a_refs, b_refs, amp)
        return carry

    lax.fori_loop(0, LINKS, fetch, 0)
    acc[...] = jnp.zeros_like(acc)

    def body(step, carry):
        for u in range(UNROLL):
            j = step * UNROLL + u
            target = info[TARGET, j]
            acc[target] = acc[target] + project(inter[j], amp[j], fock[0, j])
        return carry

    lax.fori_loop(0, LINKS // UNROLL, body, 0)
    own[...] = acc[0:PAIRS]
    other[...] = acc[PAIRS:].astype(other.dtype)


VM = pl.BlockSpec(memory_space=pltpu.VMEM)
SM = pl.BlockSpec(memory_space=pltpu.SMEM)
HB = pl.BlockSpec(memory_space=pl.ANY)


def params(mib):
    return pltpu.CompilerParams(vmem_limit_bytes=mib * 1024 * 1024)


BLOCK = jax.ShapeDtypeStruct((PAIRS, PNO, PNO), F32)


def shifted(value, axis, rel):
    return lax.ppermute(value, axis, [((i + rel) % 4, i) for i in range(4)])


def ring(value, axis):
    plus, minus = shifted(value, axis, 1), shifted(value, axis, 3)
    return [value, plus, shifted(value, axis, 2), minus]


def swap_core(value):
    return lax.ppermute(value, "core", [(0, 1), (1, 0)])


def to_class_plane(value):
    moves = []
    for z in range(4):
        for core in range(2):
            for y in range(4):
                moves.append(
                    ((z * 2 + core) * 4 + y, (y * 2 + core) * 4 + (z + 2 * core) % 4)
                )
    return lax.ppermute(value, ("z", "core", "grp"), moves)


def ways(rel, here):
    lean = 1 + 2 * (here % 2)
    even = (rel == 2) | (rel == lean)
    odd = (rel == 2) | (rel == 4 - lean)
    return even.astype(jnp.int32), odd.astype(jnp.int32)


def plane_gather(half_a, half_b):
    a, b = lax.optimization_barrier(
        (jnp.stack(ring(half_a, "x")), jnp.stack(ring(half_b, "z")))
    )
    return ring(a, "z"), ring(b, "x")


def reduce_core_y(own, other, y):
    total = own + swap_core(other)
    pieces = [lax.dynamic_slice_in_dim(total, 4 * ((y + d) % 4), 4, 0) for d in range(4)]
    result = pieces[0]
    for d in (1, 3, 2):
        result = result + shifted(pieces[d], "grp", 4 - d)
    return result


def on_device(
    coefficients,
    domain,
    coupling_owner,
    coupling_slot,
    coupling_fock,
    exchange_integrals,
    pno_energy,
    pair_shift,
    amplitudes_start,
):
    z, x, core, y = [lax.axis_index(name) for name in ("z", "x", "core", "grp")]
    class_z = (y + 2 * core) % 4
    flat = coefficients.reshape(PAIRS * PNO, PNO)
    local = (domain - y * NB).astype(BF16)
    start = lax.dynamic_slice_in_dim(amplitudes_start, 4 * y, 4, 0).astype(BF16)
    start = start.reshape(4 * PNO, PNO)
    colours = [
        to_class_plane(
            jnp.concatenate(
                [flat[k * ORBITALS : (k + 1) * ORBITALS], start[k * PNO : (k + 1) * PNO]]
            )
        )[None]
        for k in range(4)
    ]
    domains = to_class_plane(local)
    *colours, own_targets = lax.optimization_barrier(
        (*colours, jnp.concatenate([flat, local]))
    )
    targets = lax.all_gather(own_targets, ("core", "grp"))

    table = jnp.stack(
        [(coupling_owner * PAIRS + coupling_slot).astype(F32), coupling_fock]
    )
    table = jnp.concatenate([table, swap_core(table)], axis=1).reshape(2, -1)
    named = table[0].astype(jnp.int32)
    slots, owners = named % PAIRS, named // PAIRS
    owner_x = (owners // 2) % 4
    mine = (owners % 2 == core) & (owners // 8 == class_z)
    order = jnp.cumsum(mine.astype(jnp.int32)) - 1
    hit = mine[None, :] & (order[None, :] == jnp.arange(LINKS, dtype=jnp.int32)[:, None])
    target_of = jnp.arange(2 * PAIRS * 8, dtype=jnp.int32) // 8
    x_even, x_odd = ways((owner_x - x) % 4, x)
    z_even, z_odd = ways((slots // 4 - z) % 4, z)
    bits = (
        (x_even, z_even, x_odd, z_odd),
        (z_even, x_even, z_odd, x_odd),
        (x_odd, z_odd, x_even, z_even),
        (z_odd, x_odd, z_even, x_even),
    )
    amp_list, amp_at = jnp.zeros_like(slots), jnp.zeros_like(slots)
    for k in range(4):
        b = bits[k]
        amp_list = jnp.where(slots % 4 == k, 2 * k + b[3], amp_list)
        amp_at = jnp.where(slots % 4 == k, b[0] + 2 * b[1] + 4 * b[2], amp_at)
    columns = jnp.stack(
        [
            target_of, slots, owner_x, (owner_x - x) % 4, (slots // 4 - z) % 4,
            x_even, x_odd, amp_list, amp_at,
        ]
    )
    info = jnp.sum(jnp.where(hit[None], columns[:, None, :], 0), axis=2).astype(jnp.int32)
    fock = jnp.sum(jnp.where(hit, table[1][None, :], 0.0), axis=1)[None, :]

    for step in range(4):
        got = [lax.ppermute(colours[k], *STEPS[k][step]) for k in range(4)]
        if step == 3:
            break
        colours = [jnp.concatenate([colours[k], got[k]]) for k in range(4)]
        if step == 1:
            _, domains = lax.optimization_barrier((colours[3], domains))
            domains = jnp.broadcast_to(domains[None], (16, PAIRS, PNO))
            domains = lax.all_to_all(domains, ("z", "x"), 0, 0, tiled=True)
        elif step == 2:
            _, domains = lax.optimization_barrier((colours[3], domains))
    lists = []
    for k in range(4):
        lists.append(colours[k].reshape(2, 2, 2, COLOUR, PNO))
        lists.append(got[k].reshape(2, 2, 2, COLOUR, PNO))

    lean = 1 - 2 * (z % 2)
    ranges = jnp.stack([z, z + lean, z - lean, z + 2]) % 4
    place = jnp.concatenate([ranges, 4 * core + ranges, 4 * (1 - core) + ranges])
    picked = pl.pallas_call(
        pick_kernel,
        out_shape=jax.ShapeDtypeStruct((LINKS, PNO, RANGES * PNO), BF16),
        in_specs=[SM, SM, VM, VM],
        out_specs=VM,
        scratch_shapes=[
            pltpu.VMEM((2 * PAIRS, RANGES, PNO, NB), BF16),
            pltpu.VMEM((2 * RANGES, PAIRS, PNO), F32),
            pltpu.VMEM((RANGES, 4, PAIRS, PNO), F32),
        ],
        compiler_params=params(20),
        name="pick_targets",
    )(info, place.astype(jnp.int32), targets, domains.reshape(RANGES, 4, PAIRS, PNO))

    inter, own, other = pl.pallas_call(
        first_kernel,
        out_shape=(jax.ShapeDtypeStruct((LINKS, PNO, PNO), BF16), BLOCK, BLOCK),
        in_specs=[SM, SM] + [HB] * 8 + [VM],
        out_specs=(VM, VM, VM),
        scratch_shapes=[
            pltpu.VMEM((LINKS, 2, 2, PNO, PNO), BF16),
            pltpu.VMEM((LINKS, PNO, PNO), BF16),
            pltpu.VMEM((2 * PAIRS, PNO, PNO), F32),
            pltpu.SemaphoreType.DMA((LINKS,)),
            pltpu.SemaphoreType.DMA((LINKS,)),
        ],
        compiler_params=params(19),
        name="intersect_and_project",
    )(info, fock, *lists, picked)

    energy = lax.dynamic_slice_in_dim(pno_energy, 4 * y, 4, 0)
    shift = lax.dynamic_slice_in_dim(pair_shift, 4 * y, 4, 0)
    exchange = lax.dynamic_slice_in_dim(exchange_integrals, 4 * y, 4, 0)
    denominator = energy[:, :, None] + energy[:, None, :] + shift[:, None, None]

    amplitudes = -(exchange + reduce_core_y(own, other, y)) / denominator
    sent = to_class_plane(amplitudes.astype(BF16).reshape(4 * PNO, PNO))
    a_refs, b_refs = plane_gather(sent[: 2 * PNO], sent[2 * PNO :])
    own, other = pl.pallas_call(
        next_kernel,
        out_shape=(BLOCK, BLOCK),
        in_specs=[SM, SM] + [VM] * 9,
        out_specs=(VM, VM),
        scratch_shapes=[
            pltpu.VMEM((LINKS, PNO, PNO), BF16),
            pltpu.VMEM((2 * PAIRS, PNO, PNO), F32),
        ],
        compiler_params=params(12),
        name="project",
    )(info, fock, inter, *a_refs, *b_refs)
    amplitudes = -(exchange + reduce_core_y(own, other, y)) / denominator
    gathered = ring(amplitudes, "grp")
    result = jnp.zeros_like(exchange_integrals)
    for d in range(4):
        result = lax.dynamic_update_slice_in_dim(result, gathered[d], 4 * ((y + d) % 4), 0)
    return result


def solution(mesh):
    fine = Mesh(mesh.devices.reshape(4, 4, 2, 4), ("z", "x", "core", "grp"))
    placed = (
        P(SPLIT, "grp", None),
        P(SPLIT, "grp"),
        P(SPLIT, None),
        P(SPLIT, None),
        P(SPLIT, None),
        P(SPLIT, None, None),
        P(SPLIT, None),
        P(SPLIT),
        P(SPLIT, None, None),
    )
    return jax.shard_map(
        on_device, mesh=fine, in_specs=placed, out_specs=P(SPLIT, None, None), check_vma=False
    )
```

```python
import jax
import jax.numpy as jnp
from jax import lax
from jax.experimental import pallas as pl
from jax.experimental.pallas import tpu as pltpu
from jax.sharding import Mesh, PartitionSpec as P

NB = 192
RANGES = 4
PAIRS = 16
PNO = 128
LINKS = 40
UNROLL = 8
ORBITALS = 4 * PNO
COLOUR = ORBITALS + PNO
EVEN = [(0, 1), (1, 0), (2, 3), (3, 2)]
ODD = [(1, 2), (2, 1), (3, 0), (0, 3)]
STEPS = (
    (("x", EVEN), ("z", EVEN), ("x", ODD), ("z", ODD)),
    (("z", EVEN), ("x", EVEN), ("z", ODD), ("x", ODD)),
    (("x", ODD), ("z", ODD), ("x", EVEN), ("z", EVEN)),
    (("z", ODD), ("x", ODD), ("z", EVEN), ("x", EVEN)),
)
BF16 = jnp.bfloat16
F32 = jnp.float32
SPLIT = ("z", "x", "core")
TARGET, SLOT, REL_X, REL_Z, X_EVEN, X_ODD, AMP_LIST, AMP_AT = range(8)


def one_hot(row):
    functions = lax.broadcasted_iota(jnp.int32, (NB, PNO), 0).astype(F32)
    return jnp.where(functions == row, 1.0, 0.0).astype(BF16)


def pick_kernel(info, place, targets, held, got, picked, expanded, dom, source_dom):
    for i in range(2 * RANGES):
        dom[i] = targets[i, PAIRS * PNO : PAIRS * PNO + PAIRS, :].astype(F32)
    for i in range(8):
        source_dom[0, i] = held[i].astype(F32)
        source_dom[1, i] = got[i].astype(F32)

    def expand(i, carry):
        for block in range(2):
            for r in range(RANGES):
                d = place[4 * block + r]
                hot = one_hot(dom[d, pl.ds(i, 1), :])
                rows = targets[d, pl.ds(pl.multiple_of(i * PNO, PNO), PNO), :]
                full = jnp.dot(hot, rows, preferred_element_type=F32)
                expanded[block * PAIRS + i, r] = full.T.astype(BF16)
        return carry

    lax.fori_loop(0, PAIRS, expand, 0)

    def pick(step, carry):
        for u in range(4):
            j = step * 4 + u
            for r in range(RANGES):
                at = 4 * info[X_ODD, j] + 2 * (r % 2) + info[X_EVEN, j]
                row = source_dom[r // 2, at, pl.ds(info[SLOT, j], 1), :]
                part = jnp.dot(
                    expanded[info[TARGET, j], r], one_hot(row), preferred_element_type=F32
                )
                picked[j, :, r * PNO : (r + 1) * PNO] = part.astype(BF16)
        return carry

    lax.fori_loop(0, LINKS // 4, pick, 0)


def choose(which, low, high, act):
    if high - low == 1:
        act(low)
        return
    middle = (low + high) // 2

    @pl.when(which < middle)
    def _():
        choose(which, low, middle, act)

    @pl.when(which >= middle)
    def _():
        choose(which, middle, high, act)


def fetch_amplitudes(info, j, a_refs, b_refs, amp):
    rx, slot, rz = info[REL_X, j], info[SLOT, j], info[REL_Z, j]
    rows = pl.ds(pl.multiple_of(lax.rem(slot, 2) * PNO, PNO), PNO)

    def from_a(r):
        amp[j] = a_refs[r][rx, rows, :]

    def from_b(r):
        amp[j] = b_refs[r][rz, rows, :]

    @pl.when(lax.rem(slot, 4) < 2)
    def _():
        choose(rz, 0, 4, from_a)

    @pl.when(lax.rem(slot, 4) >= 2)
    def _():
        choose(rx, 0, 4, from_b)


def project_all(info, fock, inter, amp, acc):
    def body(step, carry):
        for u in range(UNROLL):
            j = step * UNROLL + u
            block, target = inter[j], info[TARGET, j]
            half = jnp.dot(block, amp[j], preferred_element_type=F32).astype(BF16)
            whole = lax.dot_general(
                half, block, (((1,), (1,)), ((), ())), preferred_element_type=F32
            )
            acc[target] = acc[target] + fock[0, j] * whole
        return carry

    lax.fori_loop(0, LINKS // UNROLL, body, 0)


def first_kernel(info, fock, *refs):
    lists, picked = refs[0:8], refs[8]
    inter, own, other = refs[9:12]
    source, amp, acc, sem, amp_sem = refs[12:]

    def fetch(j, carry):
        slot, even, odd = info[SLOT, j], info[X_EVEN, j], info[X_ODD, j]
        rows = pl.ds(pl.multiple_of(lax.rem(slot, 4) * PNO, PNO), PNO)

        def copy(src, dst):
            pltpu.make_async_copy(src, dst, sem.at[j]).start()

        def from_colour(colour):
            if colour == 0:
                for bit in range(2):
                    copy(lists[bit].at[odd, :, even, rows], source.at[j, bit])
            elif colour == 1:
                choose(odd, 0, 2, lambda last: copy(
                    lists[2 + last].at[:, even, :, rows], source.at[j]
                ))
            elif colour == 2:
                for bit in range(2):
                    copy(lists[4 + bit].at[even, :, odd, rows], source.at[j, :, bit])
            else:
                choose(even, 0, 2, lambda last: [
                    copy(lists[6 + last].at[bit, odd, :, rows], source.at[j, :, bit])
                    for bit in range(2)
                ])

        choose(lax.div(slot, 4), 0, 4, from_colour)
        at = info[AMP_AT, j]
        far, middle, near = lax.div(at, 4), lax.rem(lax.div(at, 2), 2), lax.rem(at, 2)
        choose(info[AMP_LIST, j], 0, 8, lambda i: pltpu.make_async_copy(
            lists[i].at[far, middle, near, pl.ds(ORBITALS, PNO)], amp.at[j], amp_sem.at[j]
        ).start())
        return carry

    lax.fori_loop(0, LINKS, fetch, 0)
    acc[...] = jnp.zeros_like(acc)

    def intersect(step, carry):
        for u in range(UNROLL):
            j = step * UNROLL + u
            pltpu.make_async_copy(source.at[j], source.at[j], sem.at[j]).wait()
            pltpu.make_async_copy(amp.at[j], amp.at[j], amp_sem.at[j]).wait()
        for u in range(UNROLL):
            j = step * UNROLL + u
            rows = source[j].reshape(RANGES * PNO, PNO)
            block = jnp.dot(picked[j], rows, preferred_element_type=F32)
            inter[j] = block.astype(BF16)
        return carry

    lax.fori_loop(0, LINKS // UNROLL, intersect, 0)
    project_all(info, fock, inter, amp, acc)
    own[...] = acc[0:PAIRS]
    other[...] = acc[PAIRS:].astype(other.dtype)


def next_kernel(info, fock, inter, *refs):
    a_refs, b_refs = refs[0:4], refs[4:8]
    own, other = refs[8:10]
    amp, acc = refs[10:]

    def fetch(j, carry):
        fetch_amplitudes(info, j, a_refs, b_refs, amp)
        return carry

    lax.fori_loop(0, LINKS, fetch, 0)
    acc[...] = jnp.zeros_like(acc)

    project_all(info, fock, inter, amp, acc)
    own[...] = acc[0:PAIRS]
    other[...] = acc[PAIRS:].astype(other.dtype)


VM = pl.BlockSpec(memory_space=pltpu.VMEM)
SM = pl.BlockSpec(memory_space=pltpu.SMEM)
HB = pl.BlockSpec(memory_space=pl.ANY)


def params(mib):
    return pltpu.CompilerParams(vmem_limit_bytes=mib * 1024 * 1024)


BLOCK = jax.ShapeDtypeStruct((PAIRS, PNO, PNO), F32)


def shifted(value, axis, rel):
    return lax.ppermute(value, axis, [((i + rel) % 4, i) for i in range(4)])


def ring(value, axis):
    plus, minus = shifted(value, axis, 1), shifted(value, axis, 3)
    return [value, plus, shifted(value, axis, 2), minus]


def swap_core(value):
    return lax.ppermute(value, "core", [(0, 1), (1, 0)])


def to_class_plane(value):
    moves = []
    for z in range(4):
        for core in range(2):
            for y in range(4):
                moves.append(
                    ((z * 2 + core) * 4 + y, (y * 2 + core) * 4 + (z + 2 * core) % 4)
                )
    return lax.ppermute(value, ("z", "core", "grp"), moves)


def ways(rel, here):
    lean = 1 + 2 * (here % 2)
    even = (rel == 2) | (rel == lean)
    odd = (rel == 2) | (rel == 4 - lean)
    return even.astype(jnp.int32), odd.astype(jnp.int32)


def plane_gather(half_a, half_b):
    a, b = lax.optimization_barrier(
        (jnp.stack(ring(half_a, "x")), jnp.stack(ring(half_b, "z")))
    )
    return ring(a, "z"), ring(b, "x")


def reduce_core_y(own, other, y):
    total = own + swap_core(other)
    pieces = [lax.dynamic_slice_in_dim(total, 4 * ((y + d) % 4), 4, 0) for d in range(4)]
    result = pieces[0]
    for d in (1, 3, 2):
        result = result + shifted(pieces[d], "grp", 4 - d)
    return result


def on_device(
    coefficients,
    domain,
    coupling_owner,
    coupling_slot,
    coupling_fock,
    exchange_integrals,
    pno_energy,
    pair_shift,
    amplitudes_start,
):
    z, x, core, y = [lax.axis_index(name) for name in ("z", "x", "core", "grp")]
    class_z = (y + 2 * core) % 4
    flat = coefficients.reshape(PAIRS * PNO, PNO)
    local = (domain - y * NB).astype(BF16)
    start = lax.dynamic_slice_in_dim(amplitudes_start, 4 * y, 4, 0).astype(BF16)
    start = start.reshape(4 * PNO, PNO)
    colours = []
    for k in range(4):
        rows = [flat[k * ORBITALS : (k + 1) * ORBITALS], start[k * PNO : (k + 1) * PNO]]
        if k == 0:
            rows.append(local)
        colours.append(to_class_plane(jnp.concatenate(rows))[None])
    own_targets = jnp.concatenate([flat, local, colours[3][0, :PAIRS]])
    targets = lax.all_gather(own_targets, ("core", "grp"))

    table = jnp.stack(
        [(coupling_owner * PAIRS + coupling_slot).astype(F32), coupling_fock]
    )
    table = jnp.concatenate([table, swap_core(table)], axis=1).reshape(2, -1)
    named = table[0].astype(jnp.int32)
    slots, owners = named % PAIRS, named // PAIRS
    owner_x = (owners // 2) % 4
    mine = (owners % 2 == core) & (owners // 8 == class_z)
    order = jnp.cumsum(mine.astype(jnp.int32)) - 1
    hit = mine[None, :] & (order[None, :] == jnp.arange(LINKS, dtype=jnp.int32)[:, None])
    target_of = jnp.arange(2 * PAIRS * 8, dtype=jnp.int32) // 8
    x_even, x_odd = ways((owner_x - x) % 4, x)
    z_even, z_odd = ways((slots // 4 - z) % 4, z)
    bits = (
        (x_even, z_even, x_odd, z_odd),
        (z_even, x_even, z_odd, x_odd),
        (x_odd, z_odd, x_even, z_even),
        (z_odd, x_odd, z_even, x_even),
    )
    amp_list, amp_at = jnp.zeros_like(slots), jnp.zeros_like(slots)
    for k in range(4):
        b = bits[k]
        amp_list = jnp.where(slots % 4 == k, 2 * k + b[3], amp_list)
        amp_at = jnp.where(slots % 4 == k, b[0] + 2 * b[1] + 4 * b[2], amp_at)
    columns = jnp.stack(
        [
            target_of, slots, (owner_x - x) % 4, (slots // 4 - z) % 4, x_even, x_odd, amp_list, amp_at,
        ]
    )
    info = jnp.sum(jnp.where(hit[None], columns[:, None, :], 0), axis=2).astype(jnp.int32)
    fock = jnp.sum(jnp.where(hit, table[1][None, :], 0.0), axis=1)[None, :]

    for step in range(4):
        if step == 3:
            held_domains = colours[0][:, COLOUR:]
            got_domains = lax.ppermute(held_domains, *STEPS[0][step])
        got = [lax.ppermute(colours[k], *STEPS[k][step]) for k in range(4)]
        if step < 3:
            colours = [jnp.concatenate([colours[k], got[k]]) for k in range(4)]
    lists = []
    for k in range(4):
        lists.append(colours[k].reshape(2, 2, 2, -1, PNO))
        lists.append(got[k].reshape(2, 2, 2, -1, PNO))

    lean = 1 - 2 * (z % 2)
    ranges = jnp.stack([z, z + lean, z - lean, z + 2]) % 4
    place = jnp.concatenate([4 * core + ranges, 4 * (1 - core) + ranges])
    picked = pl.pallas_call(
        pick_kernel,
        out_shape=jax.ShapeDtypeStruct((LINKS, PNO, RANGES * PNO), BF16),
        in_specs=[SM, SM, VM, VM, VM],
        out_specs=VM,
        scratch_shapes=[
            pltpu.VMEM((2 * PAIRS, RANGES, PNO, NB), BF16),
            pltpu.VMEM((2 * RANGES, PAIRS, PNO), F32),
            pltpu.VMEM((2, 8, PAIRS, PNO), F32),
        ],
        compiler_params=params(20),
        name="pick_targets",
    )(info, place.astype(jnp.int32), targets, held_domains, got_domains)

    inter, own, other = pl.pallas_call(
        first_kernel,
        out_shape=(jax.ShapeDtypeStruct((LINKS, PNO, PNO), BF16), BLOCK, BLOCK),
        in_specs=[SM, SM] + [HB] * 8 + [VM],
        out_specs=(VM, VM, VM),
        scratch_shapes=[
            pltpu.VMEM((LINKS, 2, 2, PNO, PNO), BF16),
            pltpu.VMEM((LINKS, PNO, PNO), BF16),
            pltpu.VMEM((2 * PAIRS, PNO, PNO), F32),
            pltpu.SemaphoreType.DMA((LINKS,)),
            pltpu.SemaphoreType.DMA((LINKS,)),
        ],
        compiler_params=params(19),
        name="intersect_and_project",
    )(info, fock, *lists, picked)

    energy = lax.dynamic_slice_in_dim(pno_energy, 4 * y, 4, 0)
    shift = lax.dynamic_slice_in_dim(pair_shift, 4 * y, 4, 0)
    exchange = lax.dynamic_slice_in_dim(exchange_integrals, 4 * y, 4, 0)
    denominator = energy[:, :, None] + energy[:, None, :] + shift[:, None, None]

    amplitudes = -(exchange + reduce_core_y(own, other, y)) / denominator
    sent = to_class_plane(amplitudes.astype(BF16).reshape(4 * PNO, PNO))
    a_refs, b_refs = plane_gather(sent[: 2 * PNO], sent[2 * PNO :])
    own, other = pl.pallas_call(
        next_kernel,
        out_shape=(BLOCK, BLOCK),
        in_specs=[SM, SM] + [VM] * 9,
        out_specs=(VM, VM),
        scratch_shapes=[
            pltpu.VMEM((LINKS, PNO, PNO), BF16),
            pltpu.VMEM((2 * PAIRS, PNO, PNO), F32),
        ],
        compiler_params=params(12),
        name="project",
    )(info, fock, inter, *a_refs, *b_refs)
    amplitudes = -(exchange + reduce_core_y(own, other, y)) / denominator
    gathered = ring(amplitudes, "grp")
    result = jnp.zeros_like(exchange_integrals)
    for d in range(4):
        result = lax.dynamic_update_slice_in_dim(result, gathered[d], 4 * ((y + d) % 4), 0)
    return result


def solution(mesh):
    fine = Mesh(mesh.devices.reshape(4, 4, 2, 4), ("z", "x", "core", "grp"))
    placed = (
        P(SPLIT, "grp", None),
        P(SPLIT, "grp"),
        P(SPLIT, None),
        P(SPLIT, None),
        P(SPLIT, None),
        P(SPLIT, None, None),
        P(SPLIT, None),
        P(SPLIT),
        P(SPLIT, None, None),
    )
    return jax.shard_map(
        on_device, mesh=fine, in_specs=placed, out_specs=P(SPLIT, None, None), check_vma=False
    )
```

```python
import jax
import jax.numpy as jnp
from jax import lax
from jax.experimental import pallas as pl
from jax.experimental.pallas import tpu as pltpu
from jax.sharding import Mesh, PartitionSpec as P

NB = 192
RANGES = 4
PAIRS = 16
PNO = 128
LINKS = 40
UNROLL = 8
ORBITALS = 4 * PNO
COLOUR = ORBITALS + PNO
EVEN = [(0, 1), (1, 0), (2, 3), (3, 2)]
ODD = [(1, 2), (2, 1), (3, 0), (0, 3)]
STEPS = (
    (("x", EVEN), ("z", EVEN), ("x", ODD), ("z", ODD)),
    (("z", EVEN), ("x", EVEN), ("z", ODD), ("x", ODD)),
    (("x", ODD), ("z", ODD), ("x", EVEN), ("z", EVEN)),
    (("z", ODD), ("x", ODD), ("z", EVEN), ("x", EVEN)),
)
BF16 = jnp.bfloat16
F32 = jnp.float32
SPLIT = ("z", "x", "core")
TARGET, SLOT, REL_X, REL_Z, X_EVEN, X_ODD, AMP_LIST, AMP_AT = range(8)


def one_hot(row):
    functions = lax.broadcasted_iota(jnp.int32, (NB, PNO), 0).astype(F32)
    return jnp.where(functions == row, 1.0, 0.0).astype(BF16)


def pick_kernel(info, place, targets, held, got, picked, expanded, dom, source_dom):
    for i in range(2 * RANGES):
        dom[i] = targets[i, PAIRS * PNO : PAIRS * PNO + PAIRS, :].astype(F32)
    for i in range(8):
        source_dom[0, i] = held[i].astype(F32)
        source_dom[1, i] = got[i].astype(F32)

    def expand(i, carry):
        for block in range(2):
            for r in range(RANGES):
                d = place[4 * block + r]
                hot = one_hot(dom[d, pl.ds(i, 1), :])
                rows = targets[d, pl.ds(pl.multiple_of(i * PNO, PNO), PNO), :]
                full = jnp.dot(hot, rows, preferred_element_type=F32)
                expanded[block * PAIRS + i, r] = full.T.astype(BF16)
        return carry

    lax.fori_loop(0, PAIRS, expand, 0)

    def pick(step, carry):
        for u in range(4):
            j = step * 4 + u
            for r in range(RANGES):
                at = 4 * info[X_ODD, j] + 2 * (r % 2) + info[X_EVEN, j]
                row = source_dom[r // 2, at, pl.ds(info[SLOT, j], 1), :]
                part = jnp.dot(
                    expanded[info[TARGET, j], r], one_hot(row), preferred_element_type=F32
                )
                picked[j, :, r * PNO : (r + 1) * PNO] = part.astype(BF16)
        return carry

    lax.fori_loop(0, LINKS // 4, pick, 0)


def choose(which, low, high, act):
    if high - low == 1:
        act(low)
        return
    middle = (low + high) // 2

    @pl.when(which < middle)
    def _():
        choose(which, low, middle, act)

    @pl.when(which >= middle)
    def _():
        choose(which, middle, high, act)


def fetch_amplitudes(info, j, a_refs, b_refs, amp):
    rx, slot, rz = info[REL_X, j], info[SLOT, j], info[REL_Z, j]
    rows = pl.ds(pl.multiple_of(lax.rem(slot, 2) * PNO, PNO), PNO)

    def from_a(r):
        amp[j] = a_refs[r][rx, rows, :]

    def from_b(r):
        amp[j] = b_refs[r][rz, rows, :]

    @pl.when(lax.rem(slot, 4) < 2)
    def _():
        choose(rz, 0, 4, from_a)

    @pl.when(lax.rem(slot, 4) >= 2)
    def _():
        choose(rx, 0, 4, from_b)


def project_all(info, fock, inter, amp, acc):
    def body(step, carry):
        for u in range(UNROLL):
            j = step * UNROLL + u
            block, target = inter[j], info[TARGET, j]
            half = jnp.dot(block, amp[j], preferred_element_type=F32).astype(BF16)
            whole = lax.dot_general(
                half, block, (((1,), (1,)), ((), ())), preferred_element_type=F32
            )
            acc[target] = acc[target] + fock[0, j] * whole
        return carry

    lax.fori_loop(0, LINKS // UNROLL, body, 0)


def first_kernel(info, fock, *refs):
    lists, picked = refs[0:16], refs[16]
    inter, own, other = refs[17:20]
    source, amp, acc, sem, amp_sem = refs[20:]

    def fetch(j, carry):
        slot, even, odd = info[SLOT, j], info[X_EVEN, j], info[X_ODD, j]
        rows = pl.ds(pl.multiple_of(lax.rem(slot, 4) * PNO, PNO), PNO)

        def copy(src, dst):
            pltpu.make_async_copy(src, dst, sem.at[j]).start()

        def from_colour(colour):
            def pieces(x_bit):
                for z_bit in range(2):
                    if colour == 0:
                        piece = lists[2 * z_bit + x_bit].at[:, even, rows]
                        copy(piece, source.at[j, z_bit])
                    elif colour == 1:
                        piece = lists[4 + 2 * x_bit + z_bit].at[even, :, rows]
                        copy(piece, source.at[j, z_bit])
                    elif colour == 2:
                        piece = lists[8 + 2 * z_bit + x_bit].at[:, odd, rows]
                        copy(piece, source.at[j, :, z_bit])
                    else:
                        piece = lists[12 + 2 * x_bit + z_bit].at[odd, :, rows]
                        copy(piece, source.at[j, :, z_bit])

            choose(odd if colour < 2 else even, 0, 2, pieces)

        choose(lax.div(slot, 4), 0, 4, from_colour)
        high, low = lax.div(info[AMP_AT, j], 2), lax.rem(info[AMP_AT, j], 2)
        choose(info[AMP_LIST, j], 0, 16, lambda i: pltpu.make_async_copy(
            lists[i].at[high, low, pl.ds(ORBITALS, PNO)], amp.at[j], amp_sem.at[j]
        ).start())
        return carry

    lax.fori_loop(0, LINKS, fetch, 0)
    acc[...] = jnp.zeros_like(acc)

    def intersect(step, carry):
        for u in range(UNROLL):
            j = step * UNROLL + u
            pltpu.make_async_copy(source.at[j], source.at[j], sem.at[j]).wait()
            pltpu.make_async_copy(amp.at[j], amp.at[j], amp_sem.at[j]).wait()
        for u in range(UNROLL):
            j = step * UNROLL + u
            rows = source[j].reshape(RANGES * PNO, PNO)
            block = jnp.dot(picked[j], rows, preferred_element_type=F32)
            inter[j] = block.astype(BF16)
        return carry

    lax.fori_loop(0, LINKS // UNROLL, intersect, 0)
    project_all(info, fock, inter, amp, acc)
    own[...] = acc[0:PAIRS]
    other[...] = acc[PAIRS:].astype(other.dtype)


def next_kernel(info, fock, inter, *refs):
    a_refs, b_refs = refs[0:4], refs[4:8]
    own, other = refs[8:10]
    amp, acc = refs[10:]

    def fetch(j, carry):
        fetch_amplitudes(info, j, a_refs, b_refs, amp)
        return carry

    lax.fori_loop(0, LINKS, fetch, 0)
    acc[...] = jnp.zeros_like(acc)

    project_all(info, fock, inter, amp, acc)
    own[...] = acc[0:PAIRS]
    other[...] = acc[PAIRS:].astype(other.dtype)


VM = pl.BlockSpec(memory_space=pltpu.VMEM)
SM = pl.BlockSpec(memory_space=pltpu.SMEM)
HB = pl.BlockSpec(memory_space=pl.ANY)


def params(mib):
    return pltpu.CompilerParams(vmem_limit_bytes=mib * 1024 * 1024)


BLOCK = jax.ShapeDtypeStruct((PAIRS, PNO, PNO), F32)


def shifted(value, axis, rel):
    return lax.ppermute(value, axis, [((i + rel) % 4, i) for i in range(4)])


def ring(value, axis):
    plus, minus = shifted(value, axis, 1), shifted(value, axis, 3)
    return [value, plus, shifted(value, axis, 2), minus]


def swap_core(value):
    return lax.ppermute(value, "core", [(0, 1), (1, 0)])


def to_class_plane(value):
    moves = []
    for z in range(4):
        for core in range(2):
            for y in range(4):
                moves.append(
                    ((z * 2 + core) * 4 + y, (y * 2 + core) * 4 + (z + 2 * core) % 4)
                )
    return lax.ppermute(value, ("z", "core", "grp"), moves)


def ways(rel, here):
    lean = 1 + 2 * (here % 2)
    even = (rel == 2) | (rel == lean)
    odd = (rel == 2) | (rel == 4 - lean)
    return even.astype(jnp.int32), odd.astype(jnp.int32)


def plane_gather(half_a, half_b):
    a, b = lax.optimization_barrier(
        (jnp.stack(ring(half_a, "x")), jnp.stack(ring(half_b, "z")))
    )
    return ring(a, "z"), ring(b, "x")


def reduce_core_y(own, other, y):
    total = own + swap_core(other)
    pieces = [lax.dynamic_slice_in_dim(total, 4 * ((y + d) % 4), 4, 0) for d in range(4)]
    result = pieces[0]
    for d in (1, 3, 2):
        result = result + shifted(pieces[d], "grp", 4 - d)
    return result


def on_device(
    coefficients,
    domain,
    coupling_owner,
    coupling_slot,
    coupling_fock,
    exchange_integrals,
    pno_energy,
    pair_shift,
    amplitudes_start,
):
    z, x, core, y = [lax.axis_index(name) for name in ("z", "x", "core", "grp")]
    class_z = (y + 2 * core) % 4
    flat = coefficients.reshape(PAIRS * PNO, PNO)
    local = (domain - y * NB).astype(BF16)
    start = lax.dynamic_slice_in_dim(amplitudes_start, 4 * y, 4, 0).astype(BF16)
    start = start.reshape(4 * PNO, PNO)
    colours = []
    for k in range(4):
        rows = [flat[k * ORBITALS : (k + 1) * ORBITALS], start[k * PNO : (k + 1) * PNO]]
        if k == 0:
            rows.append(local)
        colours.append(to_class_plane(jnp.concatenate(rows))[None])
    arrived = [colours[k][0, :PAIRS] for k in range(4)]
    own_targets = jnp.concatenate([flat, local, *arrived])
    targets = lax.all_gather(own_targets, ("core", "grp"))

    table = jnp.stack(
        [(coupling_owner * PAIRS + coupling_slot).astype(F32), coupling_fock]
    )
    table = jnp.concatenate([table, swap_core(table)], axis=1).reshape(2, -1)
    named = table[0].astype(jnp.int32)
    slots, owners = named % PAIRS, named // PAIRS
    owner_x = (owners // 2) % 4
    mine = (owners % 2 == core) & (owners // 8 == class_z)
    order = jnp.cumsum(mine.astype(jnp.int32)) - 1
    hit = mine[None, :] & (order[None, :] == jnp.arange(LINKS, dtype=jnp.int32)[:, None])
    target_of = jnp.arange(2 * PAIRS * 8, dtype=jnp.int32) // 8
    x_even, x_odd = ways((owner_x - x) % 4, x)
    z_even, z_odd = ways((slots // 4 - z) % 4, z)
    bits = (
        (x_even, z_even, x_odd, z_odd),
        (z_even, x_even, z_odd, x_odd),
        (x_odd, z_odd, x_even, z_even),
        (z_odd, x_odd, z_even, x_even),
    )
    amp_list, amp_at = jnp.zeros_like(slots), jnp.zeros_like(slots)
    for k in range(4):
        b = bits[k]
        amp_list = jnp.where(slots % 4 == k, 4 * k + 2 * b[3] + b[2], amp_list)
        amp_at = jnp.where(slots % 4 == k, b[0] + 2 * b[1], amp_at)
    columns = jnp.stack(
        [
            target_of, slots, (owner_x - x) % 4, (slots // 4 - z) % 4, x_even, x_odd, amp_list, amp_at,
        ]
    )
    info = jnp.sum(jnp.where(hit[None], columns[:, None, :], 0), axis=2).astype(jnp.int32)
    fock = jnp.sum(jnp.where(hit, table[1][None, :], 0.0), axis=1)[None, :]

    for step in range(3):
        got = [lax.ppermute(colours[k], *STEPS[k][step]) for k in range(4)]
        if step < 2:
            colours = [jnp.concatenate([colours[k], got[k]]) for k in range(4)]
    held_domains = jnp.concatenate([colours[0][:, COLOUR:], got[0][:, COLOUR:]])
    got_domains = lax.ppermute(held_domains, *STEPS[0][3])
    got[3] = jnp.concatenate([got[3], got_domains[:4]], axis=1)
    lists = []
    for k in range(4):
        pieces = [colours[k], got[k]]
        pieces += [lax.ppermute(piece, *STEPS[k][3]) for piece in pieces]
        lists += [piece.reshape(2, 2, -1, PNO) for piece in pieces]

    lean = 1 - 2 * (z % 2)
    ranges = jnp.stack([z, z + lean, z - lean, z + 2]) % 4
    place = jnp.concatenate([4 * core + ranges, 4 * (1 - core) + ranges])
    picked = pl.pallas_call(
        pick_kernel,
        out_shape=jax.ShapeDtypeStruct((LINKS, PNO, RANGES * PNO), BF16),
        in_specs=[SM, SM, VM, VM, VM],
        out_specs=VM,
        scratch_shapes=[
            pltpu.VMEM((2 * PAIRS, RANGES, PNO, NB), BF16),
            pltpu.VMEM((2 * RANGES, PAIRS, PNO), F32),
            pltpu.VMEM((2, 8, PAIRS, PNO), F32),
        ],
        compiler_params=params(20),
        name="pick_targets",
    )(info, place.astype(jnp.int32), targets, held_domains, got_domains)

    inter, own, other = pl.pallas_call(
        first_kernel,
        out_shape=(jax.ShapeDtypeStruct((LINKS, PNO, PNO), BF16), BLOCK, BLOCK),
        in_specs=[SM, SM] + [HB] * 16 + [VM],
        out_specs=(VM, VM, VM),
        scratch_shapes=[
            pltpu.VMEM((LINKS, 2, 2, PNO, PNO), BF16),
            pltpu.VMEM((LINKS, PNO, PNO), BF16),
            pltpu.VMEM((2 * PAIRS, PNO, PNO), F32),
            pltpu.SemaphoreType.DMA((LINKS,)),
            pltpu.SemaphoreType.DMA((LINKS,)),
        ],
        compiler_params=params(19),
        name="intersect_and_project",
    )(info, fock, *lists, picked)

    energy = lax.dynamic_slice_in_dim(pno_energy, 4 * y, 4, 0)
    shift = lax.dynamic_slice_in_dim(pair_shift, 4 * y, 4, 0)
    exchange = lax.dynamic_slice_in_dim(exchange_integrals, 4 * y, 4, 0)
    denominator = energy[:, :, None] + energy[:, None, :] + shift[:, None, None]

    amplitudes = -(exchange + reduce_core_y(own, other, y)) / denominator
    sent = to_class_plane(amplitudes.astype(BF16).reshape(4 * PNO, PNO))
    a_refs, b_refs = plane_gather(sent[: 2 * PNO], sent[2 * PNO :])
    own, other = pl.pallas_call(
        next_kernel,
        out_shape=(BLOCK, BLOCK),
        in_specs=[SM, SM] + [VM] * 9,
        out_specs=(VM, VM),
        scratch_shapes=[
            pltpu.VMEM((LINKS, PNO, PNO), BF16),
            pltpu.VMEM((2 * PAIRS, PNO, PNO), F32),
        ],
        compiler_params=params(12),
        name="project",
    )(info, fock, inter, *a_refs, *b_refs)
    amplitudes = -(exchange + reduce_core_y(own, other, y)) / denominator
    gathered = ring(amplitudes, "grp")
    result = jnp.zeros_like(exchange_integrals)
    for d in range(4):
        result = lax.dynamic_update_slice_in_dim(result, gathered[d], 4 * ((y + d) % 4), 0)
    return result


def solution(mesh):
    fine = Mesh(mesh.devices.reshape(4, 4, 2, 4), ("z", "x", "core", "grp"))
    placed = (
        P(SPLIT, "grp", None),
        P(SPLIT, "grp"),
        P(SPLIT, None),
        P(SPLIT, None),
        P(SPLIT, None),
        P(SPLIT, None, None),
        P(SPLIT, None),
        P(SPLIT),
        P(SPLIT, None, None),
    )
    return jax.shard_map(
        on_device, mesh=fine, in_specs=placed, out_specs=P(SPLIT, None, None), check_vma=False
    )
```

```python
import jax
import jax.numpy as jnp
from jax import lax
from jax.experimental import pallas as pl
from jax.experimental.pallas import tpu as pltpu
from jax.sharding import Mesh, PartitionSpec as P

NB = 192
RANGES = 4
PAIRS = 16
PNO = 128
LINKS = 40
UNROLL = 8
ORBITALS = 4 * PNO
COLOUR = ORBITALS + PNO
EVEN = [(0, 1), (1, 0), (2, 3), (3, 2)]
ODD = [(1, 2), (2, 1), (3, 0), (0, 3)]
STEPS = (
    (("x", EVEN), ("z", EVEN), ("x", ODD), ("z", ODD)),
    (("z", EVEN), ("x", EVEN), ("z", ODD), ("x", ODD)),
    (("x", ODD), ("z", ODD), ("x", EVEN), ("z", EVEN)),
    (("z", ODD), ("x", ODD), ("z", EVEN), ("x", EVEN)),
)
BF16 = jnp.bfloat16
F32 = jnp.float32
SPLIT = ("z", "x", "core")
TARGET, SLOT, REL_X, REL_Z, X_EVEN, X_ODD, AMP_LIST, AMP_AT = range(8)


def one_hot(row):
    functions = lax.broadcasted_iota(jnp.int32, (NB, PNO), 0).astype(F32)
    return jnp.where(functions == row, 1.0, 0.0).astype(BF16)


def ways(rel, here):
    lean = 1 + 2 * lax.rem(here, 2)
    even = (rel == 2) | (rel == lean)
    odd = (rel == 2) | (rel == 4 - lean)
    return even.astype(jnp.int32), odd.astype(jnp.int32)


def list_couplings(place, table, other_table, info, fock):
    z, x, core, class_z = [place[2 * RANGES + i] for i in range(4)]

    def clear(j, carry):
        for i in range(8):
            info[i, j] = 0
        fock[0, j] = 0.0
        return carry

    lax.fori_loop(0, LINKS, clear, 0)
    count = jnp.int32(0)
    for block, ref in enumerate((table, other_table)):

        def look(i, count):
            named = ref[0, i].astype(jnp.int32)
            owner, slot = lax.div(named, PAIRS), lax.rem(named, PAIRS)
            mine = (lax.rem(owner, 2) == core) & (lax.div(owner, 8) == class_z)

            @pl.when(mine)
            def _():
                rel_x = lax.rem(lax.rem(lax.div(owner, 2), 4) - x + 4, 4)
                rel_z = lax.rem(lax.div(slot, 4) - z + 4, 4)
                x_even, x_odd = ways(rel_x, x)
                z_even, z_odd = ways(rel_z, z)
                colour = lax.rem(slot, 4)
                x_first = lax.rem(colour, 2) == 0
                even_first = colour < 2
                x_one, x_two = jnp.where(even_first, x_even, x_odd), jnp.where(
                    even_first, x_odd, x_even
                )
                z_one, z_two = jnp.where(even_first, z_even, z_odd), jnp.where(
                    even_first, z_odd, z_even
                )
                near = jnp.where(x_first, x_one + 2 * z_one, z_one + 2 * x_one)
                far, last = jnp.where(x_first, x_two, z_two), jnp.where(x_first, z_two, x_two)
                info[TARGET, count] = block * PAIRS + lax.div(i, 8)
                info[SLOT, count] = slot
                info[REL_X, count] = rel_x
                info[REL_Z, count] = rel_z
                info[X_EVEN, count] = x_even
                info[X_ODD, count] = x_odd
                info[AMP_LIST, count] = 2 * colour + last
                info[AMP_AT, count] = near + 4 * far
                fock[0, count] = ref[1, i]

            return count + mine.astype(jnp.int32)

        count = lax.fori_loop(0, PAIRS * 8, look, count)


def pick_kernel(
    place, table, other_table, gathered, held, got,
    info, fock, picked, targets, expanded, dom, source_dom, sem,
):
    copy = pltpu.make_async_copy(
        gathered.at[:, pl.ds(0, PAIRS * PNO + PAIRS)], targets, sem
    )
    copy.start()
    list_couplings(place, table, other_table, info, fock)
    copy.wait()
    for i in range(2 * RANGES):
        dom[i] = targets[i, PAIRS * PNO : PAIRS * PNO + PAIRS, :].astype(F32)
    for i in range(8):
        source_dom[0, i] = held[i].astype(F32)
        source_dom[1, i] = got[i].astype(F32)

    def expand(i, carry):
        for block in range(2):
            for r in range(RANGES):
                d = place[4 * block + r]
                hot = one_hot(dom[d, pl.ds(i, 1), :])
                rows = targets[d, pl.ds(pl.multiple_of(i * PNO, PNO), PNO), :]
                full = jnp.dot(hot, rows, preferred_element_type=F32)
                expanded[block * PAIRS + i, r] = full.T.astype(BF16)
        return carry

    lax.fori_loop(0, PAIRS, expand, 0)

    def pick(step, carry):
        for u in range(4):
            j = step * 4 + u
            for r in range(RANGES):
                at = 4 * info[X_ODD, j] + 2 * (r % 2) + info[X_EVEN, j]
                row = source_dom[r // 2, at, pl.ds(info[SLOT, j], 1), :]
                part = jnp.dot(
                    expanded[info[TARGET, j], r], one_hot(row), preferred_element_type=F32
                )
                picked[j, :, r * PNO : (r + 1) * PNO] = part.astype(BF16)
        return carry

    lax.fori_loop(0, LINKS // 4, pick, 0)


def choose(which, low, high, act):
    if high - low == 1:
        act(low)
        return
    middle = (low + high) // 2

    @pl.when(which < middle)
    def _():
        choose(which, low, middle, act)

    @pl.when(which >= middle)
    def _():
        choose(which, middle, high, act)


def fetch_amplitudes(info, j, a_refs, b_refs, amp):
    rx, slot, rz = info[REL_X, j], info[SLOT, j], info[REL_Z, j]
    rows = pl.ds(pl.multiple_of(lax.rem(slot, 2) * PNO, PNO), PNO)

    def from_a(r):
        amp[j] = a_refs[r][rx, rows, :]

    def from_b(r):
        amp[j] = b_refs[r][rz, rows, :]

    @pl.when(lax.rem(slot, 4) < 2)
    def _():
        choose(rz, 0, 4, from_a)

    @pl.when(lax.rem(slot, 4) >= 2)
    def _():
        choose(rx, 0, 4, from_b)


def project_all(info, fock, inter, amp, acc):
    def body(step, carry):
        for u in range(UNROLL):
            j = step * UNROLL + u
            block, target = inter[j], info[TARGET, j]
            half = jnp.dot(block, amp[j], preferred_element_type=F32).astype(BF16)
            whole = lax.dot_general(
                half, block, (((1,), (1,)), ((), ())), preferred_element_type=F32
            )
            acc[target] = acc[target] + fock[0, j] * whole
        return carry

    lax.fori_loop(0, LINKS // UNROLL, body, 0)


def first_kernel(info, fock, *refs):
    lists, picked = refs[0:8], refs[8]
    inter, own, other = refs[9:12]
    source, amp, acc, sem, amp_sem = refs[12:]

    def fetch(j, carry):
        slot, even, odd = info[SLOT, j], info[X_EVEN, j], info[X_ODD, j]
        rows = pl.ds(pl.multiple_of(lax.rem(slot, 4) * PNO, PNO), PNO)

        def copy(src, dst):
            pltpu.make_async_copy(src, dst, sem.at[j]).start()

        def from_colour(colour):
            if colour == 0:
                for bit in range(2):
                    copy(lists[bit].at[odd, :, even, rows], source.at[j, bit])
            elif colour == 1:
                choose(odd, 0, 2, lambda last: copy(
                    lists[2 + last].at[:, even, :, rows], source.at[j]
                ))
            elif colour == 2:
                for bit in range(2):
                    copy(lists[4 + bit].at[even, :, odd, rows], source.at[j, :, bit])
            else:
                choose(even, 0, 2, lambda last: [
                    copy(lists[6 + last].at[bit, odd, :, rows], source.at[j, :, bit])
                    for bit in range(2)
                ])

        choose(lax.div(slot, 4), 0, 4, from_colour)
        at = info[AMP_AT, j]
        far, middle, near = lax.div(at, 4), lax.rem(lax.div(at, 2), 2), lax.rem(at, 2)
        choose(info[AMP_LIST, j], 0, 8, lambda i: pltpu.make_async_copy(
            lists[i].at[far, middle, near, pl.ds(ORBITALS, PNO)], amp.at[j], amp_sem.at[j]
        ).start())
        return carry

    lax.fori_loop(0, LINKS, fetch, 0)
    acc[...] = jnp.zeros_like(acc)

    def intersect(step, carry):
        for u in range(UNROLL):
            j = step * UNROLL + u
            pltpu.make_async_copy(source.at[j], source.at[j], sem.at[j]).wait()
            pltpu.make_async_copy(amp.at[j], amp.at[j], amp_sem.at[j]).wait()
        for u in range(UNROLL):
            j = step * UNROLL + u
            rows = source[j].reshape(RANGES * PNO, PNO)
            block = jnp.dot(picked[j], rows, preferred_element_type=F32)
            inter[j] = block.astype(BF16)
        return carry

    lax.fori_loop(0, LINKS // UNROLL, intersect, 0)
    project_all(info, fock, inter, amp, acc)
    own[...] = acc[0:PAIRS]
    other[...] = acc[PAIRS:].astype(other.dtype)


def next_kernel(info, fock, inter, *refs):
    a_refs, b_refs = refs[0:4], refs[4:8]
    own, other = refs[8:10]
    amp, acc = refs[10:]

    def fetch(j, carry):
        fetch_amplitudes(info, j, a_refs, b_refs, amp)
        return carry

    lax.fori_loop(0, LINKS, fetch, 0)
    acc[...] = jnp.zeros_like(acc)

    project_all(info, fock, inter, amp, acc)
    own[...] = acc[0:PAIRS]
    other[...] = acc[PAIRS:].astype(other.dtype)


VM = pl.BlockSpec(memory_space=pltpu.VMEM)
SM = pl.BlockSpec(memory_space=pltpu.SMEM)
HB = pl.BlockSpec(memory_space=pl.ANY)


def params(mib):
    return pltpu.CompilerParams(vmem_limit_bytes=mib * 1024 * 1024)


BLOCK = jax.ShapeDtypeStruct((PAIRS, PNO, PNO), F32)


def shifted(value, axis, rel):
    return lax.ppermute(value, axis, [((i + rel) % 4, i) for i in range(4)])


def ring(value, axis):
    plus, minus = shifted(value, axis, 1), shifted(value, axis, 3)
    return [value, plus, shifted(value, axis, 2), minus]


def swap_core(value):
    return lax.ppermute(value, "core", [(0, 1), (1, 0)])


def to_class_plane(value):
    moves = []
    for z in range(4):
        for core in range(2):
            for y in range(4):
                moves.append(
                    ((z * 2 + core) * 4 + y, (y * 2 + core) * 4 + (z + 2 * core) % 4)
                )
    return lax.ppermute(value, ("z", "core", "grp"), moves)


def plane_gather(half_a, half_b):
    a, b = lax.optimization_barrier(
        (jnp.stack(ring(half_a, "x")), jnp.stack(ring(half_b, "z")))
    )
    return ring(a, "z"), ring(b, "x")


def reduce_core_y(own, other, y):
    total = own + swap_core(other)
    pieces = [lax.dynamic_slice_in_dim(total, 4 * ((y + d) % 4), 4, 0) for d in range(4)]
    result = pieces[0]
    for d in (1, 3, 2):
        result = result + shifted(pieces[d], "grp", 4 - d)
    return result


def on_device(
    coefficients,
    domain,
    coupling_owner,
    coupling_slot,
    coupling_fock,
    exchange_integrals,
    pno_energy,
    pair_shift,
    amplitudes_start,
):
    z, x, core, y = [lax.axis_index(name) for name in ("z", "x", "core", "grp")]
    class_z = (y + 2 * core) % 4
    flat = coefficients.reshape(PAIRS * PNO, PNO)
    local = (domain - y * NB).astype(BF16)
    start = lax.dynamic_slice_in_dim(amplitudes_start, 4 * y, 4, 0).astype(BF16)
    start = start.reshape(4 * PNO, PNO)
    colours = []
    for k in range(4):
        rows = [flat[k * ORBITALS : (k + 1) * ORBITALS], start[k * PNO : (k + 1) * PNO]]
        if k == 0:
            rows.append(local)
        colours.append(to_class_plane(jnp.concatenate(rows))[None])
    arrived = [colours[k][0, :PAIRS] for k in range(4)]
    own_targets = jnp.concatenate([flat, local, *arrived])
    targets = lax.all_gather(own_targets, ("core", "grp"))

    table = jnp.stack(
        [(coupling_owner * PAIRS + coupling_slot).astype(F32), coupling_fock]
    ).reshape(2, -1)
    other_table = swap_core(table)

    for step in range(3):
        got = [lax.ppermute(colours[k], *STEPS[k][step]) for k in range(4)]
        if step == 2:
            held_domains = jnp.concatenate([colours[0][:, COLOUR:], got[0][:, COLOUR:]])
        colours = [jnp.concatenate([colours[k], got[k]]) for k in range(4)]
    got_domains = lax.ppermute(held_domains, *STEPS[0][3])
    colours[3] = jnp.concatenate([colours[3], got_domains], axis=1)
    got = [lax.ppermute(colours[k], *STEPS[k][3]) for k in range(4)]
    lists = []
    for k in range(4):
        lists.append(colours[k].reshape(2, 2, 2, -1, PNO))
        lists.append(got[k].reshape(2, 2, 2, -1, PNO))

    lean = 1 - 2 * (z % 2)
    ranges = jnp.stack([z, z + lean, z - lean, z + 2]) % 4
    place = jnp.concatenate(
        [4 * core + ranges, 4 * (1 - core) + ranges, jnp.stack([z, x, core, class_z])]
    )
    info, fock, picked = pl.pallas_call(
        pick_kernel,
        out_shape=(
            jax.ShapeDtypeStruct((8, LINKS), jnp.int32),
            jax.ShapeDtypeStruct((1, LINKS), F32),
            jax.ShapeDtypeStruct((LINKS, PNO, RANGES * PNO), BF16),
        ),
        in_specs=[SM, SM, SM, HB, VM, VM],
        out_specs=(SM, SM, VM),
        scratch_shapes=[
            pltpu.VMEM((2 * RANGES, PAIRS * PNO + PAIRS, PNO), BF16),
            pltpu.VMEM((2 * PAIRS, RANGES, PNO, NB), BF16),
            pltpu.VMEM((2 * RANGES, PAIRS, PNO), F32),
            pltpu.VMEM((2, 8, PAIRS, PNO), F32),
            pltpu.SemaphoreType.DMA,
        ],
        compiler_params=params(22),
        name="pick_targets",
    )(place.astype(jnp.int32), table, other_table, targets, held_domains, got_domains)

    inter, own, other = pl.pallas_call(
        first_kernel,
        out_shape=(jax.ShapeDtypeStruct((LINKS, PNO, PNO), BF16), BLOCK, BLOCK),
        in_specs=[SM, SM] + [HB] * 8 + [VM],
        out_specs=(VM, VM, VM),
        scratch_shapes=[
            pltpu.VMEM((LINKS, 2, 2, PNO, PNO), BF16),
            pltpu.VMEM((LINKS, PNO, PNO), BF16),
            pltpu.VMEM((2 * PAIRS, PNO, PNO), F32),
            pltpu.SemaphoreType.DMA((LINKS,)),
            pltpu.SemaphoreType.DMA((LINKS,)),
        ],
        compiler_params=params(19),
        name="intersect_and_project",
    )(info, fock, *lists, picked)

    energy = lax.dynamic_slice_in_dim(pno_energy, 4 * y, 4, 0)
    shift = lax.dynamic_slice_in_dim(pair_shift, 4 * y, 4, 0)
    exchange = lax.dynamic_slice_in_dim(exchange_integrals, 4 * y, 4, 0)
    denominator = energy[:, :, None] + energy[:, None, :] + shift[:, None, None]

    amplitudes = -(exchange + reduce_core_y(own, other, y)) / denominator
    sent = to_class_plane(amplitudes.astype(BF16).reshape(4 * PNO, PNO))
    a_refs, b_refs = plane_gather(sent[: 2 * PNO], sent[2 * PNO :])
    own, other = pl.pallas_call(
        next_kernel,
        out_shape=(BLOCK, BLOCK),
        in_specs=[SM, SM] + [VM] * 9,
        out_specs=(VM, VM),
        scratch_shapes=[
            pltpu.VMEM((LINKS, PNO, PNO), BF16),
            pltpu.VMEM((2 * PAIRS, PNO, PNO), F32),
        ],
        compiler_params=params(12),
        name="project",
    )(info, fock, inter, *a_refs, *b_refs)
    amplitudes = -(exchange + reduce_core_y(own, other, y)) / denominator
    gathered = ring(amplitudes, "grp")
    result = jnp.zeros_like(exchange_integrals)
    for d in range(4):
        result = lax.dynamic_update_slice_in_dim(result, gathered[d], 4 * ((y + d) % 4), 0)
    return result


def solution(mesh):
    fine = Mesh(mesh.devices.reshape(4, 4, 2, 4), ("z", "x", "core", "grp"))
    placed = (
        P(SPLIT, "grp", None),
        P(SPLIT, "grp"),
        P(SPLIT, None),
        P(SPLIT, None),
        P(SPLIT, None),
        P(SPLIT, None, None),
        P(SPLIT, None),
        P(SPLIT),
        P(SPLIT, None, None),
    )
    return jax.shard_map(
        on_device, mesh=fine, in_specs=placed, out_specs=P(SPLIT, None, None), check_vma=False
    )
```

```python
import jax
import jax.numpy as jnp
from jax import lax
from jax.experimental import pallas as pl
from jax.experimental.pallas import tpu as pltpu
from jax.sharding import Mesh, PartitionSpec as P

NB = 192
RANGES = 4
PAIRS = 16
PNO = 128
LINKS = 40
UNROLL = 8
ORBITALS = 4 * PNO
COLOUR = ORBITALS + PNO
EVEN = [(0, 1), (1, 0), (2, 3), (3, 2)]
ODD = [(1, 2), (2, 1), (3, 0), (0, 3)]
STEPS = (
    (("x", EVEN), ("z", EVEN), ("x", ODD), ("z", ODD)),
    (("z", EVEN), ("x", EVEN), ("z", ODD), ("x", ODD)),
    (("x", ODD), ("z", ODD), ("x", EVEN), ("z", EVEN)),
    (("z", ODD), ("x", ODD), ("z", EVEN), ("x", EVEN)),
)
BF16 = jnp.bfloat16
F32 = jnp.float32
SPLIT = ("z", "x", "core")
TARGET, SLOT, REL_X, REL_Z, X_EVEN, X_ODD, AMP_LIST, AMP_AT = range(8)


def one_hot(row):
    functions = lax.broadcasted_iota(jnp.int32, (NB, PNO), 0).astype(F32)
    return jnp.where(functions == row, 1.0, 0.0).astype(BF16)


def ways(rel, here):
    lean = 1 + 2 * lax.rem(here, 2)
    even = (rel == 2) | (rel == lean)
    odd = (rel == 2) | (rel == 4 - lean)
    return even.astype(jnp.int32), odd.astype(jnp.int32)


FIELDS = (5, 4, 2, 2, 1, 1, 3, 3)


def pack_couplings(named, z, x, core, class_z):
    owner, slot = named // PAIRS, named % PAIRS
    mine = (owner % 2 == core) & (owner // 8 == class_z)
    rel_x, rel_z = ((owner // 2) % 4 - x) % 4, (slot // 4 - z) % 4
    x_even, x_odd = ways(rel_x, x)
    z_even, z_odd = ways(rel_z, z)
    colour = slot % 4
    x_first, even_first = colour % 2 == 0, colour < 2
    x_one, x_two = jnp.where(even_first, x_even, x_odd), jnp.where(even_first, x_odd, x_even)
    z_one, z_two = jnp.where(even_first, z_even, z_odd), jnp.where(even_first, z_odd, z_even)
    near = jnp.where(x_first, x_one + 2 * z_one, z_one + 2 * x_one)
    far, last = jnp.where(x_first, x_two, z_two), jnp.where(x_first, z_two, x_two)
    target = lax.broadcasted_iota(jnp.int32, named.shape, 0) * PAIRS
    target = target + lax.broadcasted_iota(jnp.int32, named.shape, 1) // 8
    values = (target, slot, rel_x, rel_z, x_even, x_odd, 2 * colour + last, near + 4 * far)
    code, place = 0, 1
    for bits, value in zip(FIELDS, values):
        code = code + value * place
        place *= 2**bits
    return jnp.where(mine, code, -1).astype(jnp.int32)


def list_couplings(packed, tables, info, fock, found):
    def clear(j, carry):
        found[j] = 0
        fock[0, j] = 0.0
        return carry

    lax.fori_loop(0, LINKS + 1, clear, 0)
    count = jnp.int32(0)
    for block in range(2):

        def look(step, count):
            for u in range(8):
                code = packed[block, step * 8 + u]
                fits = (code >= 0).astype(jnp.int32)
                spot = jnp.where(code >= 0, count, LINKS)
                found[spot] = code
                fock[0, spot] = tables[block, 1, step * 8 + u]
                count = count + fits
            return count

        count = lax.fori_loop(0, PAIRS, look, count)

    def unpack(j, carry):
        code = found[j]
        for row, bits in enumerate(FIELDS):
            info[row, j] = lax.rem(code, 2**bits)
            code = lax.div(code, 2**bits)
        return carry

    lax.fori_loop(0, LINKS, unpack, 0)


def pick_kernel(
    place, packed, tables, targets, held, got,
    info, fock, picked, expanded, dom, source_dom, found,
):
    list_couplings(packed, tables, info, fock, found)
    for i in range(2 * RANGES):
        dom[i] = targets[i, PAIRS * PNO : PAIRS * PNO + PAIRS, :].astype(F32)
    for i in range(8):
        source_dom[0, i] = held[i].astype(F32)
        source_dom[1, i] = got[i].astype(F32)

    def expand(i, carry):
        for block in range(2):
            for r in range(RANGES):
                d = place[4 * block + r]
                hot = one_hot(dom[d, pl.ds(i, 1), :])
                rows = targets[d, pl.ds(pl.multiple_of(i * PNO, PNO), PNO), :]
                full = jnp.dot(hot, rows, preferred_element_type=F32)
                expanded[block * PAIRS + i, r] = full.T.astype(BF16)
        return carry

    lax.fori_loop(0, PAIRS, expand, 0)

    def pick(step, carry):
        for u in range(4):
            j = step * 4 + u
            for r in range(RANGES):
                at = 4 * info[X_ODD, j] + 2 * (r % 2) + info[X_EVEN, j]
                row = source_dom[r // 2, at, pl.ds(info[SLOT, j], 1), :]
                part = jnp.dot(
                    expanded[info[TARGET, j], r], one_hot(row), preferred_element_type=F32
                )
                picked[j, :, r * PNO : (r + 1) * PNO] = part.astype(BF16)
        return carry

    lax.fori_loop(0, LINKS // 4, pick, 0)


def choose(which, low, high, act):
    if high - low == 1:
        act(low)
        return
    middle = (low + high) // 2

    @pl.when(which < middle)
    def _():
        choose(which, low, middle, act)

    @pl.when(which >= middle)
    def _():
        choose(which, middle, high, act)


def fetch_amplitudes(info, j, a_refs, b_refs, amp):
    rx, slot, rz = info[REL_X, j], info[SLOT, j], info[REL_Z, j]
    rows = pl.ds(pl.multiple_of(lax.rem(slot, 2) * PNO, PNO), PNO)

    def from_a(r):
        amp[j] = a_refs[r][rx, rows, :]

    def from_b(r):
        amp[j] = b_refs[r][rz, rows, :]

    @pl.when(lax.rem(slot, 4) < 2)
    def _():
        choose(rz, 0, 4, from_a)

    @pl.when(lax.rem(slot, 4) >= 2)
    def _():
        choose(rx, 0, 4, from_b)


def project_all(info, fock, inter, amp, acc):
    def body(step, carry):
        for u in range(UNROLL):
            j = step * UNROLL + u
            block, target = inter[j], info[TARGET, j]
            half = jnp.dot(block, amp[j], preferred_element_type=F32).astype(BF16)
            whole = lax.dot_general(
                half, block, (((1,), (1,)), ((), ())), preferred_element_type=F32
            )
            acc[target] = acc[target] + fock[0, j] * whole
        return carry

    lax.fori_loop(0, LINKS // UNROLL, body, 0)


def first_kernel(info, fock, *refs):
    lists, picked = refs[0:8], refs[8]
    inter, own, other = refs[9:12]
    source, amp, acc, sem, amp_sem = refs[12:]

    def fetch(j, carry):
        slot, even, odd = info[SLOT, j], info[X_EVEN, j], info[X_ODD, j]
        rows = pl.ds(pl.multiple_of(lax.rem(slot, 4) * PNO, PNO), PNO)

        def copy(src, dst):
            pltpu.make_async_copy(src, dst, sem.at[j]).start()

        def from_colour(colour):
            if colour == 0:
                for bit in range(2):
                    copy(lists[bit].at[odd, :, even, rows], source.at[j, bit])
            elif colour == 1:
                choose(odd, 0, 2, lambda last: copy(
                    lists[2 + last].at[:, even, :, rows], source.at[j]
                ))
            elif colour == 2:
                for bit in range(2):
                    copy(lists[4 + bit].at[even, :, odd, rows], source.at[j, :, bit])
            else:
                choose(even, 0, 2, lambda last: [
                    copy(lists[6 + last].at[bit, odd, :, rows], source.at[j, :, bit])
                    for bit in range(2)
                ])

        choose(lax.div(slot, 4), 0, 4, from_colour)
        at = info[AMP_AT, j]
        far, middle, near = lax.div(at, 4), lax.rem(lax.div(at, 2), 2), lax.rem(at, 2)
        choose(info[AMP_LIST, j], 0, 8, lambda i: pltpu.make_async_copy(
            lists[i].at[far, middle, near, pl.ds(ORBITALS, PNO)], amp.at[j], amp_sem.at[j]
        ).start())
        return carry

    lax.fori_loop(0, LINKS, fetch, 0)
    acc[...] = jnp.zeros_like(acc)

    def intersect(step, carry):
        for u in range(UNROLL):
            j = step * UNROLL + u
            pltpu.make_async_copy(source.at[j], source.at[j], sem.at[j]).wait()
            pltpu.make_async_copy(amp.at[j], amp.at[j], amp_sem.at[j]).wait()
        for u in range(UNROLL):
            j = step * UNROLL + u
            rows = source[j].reshape(RANGES * PNO, PNO)
            block = jnp.dot(picked[j], rows, preferred_element_type=F32)
            inter[j] = block.astype(BF16)
        return carry

    lax.fori_loop(0, LINKS // UNROLL, intersect, 0)
    project_all(info, fock, inter, amp, acc)
    own[...] = acc[0:PAIRS]
    other[...] = acc[PAIRS:].astype(other.dtype)


def next_kernel(info, fock, inter, *refs):
    a_refs, b_refs = refs[0:4], refs[4:8]
    own, other = refs[8:10]
    amp, acc = refs[10:]

    def fetch(j, carry):
        fetch_amplitudes(info, j, a_refs, b_refs, amp)
        return carry

    lax.fori_loop(0, LINKS, fetch, 0)
    acc[...] = jnp.zeros_like(acc)

    project_all(info, fock, inter, amp, acc)
    own[...] = acc[0:PAIRS]
    other[...] = acc[PAIRS:].astype(other.dtype)


VM = pl.BlockSpec(memory_space=pltpu.VMEM)
SM = pl.BlockSpec(memory_space=pltpu.SMEM)
HB = pl.BlockSpec(memory_space=pl.ANY)


def params(mib):
    return pltpu.CompilerParams(vmem_limit_bytes=mib * 1024 * 1024)


BLOCK = jax.ShapeDtypeStruct((PAIRS, PNO, PNO), F32)


def shifted(value, axis, rel):
    return lax.ppermute(value, axis, [((i + rel) % 4, i) for i in range(4)])


def ring(value, axis):
    plus, minus = shifted(value, axis, 1), shifted(value, axis, 3)
    return [value, plus, shifted(value, axis, 2), minus]


def swap_core(value):
    return lax.ppermute(value, "core", [(0, 1), (1, 0)])


def to_class_plane(value):
    moves = []
    for z in range(4):
        for core in range(2):
            for y in range(4):
                moves.append(
                    ((z * 2 + core) * 4 + y, (y * 2 + core) * 4 + (z + 2 * core) % 4)
                )
    return lax.ppermute(value, ("z", "core", "grp"), moves)


def plane_gather(half_a, half_b):
    a, b = lax.optimization_barrier(
        (jnp.stack(ring(half_a, "x")), jnp.stack(ring(half_b, "z")))
    )
    return ring(a, "z"), ring(b, "x")


def reduce_core_y(own, other, y, dtype):
    total = own + swap_core(other)
    pieces = [lax.dynamic_slice_in_dim(total, 4 * ((y + d) % 4), 4, 0) for d in range(4)]
    result = pieces[0]
    for d in (1, 3, 2):
        arrived = shifted(pieces[d].astype(dtype), "grp", 4 - d)
        result = result + arrived.astype(F32)
    return result


def on_device(
    coefficients,
    domain,
    coupling_owner,
    coupling_slot,
    coupling_fock,
    exchange_integrals,
    pno_energy,
    pair_shift,
    amplitudes_start,
):
    z, x, core, y = [lax.axis_index(name) for name in ("z", "x", "core", "grp")]
    class_z = (y + 2 * core) % 4
    flat = coefficients.reshape(PAIRS * PNO, PNO)
    local = (domain - y * NB).astype(BF16)
    start = lax.dynamic_slice_in_dim(amplitudes_start, 4 * y, 4, 0).astype(BF16)
    start = start.reshape(4 * PNO, PNO)
    flat_in, start_in, local_in = [to_class_plane(v) for v in (flat, start, local)]
    colours = []
    for k in range(4):
        rows = [
            flat_in[k * ORBITALS : (k + 1) * ORBITALS],
            start_in[k * PNO : (k + 1) * PNO],
        ]
        if k == 0:
            rows.append(local_in)
        colours.append(jnp.concatenate(rows)[None])

    table = jnp.stack(
        [(coupling_owner * PAIRS + coupling_slot).astype(F32), coupling_fock]
    ).reshape(2, -1)
    tables = jnp.stack([table, swap_core(table)])
    rest = jnp.concatenate([tables[1], jnp.zeros((PAIRS - 2, PNO), F32)]).astype(BF16)
    own_targets = jnp.concatenate([flat, local, flat_in[:PAIRS], start_in[:PAIRS], rest])
    targets = lax.all_gather(own_targets, ("core", "grp"))
    packed = pack_couplings(tables[:, 0].astype(jnp.int32), z, x, core, class_z)

    for step in range(3):
        got = [lax.ppermute(colours[k], *STEPS[k][step]) for k in range(4)]
        if step == 2:
            held_domains = jnp.concatenate([colours[0][:, COLOUR:], got[0][:, COLOUR:]])
        colours = [jnp.concatenate([colours[k], got[k]]) for k in range(4)]
    got_domains = lax.ppermute(held_domains, *STEPS[0][3])
    colours[3] = jnp.concatenate([colours[3], got_domains], axis=1)
    got = [lax.ppermute(colours[k], *STEPS[k][3]) for k in range(4)]
    lists = []
    for k in range(4):
        lists.append(colours[k].reshape(2, 2, 2, -1, PNO))
        lists.append(got[k].reshape(2, 2, 2, -1, PNO))

    lean = 1 - 2 * (z % 2)
    ranges = jnp.stack([z, z + lean, z - lean, z + 2]) % 4
    place = jnp.concatenate([4 * core + ranges, 4 * (1 - core) + ranges])
    info, fock, picked = pl.pallas_call(
        pick_kernel,
        out_shape=(
            jax.ShapeDtypeStruct((8, LINKS), jnp.int32),
            jax.ShapeDtypeStruct((1, LINKS + 1), F32),
            jax.ShapeDtypeStruct((LINKS, PNO, RANGES * PNO), BF16),
        ),
        in_specs=[SM, SM, SM, VM, VM, VM],
        out_specs=(SM, SM, VM),
        scratch_shapes=[
            pltpu.VMEM((2 * PAIRS, RANGES, PNO, NB), BF16),
            pltpu.VMEM((2 * RANGES, PAIRS, PNO), F32),
            pltpu.VMEM((2, 8, PAIRS, PNO), F32),
            pltpu.SMEM((LINKS + 1,), jnp.int32),
        ],
        compiler_params=params(22),
        name="pick_targets",
    )(place.astype(jnp.int32), packed, tables, targets, held_domains, got_domains)

    inter, own, other = pl.pallas_call(
        first_kernel,
        out_shape=(jax.ShapeDtypeStruct((LINKS, PNO, PNO), BF16), BLOCK, BLOCK),
        in_specs=[SM, SM] + [HB] * 8 + [VM],
        out_specs=(VM, VM, VM),
        scratch_shapes=[
            pltpu.VMEM((LINKS, 2, 2, PNO, PNO), BF16),
            pltpu.VMEM((LINKS, PNO, PNO), BF16),
            pltpu.VMEM((2 * PAIRS, PNO, PNO), F32),
            pltpu.SemaphoreType.DMA((LINKS,)),
            pltpu.SemaphoreType.DMA((LINKS,)),
        ],
        compiler_params=params(19),
        name="intersect_and_project",
    )(info, fock, *lists, picked)

    energy = lax.dynamic_slice_in_dim(pno_energy, 4 * y, 4, 0)
    shift = lax.dynamic_slice_in_dim(pair_shift, 4 * y, 4, 0)
    exchange = lax.dynamic_slice_in_dim(exchange_integrals, 4 * y, 4, 0)
    denominator = energy[:, :, None] + energy[:, None, :] + shift[:, None, None]

    amplitudes = -(exchange + reduce_core_y(own, other, y, F32)) / denominator
    sent = to_class_plane(amplitudes.astype(BF16).reshape(4 * PNO, PNO))
    a_refs, b_refs = plane_gather(sent[: 2 * PNO], sent[2 * PNO :])
    own, other = pl.pallas_call(
        next_kernel,
        out_shape=(BLOCK, BLOCK),
        in_specs=[SM, SM] + [VM] * 9,
        out_specs=(VM, VM),
        scratch_shapes=[
            pltpu.VMEM((LINKS, PNO, PNO), BF16),
            pltpu.VMEM((2 * PAIRS, PNO, PNO), F32),
        ],
        compiler_params=params(12),
        name="project",
    )(info, fock, inter, *a_refs, *b_refs)
    amplitudes = -(exchange + reduce_core_y(own, other, y, BF16)) / denominator
    gathered = ring(amplitudes, "grp")
    result = jnp.zeros_like(exchange_integrals)
    for d in range(4):
        result = lax.dynamic_update_slice_in_dim(result, gathered[d], 4 * ((y + d) % 4), 0)
    return result


def solution(mesh):
    fine = Mesh(mesh.devices.reshape(4, 4, 2, 4), ("z", "x", "core", "grp"))
    placed = (
        P(SPLIT, "grp", None),
        P(SPLIT, "grp"),
        P(SPLIT, None),
        P(SPLIT, None),
        P(SPLIT, None),
        P(SPLIT, None, None),
        P(SPLIT, None),
        P(SPLIT),
        P(SPLIT, None, None),
    )
    return jax.shard_map(
        on_device, mesh=fine, in_specs=placed, out_specs=P(SPLIT, None, None), check_vma=False
    )
```

```python
import jax
import jax.numpy as jnp
from jax import lax
from jax.experimental import pallas as pl
from jax.experimental.pallas import tpu as pltpu
from jax.sharding import Mesh, PartitionSpec as P

NB = 192
RANGES = 4
PAIRS = 16
PNO = 128
LINKS = 40
UNROLL = 8
ORBITALS = 4 * PNO
COLOUR = ORBITALS + PNO
EVEN = [(0, 1), (1, 0), (2, 3), (3, 2)]
ODD = [(1, 2), (2, 1), (3, 0), (0, 3)]
STEPS = (
    (("x", EVEN), ("z", EVEN), ("x", ODD), ("z", ODD)),
    (("z", EVEN), ("x", EVEN), ("z", ODD), ("x", ODD)),
    (("x", ODD), ("z", ODD), ("x", EVEN), ("z", EVEN)),
    (("z", ODD), ("x", ODD), ("z", EVEN), ("x", EVEN)),
)
BF16 = jnp.bfloat16
F32 = jnp.float32
SPLIT = ("z", "x", "core")
TARGET, SLOT, REL_X, REL_Z, X_EVEN, X_ODD, AMP_LIST, AMP_AT = range(8)


def one_hot(row):
    functions = lax.broadcasted_iota(jnp.int32, (NB, PNO), 0).astype(F32)
    return jnp.where(functions == row, 1.0, 0.0).astype(BF16)


def ways(rel, here):
    lean = 1 + 2 * lax.rem(here, 2)
    even = (rel == 2) | (rel == lean)
    odd = (rel == 2) | (rel == 4 - lean)
    return even.astype(jnp.int32), odd.astype(jnp.int32)


FIELDS = (5, 4, 2, 2, 1, 1, 3, 3)


def pack_couplings(named, z, x, core, class_z):
    owner, slot = named // PAIRS, named % PAIRS
    mine = (owner % 2 == core) & (owner // 8 == class_z)
    rel_x, rel_z = ((owner // 2) % 4 - x) % 4, (slot // 4 - z) % 4
    x_even, x_odd = ways(rel_x, x)
    z_even, z_odd = ways(rel_z, z)
    colour = slot % 4
    x_first, even_first = colour % 2 == 0, colour < 2
    x_one, x_two = jnp.where(even_first, x_even, x_odd), jnp.where(even_first, x_odd, x_even)
    z_one, z_two = jnp.where(even_first, z_even, z_odd), jnp.where(even_first, z_odd, z_even)
    near = jnp.where(x_first, x_one + 2 * z_one, z_one + 2 * x_one)
    far, last = jnp.where(x_first, x_two, z_two), jnp.where(x_first, z_two, x_two)
    target = lax.broadcasted_iota(jnp.int32, named.shape, 0) * PAIRS
    target = target + lax.broadcasted_iota(jnp.int32, named.shape, 1) // 8
    values = (target, slot, rel_x, rel_z, x_even, x_odd, 2 * colour + last, near + 4 * far)
    code, place = 0, 1
    for bits, value in zip(FIELDS, values):
        code = code + value * place
        place *= 2**bits
    return jnp.where(mine, code, -1).astype(jnp.int32)


def list_couplings(packed, tables, info, fock, found):
    def clear(j, carry):
        found[j] = 0
        fock[0, j] = 0.0
        return carry

    lax.fori_loop(0, LINKS + 1, clear, 0)
    count = jnp.int32(0)
    for block in range(2):

        def look(step, count):
            for u in range(8):
                code = packed[block, step * 8 + u]
                fits = (code >= 0).astype(jnp.int32)
                spot = jnp.where(code >= 0, count, LINKS)
                found[spot] = code
                fock[0, spot] = tables[block, 1, step * 8 + u]
                count = count + fits
            return count

        count = lax.fori_loop(0, PAIRS, look, count)

    def unpack(j, carry):
        code = found[j]
        for row, bits in enumerate(FIELDS):
            info[row, j] = lax.rem(code, 2**bits)
            code = lax.div(code, 2**bits)
        return carry

    lax.fori_loop(0, LINKS, unpack, 0)


def pick_kernel(
    place, packed, tables, targets, held, got,
    info, fock, picked, expanded, dom, source_dom, found,
):
    list_couplings(packed, tables, info, fock, found)
    for i in range(2 * RANGES):
        dom[i] = targets[i, PAIRS * PNO : PAIRS * PNO + PAIRS, :].astype(F32)
    for i in range(8):
        source_dom[0, i] = held[i].astype(F32)
        source_dom[1, i] = got[i].astype(F32)

    def expand(i, carry):
        for block in range(2):
            for r in range(RANGES):
                d = place[4 * block + r]
                hot = one_hot(dom[d, pl.ds(i, 1), :])
                rows = targets[d, pl.ds(pl.multiple_of(i * PNO, PNO), PNO), :]
                full = jnp.dot(hot, rows, preferred_element_type=F32)
                expanded[block * PAIRS + i, r] = full.T.astype(BF16)
        return carry

    lax.fori_loop(0, PAIRS, expand, 0)

    def pick(step, carry):
        for u in range(4):
            j = step * 4 + u
            for r in range(RANGES):
                at = 4 * info[X_ODD, j] + 2 * (r % 2) + info[X_EVEN, j]
                row = source_dom[r // 2, at, pl.ds(info[SLOT, j], 1), :]
                part = jnp.dot(
                    expanded[info[TARGET, j], r], one_hot(row), preferred_element_type=F32
                )
                picked[j, :, r * PNO : (r + 1) * PNO] = part.astype(BF16)
        return carry

    lax.fori_loop(0, LINKS // 4, pick, 0)


def choose(which, low, high, act):
    if high - low == 1:
        act(low)
        return
    middle = (low + high) // 2

    @pl.when(which < middle)
    def _():
        choose(which, low, middle, act)

    @pl.when(which >= middle)
    def _():
        choose(which, middle, high, act)


def fetch_amplitudes(info, j, a_refs, b_refs, amp):
    rx, slot, rz = info[REL_X, j], info[SLOT, j], info[REL_Z, j]
    rows = pl.ds(pl.multiple_of(lax.rem(slot, 2) * PNO, PNO), PNO)

    def from_a(r):
        amp[j] = a_refs[r][rx, rows, :]

    def from_b(r):
        amp[j] = b_refs[r][rz, rows, :]

    @pl.when(lax.rem(slot, 4) < 2)
    def _():
        choose(rz, 0, 4, from_a)

    @pl.when(lax.rem(slot, 4) >= 2)
    def _():
        choose(rx, 0, 4, from_b)


def project_all(info, fock, inter, amp, acc):
    def body(step, carry):
        for u in range(UNROLL):
            j = step * UNROLL + u
            block, target = inter[j], info[TARGET, j]
            half = jnp.dot(block, amp[j], preferred_element_type=F32).astype(BF16)
            whole = lax.dot_general(
                half, block, (((1,), (1,)), ((), ())), preferred_element_type=F32
            )
            acc[target] = acc[target] + fock[0, j] * whole
        return carry

    lax.fori_loop(0, LINKS // UNROLL, body, 0)


def first_kernel(info, fock, *refs):
    lists, picked = refs[0:8], refs[8]
    inter_out, own, other = refs[9:12]
    source, amp, acc, inter, sem, amp_sem, out_sem = refs[12:]

    def fetch(j, carry):
        slot, even, odd = info[SLOT, j], info[X_EVEN, j], info[X_ODD, j]
        rows = pl.ds(pl.multiple_of(lax.rem(slot, 4) * PNO, PNO), PNO)

        def copy(src, dst):
            pltpu.make_async_copy(src, dst, sem.at[j]).start()

        def from_colour(colour):
            if colour == 0:
                for bit in range(2):
                    copy(lists[bit].at[odd, :, even, rows], source.at[j, bit])
            elif colour == 1:
                choose(odd, 0, 2, lambda last: copy(
                    lists[2 + last].at[:, even, :, rows], source.at[j]
                ))
            elif colour == 2:
                for bit in range(2):
                    copy(lists[4 + bit].at[even, :, odd, rows], source.at[j, :, bit])
            else:
                choose(even, 0, 2, lambda last: [
                    copy(lists[6 + last].at[bit, odd, :, rows], source.at[j, :, bit])
                    for bit in range(2)
                ])

        choose(lax.div(slot, 4), 0, 4, from_colour)
        at = info[AMP_AT, j]
        far, middle, near = lax.div(at, 4), lax.rem(lax.div(at, 2), 2), lax.rem(at, 2)
        choose(info[AMP_LIST, j], 0, 8, lambda i: pltpu.make_async_copy(
            lists[i].at[far, middle, near, pl.ds(ORBITALS, PNO)], amp.at[j], amp_sem.at[j]
        ).start())
        return carry

    lax.fori_loop(0, LINKS, fetch, 0)
    acc[...] = jnp.zeros_like(acc)

    def intersect(step, carry):
        for u in range(UNROLL):
            j = step * UNROLL + u
            pltpu.make_async_copy(source.at[j], source.at[j], sem.at[j]).wait()
            pltpu.make_async_copy(amp.at[j], amp.at[j], amp_sem.at[j]).wait()
        for u in range(UNROLL):
            j = step * UNROLL + u
            rows = source[j].reshape(RANGES * PNO, PNO)
            block = jnp.dot(picked[j], rows, preferred_element_type=F32)
            inter[j] = block.astype(BF16)
        return carry

    lax.fori_loop(0, LINKS // UNROLL, intersect, 0)
    out = pltpu.make_async_copy(inter, inter_out, out_sem)
    out.start()
    project_all(info, fock, inter, amp, acc)
    out.wait()
    own[...] = acc[0:PAIRS]
    other[...] = acc[PAIRS:].astype(other.dtype)


def next_kernel(info, fock, inter, *refs):
    a_refs, b_refs = refs[0:4], refs[4:8]
    own, other = refs[8:10]
    amp, acc = refs[10:]

    def fetch(j, carry):
        fetch_amplitudes(info, j, a_refs, b_refs, amp)
        return carry

    lax.fori_loop(0, LINKS, fetch, 0)
    acc[...] = jnp.zeros_like(acc)

    project_all(info, fock, inter, amp, acc)
    own[...] = acc[0:PAIRS]
    other[...] = acc[PAIRS:].astype(other.dtype)


VM = pl.BlockSpec(memory_space=pltpu.VMEM)
SM = pl.BlockSpec(memory_space=pltpu.SMEM)
HB = pl.BlockSpec(memory_space=pl.ANY)


def params(mib):
    return pltpu.CompilerParams(vmem_limit_bytes=mib * 1024 * 1024)


BLOCK = jax.ShapeDtypeStruct((PAIRS, PNO, PNO), F32)


def shifted(value, axis, rel):
    return lax.ppermute(value, axis, [((i + rel) % 4, i) for i in range(4)])


def ring(value, axis):
    plus, minus = shifted(value, axis, 1), shifted(value, axis, 3)
    return [value, plus, shifted(value, axis, 2), minus]


def swap_core(value):
    return lax.ppermute(value, "core", [(0, 1), (1, 0)])


def to_class_plane(value):
    moves = []
    for z in range(4):
        for core in range(2):
            for y in range(4):
                moves.append(
                    ((z * 2 + core) * 4 + y, (y * 2 + core) * 4 + (z + 2 * core) % 4)
                )
    return lax.ppermute(value, ("z", "core", "grp"), moves)


def joined(held, got, extra=0):
    count, rows, columns = held.shape
    both = jnp.zeros((2 * count, rows + extra, columns), held.dtype)
    both = lax.optimization_barrier(lax.dynamic_update_slice(both, held, (0, 0, 0)))
    return lax.dynamic_update_slice(both, got, (count, 0, 0))


def plane_gather(half_a, half_b):
    a, b = lax.optimization_barrier(
        (jnp.stack(ring(half_a, "x")), jnp.stack(ring(half_b, "z")))
    )
    return ring(a, "z"), ring(b, "x")


def reduce_core_y(own, other, y, dtype):
    total = own + swap_core(other)
    pieces = [lax.dynamic_slice_in_dim(total, 4 * ((y + d) % 4), 4, 0) for d in range(4)]
    result = pieces[0]
    for d in (1, 3, 2):
        arrived = shifted(pieces[d].astype(dtype), "grp", 4 - d)
        result = result + arrived.astype(F32)
    return result


def on_device(
    coefficients,
    domain,
    coupling_owner,
    coupling_slot,
    coupling_fock,
    exchange_integrals,
    pno_energy,
    pair_shift,
    amplitudes_start,
):
    z, x, core, y = [lax.axis_index(name) for name in ("z", "x", "core", "grp")]
    class_z = (y + 2 * core) % 4
    flat = coefficients.reshape(PAIRS * PNO, PNO)
    local = (domain - y * NB).astype(BF16)
    start = lax.dynamic_slice_in_dim(amplitudes_start, 4 * y, 4, 0).astype(BF16)
    start = start.reshape(4 * PNO, PNO)
    flat_in, start_in, local_in = [to_class_plane(v) for v in (flat, start, local)]
    colours = []
    for k in range(4):
        rows = [
            flat_in[k * ORBITALS : (k + 1) * ORBITALS],
            start_in[k * PNO : (k + 1) * PNO],
        ]
        if k == 0:
            rows.append(local_in)
        colours.append(jnp.concatenate(rows)[None])

    table = jnp.stack(
        [(coupling_owner * PAIRS + coupling_slot).astype(F32), coupling_fock]
    ).reshape(2, -1)
    tables = jnp.stack([table, swap_core(table)])
    rest = jnp.concatenate([tables[1], jnp.zeros((PAIRS - 2, PNO), F32)]).astype(BF16)
    own_targets = jnp.concatenate([flat, local, flat_in[:PAIRS], start_in[:PAIRS], rest])
    targets = lax.all_gather(own_targets, ("core", "grp"))
    packed = pack_couplings(tables[:, 0].astype(jnp.int32), z, x, core, class_z)

    for step in range(3):
        got = [lax.ppermute(colours[k], *STEPS[k][step]) for k in range(4)]
        if step == 2:
            held_domains = joined(colours[0][:, COLOUR:], got[0][:, COLOUR:])
            got_domains = lax.ppermute(held_domains, *STEPS[0][3])
            last = joined(colours[3], got[3], extra=PAIRS)
            last = lax.dynamic_update_slice(last, got_domains, (0, COLOUR, 0))
        colours = [joined(colours[k], got[k]) for k in range(4)]
    colours[3] = last
    got = [lax.ppermute(colours[k], *STEPS[k][3]) for k in range(4)]
    lists = []
    for k in range(4):
        lists.append(colours[k].reshape(2, 2, 2, -1, PNO))
        lists.append(got[k].reshape(2, 2, 2, -1, PNO))

    lean = 1 - 2 * (z % 2)
    ranges = jnp.stack([z, z + lean, z - lean, z + 2]) % 4
    place = jnp.concatenate([4 * core + ranges, 4 * (1 - core) + ranges])
    info, fock, picked = pl.pallas_call(
        pick_kernel,
        out_shape=(
            jax.ShapeDtypeStruct((8, LINKS), jnp.int32),
            jax.ShapeDtypeStruct((1, LINKS + 1), F32),
            jax.ShapeDtypeStruct((LINKS, PNO, RANGES * PNO), BF16),
        ),
        in_specs=[SM, SM, SM, VM, VM, VM],
        out_specs=(SM, SM, VM),
        scratch_shapes=[
            pltpu.VMEM((2 * PAIRS, RANGES, PNO, NB), BF16),
            pltpu.VMEM((2 * RANGES, PAIRS, PNO), F32),
            pltpu.VMEM((2, 8, PAIRS, PNO), F32),
            pltpu.SMEM((LINKS + 1,), jnp.int32),
        ],
        compiler_params=params(22),
        name="pick_targets",
    )(place.astype(jnp.int32), packed, tables, targets, held_domains, got_domains)

    inter, own, other = pl.pallas_call(
        first_kernel,
        out_shape=(jax.ShapeDtypeStruct((LINKS, PNO, PNO), BF16), BLOCK, BLOCK),
        in_specs=[SM, SM] + [HB] * 8 + [VM],
        out_specs=(pl.BlockSpec(memory_space=pltpu.HBM), VM, VM),
        scratch_shapes=[
            pltpu.VMEM((LINKS, 2, 2, PNO, PNO), BF16),
            pltpu.VMEM((LINKS, PNO, PNO), BF16),
            pltpu.VMEM((2 * PAIRS, PNO, PNO), F32),
            pltpu.VMEM((LINKS, PNO, PNO), BF16),
            pltpu.SemaphoreType.DMA((LINKS,)),
            pltpu.SemaphoreType.DMA((LINKS,)),
            pltpu.SemaphoreType.DMA,
        ],
        compiler_params=params(19),
        name="intersect_and_project",
    )(info, fock, *lists, picked)

    energy = lax.dynamic_slice_in_dim(pno_energy, 4 * y, 4, 0)
    shift = lax.dynamic_slice_in_dim(pair_shift, 4 * y, 4, 0)
    exchange = lax.dynamic_slice_in_dim(exchange_integrals, 4 * y, 4, 0)
    denominator = energy[:, :, None] + energy[:, None, :] + shift[:, None, None]

    amplitudes = -(exchange + reduce_core_y(own, other, y, F32)) / denominator
    sent = to_class_plane(amplitudes.astype(BF16).reshape(4 * PNO, PNO))
    a_refs, b_refs = plane_gather(sent[: 2 * PNO], sent[2 * PNO :])
    own, other = pl.pallas_call(
        next_kernel,
        out_shape=(BLOCK, BLOCK),
        in_specs=[SM, SM] + [VM] * 9,
        out_specs=(VM, VM),
        scratch_shapes=[
            pltpu.VMEM((LINKS, PNO, PNO), BF16),
            pltpu.VMEM((2 * PAIRS, PNO, PNO), F32),
        ],
        compiler_params=params(12),
        name="project",
    )(info, fock, inter, *a_refs, *b_refs)
    amplitudes = -(exchange + reduce_core_y(own, other, y, BF16)) / denominator
    gathered = ring(amplitudes, "grp")
    result = jnp.zeros_like(exchange_integrals)
    for d in range(4):
        result = lax.dynamic_update_slice_in_dim(result, gathered[d], 4 * ((y + d) % 4), 0)
    return result


def solution(mesh):
    fine = Mesh(mesh.devices.reshape(4, 4, 2, 4), ("z", "x", "core", "grp"))
    placed = (
        P(SPLIT, "grp", None),
        P(SPLIT, "grp"),
        P(SPLIT, None),
        P(SPLIT, None),
        P(SPLIT, None),
        P(SPLIT, None, None),
        P(SPLIT, None),
        P(SPLIT),
        P(SPLIT, None, None),
    )
    return jax.shard_map(
        on_device, mesh=fine, in_specs=placed, out_specs=P(SPLIT, None, None), check_vma=False
    )
```

```python
import jax
import jax.numpy as jnp
from jax import lax
from jax.experimental import pallas as pl
from jax.experimental.pallas import tpu as pltpu
from jax.sharding import Mesh, PartitionSpec as P

NB = 192
RANGES = 4
PAIRS = 16
PNO = 128
LINKS = 40
UNROLL = 8
ORBITALS = 4 * PNO
COLOUR = ORBITALS + PNO
EVEN = [(0, 1), (1, 0), (2, 3), (3, 2)]
ODD = [(1, 2), (2, 1), (3, 0), (0, 3)]
STEPS = (
    (("x", EVEN), ("z", EVEN), ("x", ODD), ("z", ODD)),
    (("z", EVEN), ("x", EVEN), ("z", ODD), ("x", ODD)),
    (("x", ODD), ("z", ODD), ("x", EVEN), ("z", EVEN)),
    (("z", ODD), ("x", ODD), ("z", EVEN), ("x", EVEN)),
)
BF16 = jnp.bfloat16
F32 = jnp.float32
SPLIT = ("z", "x", "core")
TARGET, SLOT, REL_X, REL_Z, X_EVEN, X_ODD, AMP_LIST, AMP_AT = range(8)


def one_hot(row):
    functions = lax.broadcasted_iota(jnp.int32, (NB, PNO), 0).astype(F32)
    return jnp.where(functions == row, 1.0, 0.0).astype(BF16)


def ways(rel, here):
    lean = 1 + 2 * lax.rem(here, 2)
    even = (rel == 2) | (rel == lean)
    odd = (rel == 2) | (rel == 4 - lean)
    return even.astype(jnp.int32), odd.astype(jnp.int32)


FIELDS = (5, 4, 2, 2, 1, 1, 3, 3)


def pack_couplings(named, z, x, core, class_z):
    owner, slot = named // PAIRS, named % PAIRS
    mine = (owner % 2 == core) & (owner // 8 == class_z)
    rel_x, rel_z = ((owner // 2) % 4 - x) % 4, (slot // 4 - z) % 4
    x_even, x_odd = ways(rel_x, x)
    z_even, z_odd = ways(rel_z, z)
    colour = slot % 4
    x_first, even_first = colour % 2 == 0, colour < 2
    x_one, x_two = jnp.where(even_first, x_even, x_odd), jnp.where(even_first, x_odd, x_even)
    z_one, z_two = jnp.where(even_first, z_even, z_odd), jnp.where(even_first, z_odd, z_even)
    near = jnp.where(x_first, x_one + 2 * z_one, z_one + 2 * x_one)
    far, last = jnp.where(x_first, x_two, z_two), jnp.where(x_first, z_two, x_two)
    target = lax.broadcasted_iota(jnp.int32, named.shape, 0) * PAIRS
    target = target + lax.broadcasted_iota(jnp.int32, named.shape, 1) // 8
    values = (target, slot, rel_x, rel_z, x_even, x_odd, 2 * colour + last, near + 4 * far)
    code, place = 0, 1
    for bits, value in zip(FIELDS, values):
        code = code + value * place
        place *= 2**bits
    return jnp.where(mine, code, -1).astype(jnp.int32)


def list_couplings(packed, tables, info, fock, found):
    def clear(j, carry):
        found[j] = 0
        fock[0, j] = 0.0
        return carry

    lax.fori_loop(0, LINKS + 1, clear, 0)
    count = jnp.int32(0)
    for block in range(2):

        def look(step, count):
            for u in range(8):
                code = packed[block, step * 8 + u]
                fits = (code >= 0).astype(jnp.int32)
                spot = jnp.where(code >= 0, count, LINKS)
                found[spot] = code
                fock[0, spot] = tables[block, 1, step * 8 + u]
                count = count + fits
            return count

        count = lax.fori_loop(0, PAIRS, look, count)

    def unpack(j, carry):
        code = found[j]
        for row, bits in enumerate(FIELDS):
            info[row, j] = lax.rem(code, 2**bits)
            code = lax.div(code, 2**bits)
        return carry

    lax.fori_loop(0, LINKS, unpack, 0)


def pick_kernel(
    place, packed, tables, targets, held, got,
    info, fock, picked, expanded, dom, source_dom, found,
):
    list_couplings(packed, tables, info, fock, found)
    for i in range(2 * RANGES):
        dom[i] = targets[i, PAIRS * PNO : PAIRS * PNO + PAIRS, :].astype(F32)
    for i in range(8):
        source_dom[0, i] = held[i].astype(F32)
        source_dom[1, i] = got[i].astype(F32)

    def expand(i, carry):
        for block in range(2):
            for r in range(RANGES):
                d = place[4 * block + r]
                hot = one_hot(dom[d, pl.ds(i, 1), :])
                rows = targets[d, pl.ds(pl.multiple_of(i * PNO, PNO), PNO), :]
                full = jnp.dot(hot, rows, preferred_element_type=F32)
                expanded[block * PAIRS + i, r] = full.T.astype(BF16)
        return carry

    lax.fori_loop(0, PAIRS, expand, 0)

    def pick(step, carry):
        for u in range(4):
            j = step * 4 + u
            for r in range(RANGES):
                at = 4 * info[X_ODD, j] + 2 * (r % 2) + info[X_EVEN, j]
                row = source_dom[r // 2, at, pl.ds(info[SLOT, j], 1), :]
                part = jnp.dot(
                    expanded[info[TARGET, j], r], one_hot(row), preferred_element_type=F32
                )
                picked[j, :, r * PNO : (r + 1) * PNO] = part.astype(BF16)
        return carry

    lax.fori_loop(0, LINKS // 4, pick, 0)


def choose(which, low, high, act):
    if high - low == 1:
        act(low)
        return
    middle = (low + high) // 2

    @pl.when(which < middle)
    def _():
        choose(which, low, middle, act)

    @pl.when(which >= middle)
    def _():
        choose(which, middle, high, act)


def fetch_amplitudes(info, j, a_refs, b_refs, amp):
    rx, slot, rz = info[REL_X, j], info[SLOT, j], info[REL_Z, j]
    rows = pl.ds(pl.multiple_of(lax.rem(slot, 2) * PNO, PNO), PNO)

    def from_a(r):
        amp[j] = a_refs[r][rx, rows, :]

    def from_b(r):
        amp[j] = b_refs[r][rz, rows, :]

    @pl.when(lax.rem(slot, 4) < 2)
    def _():
        choose(rz, 0, 4, from_a)

    @pl.when(lax.rem(slot, 4) >= 2)
    def _():
        choose(rx, 0, 4, from_b)


def project_all(info, fock, inter, amp, acc):
    def body(step, carry):
        for u in range(UNROLL):
            j = step * UNROLL + u
            block, target = inter[j], info[TARGET, j]
            half = jnp.dot(block, amp[j], preferred_element_type=F32).astype(BF16)
            whole = lax.dot_general(
                half, block, (((1,), (1,)), ((), ())), preferred_element_type=F32
            )
            acc[target] = acc[target] + fock[0, j] * whole
        return carry

    lax.fori_loop(0, LINKS // UNROLL, body, 0)


def first_kernel(info, fock, *refs):
    lists, picked = refs[0:8], refs[8]
    inter_out, own, other = refs[9:12]
    source, amp, acc, inter, sem, amp_sem, out_sem = refs[12:]

    def fetch(j, carry):
        slot, even, odd = info[SLOT, j], info[X_EVEN, j], info[X_ODD, j]
        rows = pl.ds(pl.multiple_of(lax.rem(slot, 4) * PNO, PNO), PNO)

        def copy(src, dst):
            pltpu.make_async_copy(src, dst, sem.at[j]).start()

        def from_colour(colour):
            if colour == 0:
                for bit in range(2):
                    copy(lists[bit].at[odd, :, even, rows], source.at[j, bit])
            elif colour == 1:
                choose(odd, 0, 2, lambda last: copy(
                    lists[2 + last].at[:, even, :, rows], source.at[j]
                ))
            elif colour == 2:
                for bit in range(2):
                    copy(lists[4 + bit].at[even, :, odd, rows], source.at[j, :, bit])
            else:
                choose(even, 0, 2, lambda last: [
                    copy(lists[6 + last].at[bit, odd, :, rows], source.at[j, :, bit])
                    for bit in range(2)
                ])

        choose(lax.div(slot, 4), 0, 4, from_colour)
        at = info[AMP_AT, j]
        far, middle, near = lax.div(at, 4), lax.rem(lax.div(at, 2), 2), lax.rem(at, 2)
        choose(info[AMP_LIST, j], 0, 8, lambda i: pltpu.make_async_copy(
            lists[i].at[far, middle, near, pl.ds(ORBITALS, PNO)], amp.at[j], amp_sem.at[j]
        ).start())
        return carry

    lax.fori_loop(0, LINKS, fetch, 0)
    acc[...] = jnp.zeros_like(acc)

    def intersect(step, carry):
        for u in range(UNROLL):
            j = step * UNROLL + u
            pltpu.make_async_copy(source.at[j], source.at[j], sem.at[j]).wait()
            pltpu.make_async_copy(amp.at[j], amp.at[j], amp_sem.at[j]).wait()
        for u in range(UNROLL):
            j = step * UNROLL + u
            rows = source[j].reshape(RANGES * PNO, PNO)
            block = jnp.dot(picked[j], rows, preferred_element_type=F32)
            inter[j] = block.astype(BF16)
        return carry

    lax.fori_loop(0, LINKS // UNROLL, intersect, 0)
    out = pltpu.make_async_copy(inter, inter_out, out_sem)
    out.start()
    project_all(info, fock, inter, amp, acc)
    out.wait()
    own[...] = acc[0:PAIRS]
    other[...] = acc[PAIRS:].astype(other.dtype)


def next_kernel(info, fock, inter, *refs):
    a_refs, b_refs = refs[0:4], refs[4:8]
    own, other = refs[8:10]
    amp, acc = refs[10:]

    def fetch(j, carry):
        fetch_amplitudes(info, j, a_refs, b_refs, amp)
        return carry

    lax.fori_loop(0, LINKS, fetch, 0)
    acc[...] = jnp.zeros_like(acc)

    project_all(info, fock, inter, amp, acc)
    own[...] = acc[0:PAIRS]
    other[...] = acc[PAIRS:].astype(other.dtype)


VM = pl.BlockSpec(memory_space=pltpu.VMEM)
SM = pl.BlockSpec(memory_space=pltpu.SMEM)
HB = pl.BlockSpec(memory_space=pl.ANY)


def params(mib):
    return pltpu.CompilerParams(vmem_limit_bytes=mib * 1024 * 1024)


BLOCK = jax.ShapeDtypeStruct((PAIRS, PNO, PNO), F32)


def shifted(value, axis, rel):
    return lax.ppermute(value, axis, [((i + rel) % 4, i) for i in range(4)])


def ring(value, axis):
    plus, minus = shifted(value, axis, 1), shifted(value, axis, 3)
    return [value, plus, shifted(value, axis, 2), minus]


def swap_core(value):
    return lax.ppermute(value, "core", [(0, 1), (1, 0)])


def to_class_plane(value):
    moves = []
    for z in range(4):
        for core in range(2):
            for y in range(4):
                moves.append(
                    ((z * 2 + core) * 4 + y, (y * 2 + core) * 4 + (z + 2 * core) % 4)
                )
    return lax.ppermute(value, ("z", "core", "grp"), moves)


def joined(held, got, extra=0):
    count, rows, columns = held.shape
    both = jnp.zeros((2 * count, rows + extra, columns), held.dtype)
    both = lax.optimization_barrier(lax.dynamic_update_slice(both, held, (0, 0, 0)))
    return lax.dynamic_update_slice(both, got, (count, 0, 0))


def plane_gather(half_a, half_b):
    a, b = lax.optimization_barrier(
        (jnp.stack(ring(half_a, "x")), jnp.stack(ring(half_b, "z")))
    )
    return ring(a, "z"), ring(b, "x")


def reduce_core_y(own, other, y, dtype):
    total = own + swap_core(other)
    pieces = [lax.dynamic_slice_in_dim(total, 4 * ((y + d) % 4), 4, 0) for d in range(4)]
    result = pieces[0]
    for d in (1, 3, 2):
        arrived = shifted(pieces[d].astype(dtype), "grp", 4 - d)
        result = result + arrived.astype(F32)
    return result


def on_device(
    coefficients,
    domain,
    coupling_owner,
    coupling_slot,
    coupling_fock,
    exchange_integrals,
    pno_energy,
    pair_shift,
    amplitudes_start,
):
    z, x, core, y = [lax.axis_index(name) for name in ("z", "x", "core", "grp")]
    class_z = (y + 2 * core) % 4
    flat = coefficients.reshape(PAIRS * PNO, PNO)
    local = (domain - y * NB).astype(BF16)
    start = lax.dynamic_slice_in_dim(amplitudes_start, 4 * y, 4, 0).astype(BF16)
    start = start.reshape(4 * PNO, PNO)
    flat_in = to_class_plane(flat)
    start_in = to_class_plane(jnp.concatenate([start, local]))
    local_in = start_in[4 * PNO :]
    colours = []
    for k in range(4):
        rows = [
            flat_in[k * ORBITALS : (k + 1) * ORBITALS],
            start_in[k * PNO : (k + 1) * PNO],
        ]
        if k == 0:
            rows.append(local_in)
        colours.append(jnp.concatenate(rows)[None])

    table = jnp.stack(
        [(coupling_owner * PAIRS + coupling_slot).astype(F32), coupling_fock]
    ).reshape(2, -1)
    tables = jnp.stack([table, swap_core(table)])
    rest = jnp.concatenate([tables[1], jnp.zeros((PAIRS - 2, PNO), F32)]).astype(BF16)
    own_targets = jnp.concatenate([flat, local, flat_in[:PAIRS], start_in[:PAIRS], rest])
    targets = lax.all_gather(own_targets, ("core", "grp"))
    packed = pack_couplings(tables[:, 0].astype(jnp.int32), z, x, core, class_z)

    for step in range(3):
        got = [lax.ppermute(colours[k], *STEPS[k][step]) for k in range(4)]
        if step == 2:
            held_domains = joined(colours[0][:, COLOUR:], got[0][:, COLOUR:])
            got_domains = lax.ppermute(held_domains, *STEPS[0][3])
            last = joined(colours[3], got[3], extra=PAIRS)
            last = lax.dynamic_update_slice(last, got_domains, (0, COLOUR, 0))
        colours = [joined(colours[k], got[k]) for k in range(4)]
    colours[3] = last
    got = [lax.ppermute(colours[k], *STEPS[k][3]) for k in range(4)]
    lists = []
    for k in range(4):
        lists.append(colours[k].reshape(2, 2, 2, -1, PNO))
        lists.append(got[k].reshape(2, 2, 2, -1, PNO))

    lean = 1 - 2 * (z % 2)
    ranges = jnp.stack([z, z + lean, z - lean, z + 2]) % 4
    place = jnp.concatenate([4 * core + ranges, 4 * (1 - core) + ranges])
    info, fock, picked = pl.pallas_call(
        pick_kernel,
        out_shape=(
            jax.ShapeDtypeStruct((8, LINKS), jnp.int32),
            jax.ShapeDtypeStruct((1, LINKS + 1), F32),
            jax.ShapeDtypeStruct((LINKS, PNO, RANGES * PNO), BF16),
        ),
        in_specs=[SM, SM, SM, VM, VM, VM],
        out_specs=(SM, SM, VM),
        scratch_shapes=[
            pltpu.VMEM((2 * PAIRS, RANGES, PNO, NB), BF16),
            pltpu.VMEM((2 * RANGES, PAIRS, PNO), F32),
            pltpu.VMEM((2, 8, PAIRS, PNO), F32),
            pltpu.SMEM((LINKS + 1,), jnp.int32),
        ],
        compiler_params=params(22),
        name="pick_targets",
    )(place.astype(jnp.int32), packed, tables, targets, held_domains, got_domains)

    inter, own, other = pl.pallas_call(
        first_kernel,
        out_shape=(jax.ShapeDtypeStruct((LINKS, PNO, PNO), BF16), BLOCK, BLOCK),
        in_specs=[SM, SM] + [HB] * 8 + [VM],
        out_specs=(pl.BlockSpec(memory_space=pltpu.HBM), VM, VM),
        scratch_shapes=[
            pltpu.VMEM((LINKS, 2, 2, PNO, PNO), BF16),
            pltpu.VMEM((LINKS, PNO, PNO), BF16),
            pltpu.VMEM((2 * PAIRS, PNO, PNO), F32),
            pltpu.VMEM((LINKS, PNO, PNO), BF16),
            pltpu.SemaphoreType.DMA((LINKS,)),
            pltpu.SemaphoreType.DMA((LINKS,)),
            pltpu.SemaphoreType.DMA,
        ],
        compiler_params=params(19),
        name="intersect_and_project",
    )(info, fock, *lists, picked)

    energy = lax.dynamic_slice_in_dim(pno_energy, 4 * y, 4, 0)
    shift = lax.dynamic_slice_in_dim(pair_shift, 4 * y, 4, 0)
    exchange = lax.dynamic_slice_in_dim(exchange_integrals, 4 * y, 4, 0)
    denominator = energy[:, :, None] + energy[:, None, :] + shift[:, None, None]

    amplitudes = -(exchange + reduce_core_y(own, other, y, F32)) / denominator
    sent = to_class_plane(amplitudes.astype(BF16).reshape(4 * PNO, PNO))
    a_refs, b_refs = plane_gather(sent[: 2 * PNO], sent[2 * PNO :])
    own, other = pl.pallas_call(
        next_kernel,
        out_shape=(BLOCK, BLOCK),
        in_specs=[SM, SM] + [VM] * 9,
        out_specs=(VM, VM),
        scratch_shapes=[
            pltpu.VMEM((LINKS, PNO, PNO), BF16),
            pltpu.VMEM((2 * PAIRS, PNO, PNO), F32),
        ],
        compiler_params=params(12),
        name="project",
    )(info, fock, inter, *a_refs, *b_refs)
    amplitudes = -(exchange + reduce_core_y(own, other, y, BF16)) / denominator
    amplitudes = lax.reduce_precision(amplitudes, exponent_bits=8, mantissa_bits=7)
    gathered = ring(amplitudes.astype(BF16), "grp")
    result = jnp.zeros_like(exchange_integrals)
    for d in range(4):
        piece = gathered[d].astype(F32)
        result = lax.dynamic_update_slice_in_dim(result, piece, 4 * ((y + d) % 4), 0)
    return result


def solution(mesh):
    fine = Mesh(mesh.devices.reshape(4, 4, 2, 4), ("z", "x", "core", "grp"))
    placed = (
        P(SPLIT, "grp", None),
        P(SPLIT, "grp"),
        P(SPLIT, None),
        P(SPLIT, None),
        P(SPLIT, None),
        P(SPLIT, None, None),
        P(SPLIT, None),
        P(SPLIT),
        P(SPLIT, None, None),
    )
    return jax.shard_map(
        on_device, mesh=fine, in_specs=placed, out_specs=P(SPLIT, None, None), check_vma=False
    )
```

```python
import jax
import jax.numpy as jnp
from jax import lax
from jax.experimental import pallas as pl
from jax.experimental.pallas import tpu as pltpu
from jax.sharding import Mesh, PartitionSpec as P

NB = 192
RANGES = 4
PAIRS = 16
PNO = 128
LINKS = 40
UNROLL = 8
ORBITALS = 4 * PNO
COLOUR = ORBITALS + PNO
EVEN = [(0, 1), (1, 0), (2, 3), (3, 2)]
ODD = [(1, 2), (2, 1), (3, 0), (0, 3)]
STEPS = (
    (("x", EVEN), ("z", EVEN), ("x", ODD), ("z", ODD)),
    (("z", EVEN), ("x", EVEN), ("z", ODD), ("x", ODD)),
    (("x", ODD), ("z", ODD), ("x", EVEN), ("z", EVEN)),
    (("z", ODD), ("x", ODD), ("z", EVEN), ("x", EVEN)),
)
BF16 = jnp.bfloat16
F32 = jnp.float32
SPLIT = ("z", "x", "core")
TARGET, SLOT, REL_X, REL_Z, X_EVEN, X_ODD, AMP_LIST, AMP_AT = range(8)


def one_hot(row):
    functions = lax.broadcasted_iota(jnp.int32, (NB, PNO), 0).astype(F32)
    return jnp.where(functions == row, 1.0, 0.0).astype(BF16)


def ways(rel, here):
    lean = 1 + 2 * lax.rem(here, 2)
    even = (rel == 2) | (rel == lean)
    odd = (rel == 2) | (rel == 4 - lean)
    return even.astype(jnp.int32), odd.astype(jnp.int32)


FIELDS = (5, 4, 2, 2, 1, 1, 3, 3)


def pack_couplings(named, z, x, core, class_z):
    owner, slot = named // PAIRS, named % PAIRS
    mine = (owner % 2 == core) & (owner // 8 == class_z)
    rel_x, rel_z = ((owner // 2) % 4 - x) % 4, (slot // 4 - z) % 4
    x_even, x_odd = ways(rel_x, x)
    z_even, z_odd = ways(rel_z, z)
    colour = slot % 4
    x_first, even_first = colour % 2 == 0, colour < 2
    x_one, x_two = jnp.where(even_first, x_even, x_odd), jnp.where(even_first, x_odd, x_even)
    z_one, z_two = jnp.where(even_first, z_even, z_odd), jnp.where(even_first, z_odd, z_even)
    near = jnp.where(x_first, x_one + 2 * z_one, z_one + 2 * x_one)
    far, last = jnp.where(x_first, x_two, z_two), jnp.where(x_first, z_two, x_two)
    target = lax.broadcasted_iota(jnp.int32, named.shape, 0) * PAIRS
    target = target + lax.broadcasted_iota(jnp.int32, named.shape, 1) // 8
    values = (target, slot, rel_x, rel_z, x_even, x_odd, 2 * colour + last, near + 4 * far)
    code, place = 0, 1
    for bits, value in zip(FIELDS, values):
        code = code + value * place
        place *= 2**bits
    return jnp.where(mine, code, -1).astype(jnp.int32)


def list_couplings(packed, tables, info, fock, found):
    def clear(j, carry):
        found[j] = 0
        fock[0, j] = 0.0
        return carry

    lax.fori_loop(0, LINKS + 1, clear, 0)
    count = jnp.int32(0)
    for block in range(2):

        def look(step, count):
            for u in range(8):
                code = packed[block, step * 8 + u]
                fits = (code >= 0).astype(jnp.int32)
                spot = jnp.where(code >= 0, count, LINKS)
                found[spot] = code
                fock[0, spot] = tables[block, 1, step * 8 + u]
                count = count + fits
            return count

        count = lax.fori_loop(0, PAIRS, look, count)

    def unpack(j, carry):
        code = found[j]
        for row, bits in enumerate(FIELDS):
            info[row, j] = lax.rem(code, 2**bits)
            code = lax.div(code, 2**bits)
        return carry

    lax.fori_loop(0, LINKS, unpack, 0)


def pick_kernel(
    place, packed, tables, held, got, *refs
):
    targets = refs[: 2 * RANGES]
    info, fock, picked, expanded, dom, source_dom, found = refs[2 * RANGES :]
    list_couplings(packed, tables, info, fock, found)
    for i in range(2 * RANGES):
        dom[i] = targets[i][PAIRS * PNO : PAIRS * PNO + PAIRS, :].astype(F32)
    for i in range(8):
        source_dom[0, i] = held[i].astype(F32)
        source_dom[1, i] = got[i].astype(F32)

    def expand(i, carry):
        for block in range(2):
            for d in range(RANGES):
                rows = targets[RANGES * block + d]
                hot = one_hot(dom[RANGES * block + d, pl.ds(i, 1), :])
                rows = rows[pl.ds(pl.multiple_of(i * PNO, PNO), PNO), :]
                full = jnp.dot(hot, rows, preferred_element_type=F32)
                expanded[block * PAIRS + i, place[d]] = full.T.astype(BF16)
        return carry

    lax.fori_loop(0, PAIRS, expand, 0)

    def pick(step, carry):
        for u in range(4):
            j = step * 4 + u
            for r in range(RANGES):
                at = 4 * info[X_ODD, j] + 2 * (r % 2) + info[X_EVEN, j]
                row = source_dom[r // 2, at, pl.ds(info[SLOT, j], 1), :]
                part = jnp.dot(
                    expanded[info[TARGET, j], r], one_hot(row), preferred_element_type=F32
                )
                picked[j, :, r * PNO : (r + 1) * PNO] = part.astype(BF16)
        return carry

    lax.fori_loop(0, LINKS // 4, pick, 0)


def choose(which, low, high, act):
    if high - low == 1:
        act(low)
        return
    middle = (low + high) // 2

    @pl.when(which < middle)
    def _():
        choose(which, low, middle, act)

    @pl.when(which >= middle)
    def _():
        choose(which, middle, high, act)


def fetch_amplitudes(info, j, a_refs, b_refs, amp):
    rx, slot, rz = info[REL_X, j], info[SLOT, j], info[REL_Z, j]
    rows = pl.ds(pl.multiple_of(lax.rem(slot, 2) * PNO, PNO), PNO)

    def from_a(r):
        amp[j] = a_refs[r][rx, rows, :]

    def from_b(r):
        amp[j] = b_refs[r][rz, rows, :]

    @pl.when(lax.rem(slot, 4) < 2)
    def _():
        choose(rz, 0, 4, from_a)

    @pl.when(lax.rem(slot, 4) >= 2)
    def _():
        choose(rx, 0, 4, from_b)


def project_all(info, fock, inter, amp, acc):
    def body(step, carry):
        for u in range(UNROLL):
            j = step * UNROLL + u
            block, target = inter[j], info[TARGET, j]
            half = jnp.dot(block, amp[j], preferred_element_type=F32).astype(BF16)
            whole = lax.dot_general(
                half, block, (((1,), (1,)), ((), ())), preferred_element_type=F32
            )
            acc[target] = acc[target] + fock[0, j] * whole
        return carry

    lax.fori_loop(0, LINKS // UNROLL, body, 0)


def first_kernel(info, fock, *refs):
    lists, picked = refs[0:8], refs[8]
    inter_out, own, other = refs[9:12]
    source, amp, acc, inter, sem, amp_sem, out_sem = refs[12:]

    def fetch(j, carry):
        slot, even, odd = info[SLOT, j], info[X_EVEN, j], info[X_ODD, j]
        rows = pl.ds(pl.multiple_of(lax.rem(slot, 4) * PNO, PNO), PNO)

        def copy(src, dst):
            pltpu.make_async_copy(src, dst, sem.at[j]).start()

        def from_colour(colour):
            if colour == 0:
                for bit in range(2):
                    copy(lists[bit].at[odd, :, even, rows], source.at[j, bit])
            elif colour == 1:
                choose(odd, 0, 2, lambda last: copy(
                    lists[2 + last].at[:, even, :, rows], source.at[j]
                ))
            elif colour == 2:
                for bit in range(2):
                    copy(lists[4 + bit].at[even, :, odd, rows], source.at[j, :, bit])
            else:
                choose(even, 0, 2, lambda last: [
                    copy(lists[6 + last].at[bit, odd, :, rows], source.at[j, :, bit])
                    for bit in range(2)
                ])

        choose(lax.div(slot, 4), 0, 4, from_colour)
        at = info[AMP_AT, j]
        far, middle, near = lax.div(at, 4), lax.rem(lax.div(at, 2), 2), lax.rem(at, 2)
        choose(info[AMP_LIST, j], 0, 8, lambda i: pltpu.make_async_copy(
            lists[i].at[far, middle, near, pl.ds(ORBITALS, PNO)], amp.at[j], amp_sem.at[j]
        ).start())
        return carry

    lax.fori_loop(0, LINKS, fetch, 0)
    acc[...] = jnp.zeros_like(acc)

    def intersect(step, carry):
        for u in range(UNROLL):
            j = step * UNROLL + u
            pltpu.make_async_copy(source.at[j], source.at[j], sem.at[j]).wait()
            pltpu.make_async_copy(amp.at[j], amp.at[j], amp_sem.at[j]).wait()
        for u in range(UNROLL):
            j = step * UNROLL + u
            rows = source[j].reshape(RANGES * PNO, PNO)
            block = jnp.dot(picked[j], rows, preferred_element_type=F32)
            inter[j] = block.astype(BF16)
        return carry

    lax.fori_loop(0, LINKS // UNROLL, intersect, 0)
    out = pltpu.make_async_copy(inter, inter_out, out_sem)
    out.start()
    project_all(info, fock, inter, amp, acc)
    out.wait()
    own[...] = acc[0:PAIRS]
    other[...] = acc[PAIRS:].astype(other.dtype)


def next_kernel(info, fock, inter, *refs):
    a_refs, b_refs = refs[0:4], refs[4:8]
    own, other = refs[8:10]
    amp, acc = refs[10:]

    def fetch(j, carry):
        fetch_amplitudes(info, j, a_refs, b_refs, amp)
        return carry

    lax.fori_loop(0, LINKS, fetch, 0)
    acc[...] = jnp.zeros_like(acc)

    project_all(info, fock, inter, amp, acc)
    own[...] = acc[0:PAIRS]
    other[...] = acc[PAIRS:].astype(other.dtype)


VM = pl.BlockSpec(memory_space=pltpu.VMEM)
SM = pl.BlockSpec(memory_space=pltpu.SMEM)
HB = pl.BlockSpec(memory_space=pl.ANY)


def params(mib):
    return pltpu.CompilerParams(vmem_limit_bytes=mib * 1024 * 1024)


BLOCK = jax.ShapeDtypeStruct((PAIRS, PNO, PNO), F32)


def shifted(value, axis, rel):
    return lax.ppermute(value, axis, [((i + rel) % 4, i) for i in range(4)])


def ring(value, axis):
    plus, minus = shifted(value, axis, 1), shifted(value, axis, 3)
    return [value, plus, shifted(value, axis, 2), minus]


def swap_core(value):
    return lax.ppermute(value, "core", [(0, 1), (1, 0)])


def to_class_plane(value):
    moves = []
    for z in range(4):
        for core in range(2):
            for y in range(4):
                moves.append(
                    ((z * 2 + core) * 4 + y, (y * 2 + core) * 4 + (z + 2 * core) % 4)
                )
    return lax.ppermute(value, ("z", "core", "grp"), moves)


def joined(held, got, extra=0):
    count, rows, columns = held.shape
    both = jnp.zeros((2 * count, rows + extra, columns), held.dtype)
    both = lax.optimization_barrier(lax.dynamic_update_slice(both, held, (0, 0, 0)))
    return lax.dynamic_update_slice(both, got, (count, 0, 0))


def plane_gather(half_a, half_b):
    a, b = lax.optimization_barrier(
        (jnp.stack(ring(half_a, "x")), jnp.stack(ring(half_b, "z")))
    )
    return ring(a, "z"), ring(b, "x")


def reduce_core_y(own, other, y, dtype):
    total = own + swap_core(other)
    pieces = [lax.dynamic_slice_in_dim(total, 4 * ((y + d) % 4), 4, 0) for d in range(4)]
    result = pieces[0]
    for d in (1, 3, 2):
        arrived = shifted(pieces[d].astype(dtype), "grp", 4 - d)
        result = result + arrived.astype(F32)
    return result


def on_device(
    coefficients,
    domain,
    coupling_owner,
    coupling_slot,
    coupling_fock,
    exchange_integrals,
    pno_energy,
    pair_shift,
    amplitudes_start,
):
    z, x, core, y = [lax.axis_index(name) for name in ("z", "x", "core", "grp")]
    class_z = (y + 2 * core) % 4
    flat = coefficients.reshape(PAIRS * PNO, PNO)
    local = (domain - y * NB).astype(BF16)
    start = lax.dynamic_slice_in_dim(amplitudes_start, 4 * y, 4, 0).astype(BF16)
    start = start.reshape(4 * PNO, PNO)
    flat_in = to_class_plane(flat)
    start_in = to_class_plane(jnp.concatenate([start, local]))
    local_in = start_in[4 * PNO :]
    colours = []
    for k in range(4):
        rows = [
            flat_in[k * ORBITALS : (k + 1) * ORBITALS],
            start_in[k * PNO : (k + 1) * PNO],
        ]
        if k == 0:
            rows.append(local_in)
        colours.append(jnp.concatenate(rows)[None])

    table = jnp.stack(
        [(coupling_owner * PAIRS + coupling_slot).astype(F32), coupling_fock]
    ).reshape(2, -1)
    tables = jnp.stack([table, swap_core(table)])
    rest = jnp.concatenate([tables[1], jnp.zeros((PAIRS - 2, PNO), F32)]).astype(BF16)
    own_targets = jnp.concatenate([flat, local, flat_in[:PAIRS], start_in[:PAIRS], rest])
    targets = [own_targets]
    for d in range(3):
        targets.append(shifted(targets[-1], "grp", 1))
    targets += [swap_core(rows) for rows in targets]
    packed = pack_couplings(tables[:, 0].astype(jnp.int32), z, x, core, class_z)

    for step in range(3):
        got = [lax.ppermute(colours[k], *STEPS[k][step]) for k in range(4)]
        if step == 2:
            held_domains = joined(colours[0][:, COLOUR:], got[0][:, COLOUR:])
            got_domains = lax.ppermute(held_domains, *STEPS[0][3])
            last = joined(colours[3], got[3], extra=PAIRS)
            last = lax.dynamic_update_slice(last, got_domains, (0, COLOUR, 0))
        colours = [joined(colours[k], got[k]) for k in range(4)]
    colours[3] = last
    got = [lax.ppermute(colours[k], *STEPS[k][3]) for k in range(4)]
    lists = []
    for k in range(4):
        lists.append(colours[k].reshape(2, 2, 2, -1, PNO))
        lists.append(got[k].reshape(2, 2, 2, -1, PNO))

    even, odd = ways((y + jnp.arange(RANGES, dtype=jnp.int32) - z) % 4, z)
    place = even + 2 * odd
    info, fock, picked = pl.pallas_call(
        pick_kernel,
        out_shape=(
            jax.ShapeDtypeStruct((8, LINKS), jnp.int32),
            jax.ShapeDtypeStruct((1, LINKS + 1), F32),
            jax.ShapeDtypeStruct((LINKS, PNO, RANGES * PNO), BF16),
        ),
        in_specs=[SM, SM, SM] + [VM] * 10,
        out_specs=(SM, SM, VM),
        scratch_shapes=[
            pltpu.VMEM((2 * PAIRS, RANGES, PNO, NB), BF16),
            pltpu.VMEM((2 * RANGES, PAIRS, PNO), F32),
            pltpu.VMEM((2, 8, PAIRS, PNO), F32),
            pltpu.SMEM((LINKS + 1,), jnp.int32),
        ],
        compiler_params=params(22),
        name="pick_targets",
    )(place.astype(jnp.int32), packed, tables, held_domains, got_domains, *targets)

    inter, own, other = pl.pallas_call(
        first_kernel,
        out_shape=(jax.ShapeDtypeStruct((LINKS, PNO, PNO), BF16), BLOCK, BLOCK),
        in_specs=[SM, SM] + [HB] * 8 + [VM],
        out_specs=(pl.BlockSpec(memory_space=pltpu.HBM), VM, VM),
        scratch_shapes=[
            pltpu.VMEM((LINKS, 2, 2, PNO, PNO), BF16),
            pltpu.VMEM((LINKS, PNO, PNO), BF16),
            pltpu.VMEM((2 * PAIRS, PNO, PNO), F32),
            pltpu.VMEM((LINKS, PNO, PNO), BF16),
            pltpu.SemaphoreType.DMA((LINKS,)),
            pltpu.SemaphoreType.DMA((LINKS,)),
            pltpu.SemaphoreType.DMA,
        ],
        compiler_params=params(19),
        name="intersect_and_project",
    )(info, fock, *lists, picked)

    energy = lax.dynamic_slice_in_dim(pno_energy, 4 * y, 4, 0)
    shift = lax.dynamic_slice_in_dim(pair_shift, 4 * y, 4, 0)
    exchange = lax.dynamic_slice_in_dim(exchange_integrals, 4 * y, 4, 0)
    denominator = energy[:, :, None] + energy[:, None, :] + shift[:, None, None]

    amplitudes = -(exchange + reduce_core_y(own, other, y, F32)) / denominator
    sent = to_class_plane(amplitudes.astype(BF16).reshape(4 * PNO, PNO))
    a_refs, b_refs = plane_gather(sent[: 2 * PNO], sent[2 * PNO :])
    own, other = pl.pallas_call(
        next_kernel,
        out_shape=(BLOCK, BLOCK),
        in_specs=[SM, SM] + [VM] * 9,
        out_specs=(VM, VM),
        scratch_shapes=[
            pltpu.VMEM((LINKS, PNO, PNO), BF16),
            pltpu.VMEM((2 * PAIRS, PNO, PNO), F32),
        ],
        compiler_params=params(12),
        name="project",
    )(info, fock, inter, *a_refs, *b_refs)
    amplitudes = -(exchange + reduce_core_y(own, other, y, BF16)) / denominator
    amplitudes = lax.reduce_precision(amplitudes, exponent_bits=8, mantissa_bits=7)
    gathered = ring(amplitudes.astype(BF16), "grp")
    result = jnp.zeros_like(exchange_integrals)
    for d in range(4):
        piece = gathered[d].astype(F32)
        result = lax.dynamic_update_slice_in_dim(result, piece, 4 * ((y + d) % 4), 0)
    return result


def solution(mesh):
    fine = Mesh(mesh.devices.reshape(4, 4, 2, 4), ("z", "x", "core", "grp"))
    placed = (
        P(SPLIT, "grp", None),
        P(SPLIT, "grp"),
        P(SPLIT, None),
        P(SPLIT, None),
        P(SPLIT, None),
        P(SPLIT, None, None),
        P(SPLIT, None),
        P(SPLIT),
        P(SPLIT, None, None),
    )
    return jax.shard_map(
        on_device, mesh=fine, in_specs=placed, out_specs=P(SPLIT, None, None), check_vma=False
    )
```

```python
import jax
import jax.numpy as jnp
from jax import lax
from jax.experimental import pallas as pl
from jax.experimental.pallas import tpu as pltpu
from jax.sharding import Mesh, PartitionSpec as P

NB = 192
RANGES = 4
PAIRS = 16
PNO = 128
LINKS = 40
UNROLL = 8
ORBITALS = 4 * PNO
COLOUR = ORBITALS + PNO
EVEN = [(0, 1), (1, 0), (2, 3), (3, 2)]
ODD = [(1, 2), (2, 1), (3, 0), (0, 3)]
STEPS = (
    (("x", EVEN), ("z", EVEN), ("x", ODD), ("z", ODD)),
    (("z", EVEN), ("x", EVEN), ("z", ODD), ("x", ODD)),
    (("x", ODD), ("z", ODD), ("x", EVEN), ("z", EVEN)),
    (("z", ODD), ("x", ODD), ("z", EVEN), ("x", EVEN)),
)
BF16 = jnp.bfloat16
F32 = jnp.float32
SPLIT = ("z", "x", "core")
TARGET, SLOT, REL_X, REL_Z, X_EVEN, X_ODD, AMP_LIST, AMP_AT = range(8)


def one_hot(row):
    functions = lax.broadcasted_iota(jnp.int32, (NB, PNO), 0).astype(F32)
    return jnp.where(functions == row, 1.0, 0.0).astype(BF16)


def ways(rel, here):
    lean = 1 + 2 * lax.rem(here, 2)
    even = (rel == 2) | (rel == lean)
    odd = (rel == 2) | (rel == 4 - lean)
    return even.astype(jnp.int32), odd.astype(jnp.int32)


FIELDS = (5, 4, 2, 2, 1, 1, 3, 3)


def pack_couplings(named, z, x, core, class_z):
    owner, slot = named // PAIRS, named % PAIRS
    mine = (owner % 2 == core) & (owner // 8 == class_z)
    rel_x, rel_z = ((owner // 2) % 4 - x) % 4, (slot // 4 - z) % 4
    x_even, x_odd = ways(rel_x, x)
    z_even, z_odd = ways(rel_z, z)
    colour = slot % 4
    x_first, even_first = colour % 2 == 0, colour < 2
    x_one, x_two = jnp.where(even_first, x_even, x_odd), jnp.where(even_first, x_odd, x_even)
    z_one, z_two = jnp.where(even_first, z_even, z_odd), jnp.where(even_first, z_odd, z_even)
    near = jnp.where(x_first, x_one + 2 * z_one, z_one + 2 * x_one)
    far, last = jnp.where(x_first, x_two, z_two), jnp.where(x_first, z_two, x_two)
    target = lax.broadcasted_iota(jnp.int32, named.shape, 0) * PAIRS
    target = target + lax.broadcasted_iota(jnp.int32, named.shape, 1) // 8
    values = (target, slot, rel_x, rel_z, x_even, x_odd, 2 * colour + last, near + 4 * far)
    code, place = 0, 1
    for bits, value in zip(FIELDS, values):
        code = code + value * place
        place *= 2**bits
    return jnp.where(mine, code, -1).astype(jnp.int32)


def list_couplings(packed, tables, info, fock, found):
    def clear(j, carry):
        found[j] = 0
        fock[0, j] = 0.0
        return carry

    lax.fori_loop(0, LINKS + 1, clear, 0)
    count = jnp.int32(0)
    for block in range(2):

        def look(step, count):
            for u in range(8):
                code = packed[block, step * 8 + u]
                fits = (code >= 0).astype(jnp.int32)
                spot = jnp.where(code >= 0, count, LINKS)
                found[spot] = code
                fock[0, spot] = tables[block, 1, step * 8 + u]
                count = count + fits
            return count

        count = lax.fori_loop(0, PAIRS, look, count)

    def unpack(j, carry):
        code = found[j]
        for row, bits in enumerate(FIELDS):
            info[row, j] = lax.rem(code, 2**bits)
            code = lax.div(code, 2**bits)
        return carry

    lax.fori_loop(0, LINKS, unpack, 0)


def pick_kernel(
    place, packed, tables, held, got, *refs
):
    targets = refs[: 2 * RANGES]
    info, fock, picked, expanded, dom, source_dom, found = refs[2 * RANGES :]
    list_couplings(packed, tables, info, fock, found)
    for i in range(2 * RANGES):
        dom[i] = targets[i][PAIRS * PNO : PAIRS * PNO + PAIRS, :].astype(F32)
    for i in range(8):
        source_dom[0, i] = held[i].astype(F32)
        source_dom[1, i] = got[i].astype(F32)

    def expand(i, carry):
        for block in range(2):
            for d in range(RANGES):
                rows = targets[RANGES * block + d]
                hot = one_hot(dom[RANGES * block + d, pl.ds(i, 1), :])
                rows = rows[pl.ds(pl.multiple_of(i * PNO, PNO), PNO), :]
                full = jnp.dot(hot, rows, preferred_element_type=F32)
                expanded[block * PAIRS + i, place[d]] = full.T.astype(BF16)
        return carry

    lax.fori_loop(0, PAIRS, expand, 0)

    def pick(step, carry):
        for u in range(4):
            j = step * 4 + u
            for r in range(RANGES):
                at = 4 * info[X_ODD, j] + 2 * (r % 2) + info[X_EVEN, j]
                row = source_dom[r // 2, at, pl.ds(info[SLOT, j], 1), :]
                part = jnp.dot(
                    expanded[info[TARGET, j], r], one_hot(row), preferred_element_type=F32
                )
                picked[j, :, r * PNO : (r + 1) * PNO] = part.astype(BF16)
        return carry

    lax.fori_loop(0, LINKS // 4, pick, 0)


def choose(which, low, high, act):
    if high - low == 1:
        act(low)
        return
    middle = (low + high) // 2

    @pl.when(which < middle)
    def _():
        choose(which, low, middle, act)

    @pl.when(which >= middle)
    def _():
        choose(which, middle, high, act)


def fetch_amplitudes(info, j, a_refs, b_refs, amp):
    rx, slot, rz = info[REL_X, j], info[SLOT, j], info[REL_Z, j]
    rows = pl.ds(pl.multiple_of(lax.rem(slot, 2) * PNO, PNO), PNO)

    def from_a(r):
        amp[j] = a_refs[r][rx, rows, :]

    def from_b(r):
        amp[j] = b_refs[r][rz, rows, :]

    @pl.when(lax.rem(slot, 4) < 2)
    def _():
        choose(rz, 0, 4, from_a)

    @pl.when(lax.rem(slot, 4) >= 2)
    def _():
        choose(rx, 0, 4, from_b)


def project_all(info, fock, inter, amp, acc):
    def first(step, carry):
        for u in range(UNROLL):
            j = step * UNROLL + u
            half = jnp.dot(inter[j], amp[j], preferred_element_type=F32)
            amp[j] = half.astype(BF16)
        return carry

    lax.fori_loop(0, LINKS // UNROLL, first, 0)

    def second(step, carry):
        for u in range(UNROLL):
            j = step * UNROLL + u
            target = info[TARGET, j]
            whole = lax.dot_general(
                amp[j], inter[j], (((1,), (1,)), ((), ())), preferred_element_type=F32
            )
            acc[target] = acc[target] + fock[0, j] * whole
        return carry

    lax.fori_loop(0, LINKS // UNROLL, second, 0)


def first_kernel(info, fock, *refs):
    lists, picked = refs[0:8], refs[8]
    inter_out, own, other = refs[9:12]
    source, amp, acc, inter, sem, amp_sem, out_sem = refs[12:]

    def fetch(j, carry):
        slot, even, odd = info[SLOT, j], info[X_EVEN, j], info[X_ODD, j]
        rows = pl.ds(pl.multiple_of(lax.rem(slot, 4) * PNO, PNO), PNO)

        def copy(src, dst):
            pltpu.make_async_copy(src, dst, sem.at[j]).start()

        def from_colour(colour):
            if colour == 0:
                for bit in range(2):
                    copy(lists[bit].at[odd, :, even, rows], source.at[j, bit])
            elif colour == 1:
                choose(odd, 0, 2, lambda last: copy(
                    lists[2 + last].at[:, even, :, rows], source.at[j]
                ))
            elif colour == 2:
                for bit in range(2):
                    copy(lists[4 + bit].at[even, :, odd, rows], source.at[j, :, bit])
            else:
                choose(even, 0, 2, lambda last: [
                    copy(lists[6 + last].at[bit, odd, :, rows], source.at[j, :, bit])
                    for bit in range(2)
                ])

        choose(lax.div(slot, 4), 0, 4, from_colour)
        at = info[AMP_AT, j]
        far, middle, near = lax.div(at, 4), lax.rem(lax.div(at, 2), 2), lax.rem(at, 2)
        choose(info[AMP_LIST, j], 0, 8, lambda i: pltpu.make_async_copy(
            lists[i].at[far, middle, near, pl.ds(ORBITALS, PNO)], amp.at[j], amp_sem.at[j]
        ).start())
        return carry

    lax.fori_loop(0, LINKS, fetch, 0)
    acc[...] = jnp.zeros_like(acc)

    def intersect(step, carry):
        for u in range(UNROLL):
            j = step * UNROLL + u
            pltpu.make_async_copy(source.at[j], source.at[j], sem.at[j]).wait()
            pltpu.make_async_copy(amp.at[j], amp.at[j], amp_sem.at[j]).wait()
        for u in range(UNROLL):
            j = step * UNROLL + u
            rows = source[j].reshape(RANGES * PNO, PNO)
            block = jnp.dot(picked[j], rows, preferred_element_type=F32)
            inter[j] = block.astype(BF16)
        return carry

    lax.fori_loop(0, LINKS // UNROLL, intersect, 0)
    out = pltpu.make_async_copy(inter, inter_out, out_sem)
    out.start()
    project_all(info, fock, inter, amp, acc)
    out.wait()
    own[...] = acc[0:PAIRS]
    other[...] = acc[PAIRS:].astype(other.dtype)


def next_kernel(info, fock, inter, *refs):
    a_refs, b_refs = refs[0:4], refs[4:8]
    own, other = refs[8:10]
    amp, acc = refs[10:]

    def fetch(j, carry):
        fetch_amplitudes(info, j, a_refs, b_refs, amp)
        return carry

    lax.fori_loop(0, LINKS, fetch, 0)
    acc[...] = jnp.zeros_like(acc)

    project_all(info, fock, inter, amp, acc)
    own[...] = acc[0:PAIRS]
    other[...] = acc[PAIRS:].astype(other.dtype)


VM = pl.BlockSpec(memory_space=pltpu.VMEM)
SM = pl.BlockSpec(memory_space=pltpu.SMEM)
HB = pl.BlockSpec(memory_space=pl.ANY)


def params(mib):
    return pltpu.CompilerParams(vmem_limit_bytes=mib * 1024 * 1024)


BLOCK = jax.ShapeDtypeStruct((PAIRS, PNO, PNO), F32)


def shifted(value, axis, rel):
    return lax.ppermute(value, axis, [((i + rel) % 4, i) for i in range(4)])


def ring(value, axis):
    plus, minus = shifted(value, axis, 1), shifted(value, axis, 3)
    return [value, plus, shifted(value, axis, 2), minus]


def swap_core(value):
    return lax.ppermute(value, "core", [(0, 1), (1, 0)])


def to_class_plane(value):
    moves = []
    for z in range(4):
        for core in range(2):
            for y in range(4):
                moves.append(
                    ((z * 2 + core) * 4 + y, (y * 2 + core) * 4 + (z + 2 * core) % 4)
                )
    return lax.ppermute(value, ("z", "core", "grp"), moves)


def joined(held, got, extra=0):
    count, rows, columns = held.shape
    both = jnp.zeros((2 * count, rows + extra, columns), held.dtype)
    both = lax.optimization_barrier(lax.dynamic_update_slice(both, held, (0, 0, 0)))
    return lax.dynamic_update_slice(both, got, (count, 0, 0))


def plane_gather(half_a, half_b):
    a, b = lax.optimization_barrier(
        (jnp.stack(ring(half_a, "x")), jnp.stack(ring(half_b, "z")))
    )
    return ring(a, "z"), ring(b, "x")


def reduce_core_y(own, other, y, dtype):
    other = swap_core(other)
    pieces = []
    for d in range(4):
        first = 4 * ((y + d) % 4)
        pieces.append(
            lax.dynamic_slice_in_dim(own, first, 4, 0)
            + lax.dynamic_slice_in_dim(other, first, 4, 0)
        )
    result = pieces[0]
    for d in (1, 3, 2):
        arrived = shifted(pieces[d].astype(dtype), "grp", 4 - d)
        result = result + arrived.astype(F32)
    return result


def on_device(
    coefficients,
    domain,
    coupling_owner,
    coupling_slot,
    coupling_fock,
    exchange_integrals,
    pno_energy,
    pair_shift,
    amplitudes_start,
):
    z, x, core, y = [lax.axis_index(name) for name in ("z", "x", "core", "grp")]
    class_z = (y + 2 * core) % 4
    flat = coefficients.reshape(PAIRS * PNO, PNO)
    local = (domain - y * NB).astype(BF16)
    start = lax.dynamic_slice_in_dim(amplitudes_start, 4 * y, 4, 0).astype(BF16)
    start = start.reshape(4 * PNO, PNO)
    flat_in = to_class_plane(flat)
    start_in = to_class_plane(jnp.concatenate([start, local]))
    local_in = start_in[4 * PNO :]
    colours = []
    for k in range(4):
        rows = [
            flat_in[k * ORBITALS : (k + 1) * ORBITALS],
            start_in[k * PNO : (k + 1) * PNO],
        ]
        if k == 0:
            rows.append(local_in)
        colours.append(jnp.concatenate(rows)[None])

    table = jnp.stack(
        [(coupling_owner * PAIRS + coupling_slot).astype(F32), coupling_fock]
    ).reshape(2, -1)
    tables = jnp.stack([table, swap_core(table)])
    rest = jnp.concatenate([tables[1], jnp.zeros((PAIRS - 2, PNO), F32)]).astype(BF16)
    own_targets = jnp.concatenate([flat, local, flat_in[:PAIRS], start_in[:PAIRS], rest])
    targets = [own_targets]
    for d in range(3):
        targets.append(shifted(targets[-1], "grp", 1))
    targets += [swap_core(rows) for rows in targets]
    packed = pack_couplings(tables[:, 0].astype(jnp.int32), z, x, core, class_z)

    for step in range(3):
        got = [lax.ppermute(colours[k], *STEPS[k][step]) for k in range(4)]
        if step == 2:
            held_domains = joined(colours[0][:, COLOUR:], got[0][:, COLOUR:])
            got_domains = lax.ppermute(held_domains, *STEPS[0][3])
            last = joined(colours[3], got[3], extra=PAIRS)
            last = lax.dynamic_update_slice(last, got_domains, (0, COLOUR, 0))
        colours = [joined(colours[k], got[k]) for k in range(4)]
    colours[3] = last
    got = [lax.ppermute(colours[k], *STEPS[k][3]) for k in range(4)]
    lists = []
    for k in range(4):
        lists.append(colours[k].reshape(2, 2, 2, -1, PNO))
        lists.append(got[k].reshape(2, 2, 2, -1, PNO))

    even, odd = ways((y + jnp.arange(RANGES, dtype=jnp.int32) - z) % 4, z)
    place = even + 2 * odd
    info, fock, picked = pl.pallas_call(
        pick_kernel,
        out_shape=(
            jax.ShapeDtypeStruct((8, LINKS), jnp.int32),
            jax.ShapeDtypeStruct((1, LINKS + 1), F32),
            jax.ShapeDtypeStruct((LINKS, PNO, RANGES * PNO), BF16),
        ),
        in_specs=[SM, SM, SM] + [VM] * 10,
        out_specs=(SM, SM, VM),
        scratch_shapes=[
            pltpu.VMEM((2 * PAIRS, RANGES, PNO, NB), BF16),
            pltpu.VMEM((2 * RANGES, PAIRS, PNO), F32),
            pltpu.VMEM((2, 8, PAIRS, PNO), F32),
            pltpu.SMEM((LINKS + 1,), jnp.int32),
        ],
        compiler_params=params(22),
        name="pick_targets",
    )(place.astype(jnp.int32), packed, tables, held_domains, got_domains, *targets)

    inter, own, other = pl.pallas_call(
        first_kernel,
        out_shape=(jax.ShapeDtypeStruct((LINKS, PNO, PNO), BF16), BLOCK, BLOCK),
        in_specs=[SM, SM] + [HB] * 8 + [VM],
        out_specs=(pl.BlockSpec(memory_space=pltpu.HBM), VM, VM),
        scratch_shapes=[
            pltpu.VMEM((LINKS, 2, 2, PNO, PNO), BF16),
            pltpu.VMEM((LINKS, PNO, PNO), BF16),
            pltpu.VMEM((2 * PAIRS, PNO, PNO), F32),
            pltpu.VMEM((LINKS, PNO, PNO), BF16),
            pltpu.SemaphoreType.DMA((LINKS,)),
            pltpu.SemaphoreType.DMA((LINKS,)),
            pltpu.SemaphoreType.DMA,
        ],
        compiler_params=params(19),
        name="intersect_and_project",
    )(info, fock, *lists, picked)

    energy = lax.dynamic_slice_in_dim(pno_energy, 4 * y, 4, 0)
    shift = lax.dynamic_slice_in_dim(pair_shift, 4 * y, 4, 0)
    exchange = lax.dynamic_slice_in_dim(exchange_integrals, 4 * y, 4, 0)
    denominator = energy[:, :, None] + energy[:, None, :] + shift[:, None, None]

    amplitudes = -(exchange + reduce_core_y(own, other, y, F32)) / denominator
    sent = to_class_plane(amplitudes.astype(BF16).reshape(4 * PNO, PNO))
    a_refs, b_refs = plane_gather(sent[: 2 * PNO], sent[2 * PNO :])
    own, other = pl.pallas_call(
        next_kernel,
        out_shape=(BLOCK, BLOCK),
        in_specs=[SM, SM] + [VM] * 9,
        out_specs=(VM, VM),
        scratch_shapes=[
            pltpu.VMEM((LINKS, PNO, PNO), BF16),
            pltpu.VMEM((2 * PAIRS, PNO, PNO), F32),
        ],
        compiler_params=params(12),
        name="project",
    )(info, fock, inter, *a_refs, *b_refs)
    amplitudes = -(exchange + reduce_core_y(own, other, y, BF16)) / denominator
    amplitudes = lax.reduce_precision(amplitudes, exponent_bits=8, mantissa_bits=7)
    gathered = ring(amplitudes.astype(BF16), "grp")
    result = jnp.zeros_like(exchange_integrals)
    for d in range(4):
        piece = gathered[d].astype(F32)
        result = lax.dynamic_update_slice_in_dim(result, piece, 4 * ((y + d) % 4), 0)
    return result


def solution(mesh):
    fine = Mesh(mesh.devices.reshape(4, 4, 2, 4), ("z", "x", "core", "grp"))
    placed = (
        P(SPLIT, "grp", None),
        P(SPLIT, "grp"),
        P(SPLIT, None),
        P(SPLIT, None),
        P(SPLIT, None),
        P(SPLIT, None, None),
        P(SPLIT, None),
        P(SPLIT),
        P(SPLIT, None, None),
    )
    return jax.shard_map(
        on_device, mesh=fine, in_specs=placed, out_specs=P(SPLIT, None, None), check_vma=False
    )
```

```python
import jax
import jax.numpy as jnp
from jax import lax
from jax.experimental import pallas as pl
from jax.experimental.pallas import tpu as pltpu
from jax.sharding import Mesh, PartitionSpec as P

NB = 192
RANGES = 4
PAIRS = 16
PNO = 128
LINKS = 40
UNROLL = 8
ORBITALS = 4 * PNO
COLOUR = ORBITALS + PNO
EVEN = [(0, 1), (1, 0), (2, 3), (3, 2)]
ODD = [(1, 2), (2, 1), (3, 0), (0, 3)]
STEPS = (
    (("x", EVEN), ("z", EVEN), ("x", ODD), ("z", ODD)),
    (("z", EVEN), ("x", EVEN), ("z", ODD), ("x", ODD)),
    (("x", ODD), ("z", ODD), ("x", EVEN), ("z", EVEN)),
    (("z", ODD), ("x", ODD), ("z", EVEN), ("x", EVEN)),
)
BF16 = jnp.bfloat16
F32 = jnp.float32
SPLIT = ("z", "x", "core")
TARGET, SLOT, REL_X, REL_Z, X_EVEN, X_ODD, AMP_LIST, AMP_AT = range(8)


def one_hot(row):
    functions = lax.broadcasted_iota(jnp.int32, (NB, PNO), 0).astype(F32)
    return jnp.where(functions == row, 1.0, 0.0).astype(BF16)


def ways(rel, here):
    lean = 1 + 2 * lax.rem(here, 2)
    even = (rel == 2) | (rel == lean)
    odd = (rel == 2) | (rel == 4 - lean)
    return even.astype(jnp.int32), odd.astype(jnp.int32)


FIELDS = (5, 4, 2, 2, 1, 1, 3, 3)


def pack_couplings(named, z, x, core, class_z):
    owner, slot = named // PAIRS, named % PAIRS
    mine = (owner % 2 == core) & (owner // 8 == class_z)
    rel_x, rel_z = ((owner // 2) % 4 - x) % 4, (slot // 4 - z) % 4
    x_even, x_odd = ways(rel_x, x)
    z_even, z_odd = ways(rel_z, z)
    colour = slot % 4
    x_first, even_first = colour % 2 == 0, colour < 2
    x_one, x_two = jnp.where(even_first, x_even, x_odd), jnp.where(even_first, x_odd, x_even)
    z_one, z_two = jnp.where(even_first, z_even, z_odd), jnp.where(even_first, z_odd, z_even)
    near = jnp.where(x_first, x_one + 2 * z_one, z_one + 2 * x_one)
    far, last = jnp.where(x_first, x_two, z_two), jnp.where(x_first, z_two, x_two)
    target = lax.broadcasted_iota(jnp.int32, named.shape, 0) * PAIRS
    target = target + lax.broadcasted_iota(jnp.int32, named.shape, 1) // 8
    values = (target, slot, rel_x, rel_z, x_even, x_odd, 2 * colour + last, near + 4 * far)
    code, place = 0, 1
    for bits, value in zip(FIELDS, values):
        code = code + value * place
        place *= 2**bits
    return jnp.where(mine, code, -1).astype(jnp.int32)


def list_couplings(packed, tables, info, fock, found):
    def clear(j, carry):
        found[j] = 0
        fock[0, j] = 0.0
        return carry

    lax.fori_loop(0, LINKS + 1, clear, 0)
    count = jnp.int32(0)
    for block in range(2):

        def look(step, count):
            for u in range(8):
                code = packed[block, step * 8 + u]
                fits = (code >= 0).astype(jnp.int32)
                spot = jnp.where(code >= 0, count, LINKS)
                found[spot] = code
                fock[0, spot] = tables[block, 1, step * 8 + u]
                count = count + fits
            return count

        count = lax.fori_loop(0, PAIRS, look, count)

    def unpack(j, carry):
        code = found[j]
        for row, bits in enumerate(FIELDS):
            info[row, j] = lax.rem(code, 2**bits)
            code = lax.div(code, 2**bits)
        return carry

    lax.fori_loop(0, LINKS, unpack, 0)


def pick_kernel(
    place, packed, tables, targets, held, got,
    info, fock, picked, expanded, dom, source_dom, found,
):
    list_couplings(packed, tables, info, fock, found)
    for i in range(2 * RANGES):
        dom[i] = targets[i, PAIRS * PNO : PAIRS * PNO + PAIRS, :].astype(F32)
    for i in range(8):
        source_dom[0, i] = held[i].astype(F32)
        source_dom[1, i] = got[i].astype(F32)

    def expand(i, carry):
        for block in range(2):
            for r in range(RANGES):
                d = place[4 * block + r]
                hot = one_hot(dom[d, pl.ds(i, 1), :])
                rows = targets[d, pl.ds(pl.multiple_of(i * PNO, PNO), PNO), :]
                full = jnp.dot(hot, rows, preferred_element_type=F32)
                expanded[block * PAIRS + i, r] = full.T.astype(BF16)
        return carry

    lax.fori_loop(0, PAIRS, expand, 0)

    def pick(step, carry):
        for u in range(4):
            j = step * 4 + u
            for r in range(RANGES):
                at = 4 * info[X_ODD, j] + 2 * (r % 2) + info[X_EVEN, j]
                row = source_dom[r // 2, at, pl.ds(info[SLOT, j], 1), :]
                part = jnp.dot(
                    expanded[info[TARGET, j], r], one_hot(row), preferred_element_type=F32
                )
                picked[j, :, r * PNO : (r + 1) * PNO] = part.astype(BF16)
        return carry

    lax.fori_loop(0, LINKS // 4, pick, 0)


def choose(which, low, high, act):
    if high - low == 1:
        act(low)
        return
    middle = (low + high) // 2

    @pl.when(which < middle)
    def _():
        choose(which, low, middle, act)

    @pl.when(which >= middle)
    def _():
        choose(which, middle, high, act)


def fetch_amplitudes(info, j, a_refs, b_refs, amp):
    rx, slot, rz = info[REL_X, j], info[SLOT, j], info[REL_Z, j]
    rows = pl.ds(pl.multiple_of(lax.rem(slot, 2) * PNO, PNO), PNO)

    def from_a(r):
        amp[j] = a_refs[r][rx, rows, :]

    def from_b(r):
        amp[j] = b_refs[r][rz, rows, :]

    @pl.when(lax.rem(slot, 4) < 2)
    def _():
        choose(rz, 0, 4, from_a)

    @pl.when(lax.rem(slot, 4) >= 2)
    def _():
        choose(rx, 0, 4, from_b)


def project_all(info, fock, inter, amp, acc):
    def first(step, carry):
        for u in range(UNROLL):
            j = step * UNROLL + u
            half = jnp.dot(inter[j], amp[j], preferred_element_type=F32)
            amp[j] = half.astype(BF16)
        return carry

    lax.fori_loop(0, LINKS // UNROLL, first, 0)

    def second(step, carry):
        for u in range(UNROLL):
            j = step * UNROLL + u
            target = info[TARGET, j]
            whole = lax.dot_general(
                amp[j], inter[j], (((1,), (1,)), ((), ())), preferred_element_type=F32
            )
            acc[target] = acc[target] + fock[0, j] * whole
        return carry

    lax.fori_loop(0, LINKS // UNROLL, second, 0)


def first_kernel(info, fock, *refs):
    lists, picked = refs[0:8], refs[8]
    inter_out, own, other = refs[9:12]
    source, amp, acc, inter, sem, amp_sem, out_sem = refs[12:]

    def fetch(j, carry):
        slot, even, odd = info[SLOT, j], info[X_EVEN, j], info[X_ODD, j]
        rows = pl.ds(pl.multiple_of(lax.rem(slot, 4) * PNO, PNO), PNO)

        def copy(src, dst):
            pltpu.make_async_copy(src, dst, sem.at[j]).start()

        def from_colour(colour):
            if colour == 0:
                for bit in range(2):
                    copy(lists[bit].at[odd, :, even, rows], source.at[j, bit])
            elif colour == 1:
                choose(odd, 0, 2, lambda last: copy(
                    lists[2 + last].at[:, even, :, rows], source.at[j]
                ))
            elif colour == 2:
                for bit in range(2):
                    copy(lists[4 + bit].at[even, :, odd, rows], source.at[j, :, bit])
            else:
                choose(even, 0, 2, lambda last: [
                    copy(lists[6 + last].at[bit, odd, :, rows], source.at[j, :, bit])
                    for bit in range(2)
                ])

        choose(lax.div(slot, 4), 0, 4, from_colour)
        at = info[AMP_AT, j]
        far, middle, near = lax.div(at, 4), lax.rem(lax.div(at, 2), 2), lax.rem(at, 2)
        choose(info[AMP_LIST, j], 0, 8, lambda i: pltpu.make_async_copy(
            lists[i].at[far, middle, near, pl.ds(ORBITALS, PNO)], amp.at[j], amp_sem.at[j]
        ).start())
        return carry

    lax.fori_loop(0, LINKS, fetch, 0)
    acc[...] = jnp.zeros_like(acc)

    def intersect(step, carry):
        for u in range(UNROLL):
            j = step * UNROLL + u
            pltpu.make_async_copy(source.at[j], source.at[j], sem.at[j]).wait()
            pltpu.make_async_copy(amp.at[j], amp.at[j], amp_sem.at[j]).wait()
        for u in range(UNROLL):
            j = step * UNROLL + u
            rows = source[j].reshape(RANGES * PNO, PNO)
            block = jnp.dot(picked[j], rows, preferred_element_type=F32)
            inter[j] = block.astype(BF16)
        return carry

    lax.fori_loop(0, LINKS // UNROLL, intersect, 0)
    out = pltpu.make_async_copy(inter, inter_out, out_sem)
    out.start()
    project_all(info, fock, inter, amp, acc)
    out.wait()
    own[...] = acc[0:PAIRS]
    other[...] = acc[PAIRS:].astype(other.dtype)


def next_kernel(info, fock, inter, *refs):
    a_refs, b_refs = refs[0:4], refs[4:8]
    own, other = refs[8:10]
    amp, acc = refs[10:]

    def fetch(j, carry):
        fetch_amplitudes(info, j, a_refs, b_refs, amp)
        return carry

    lax.fori_loop(0, LINKS, fetch, 0)
    acc[...] = jnp.zeros_like(acc)

    project_all(info, fock, inter, amp, acc)
    own[...] = acc[0:PAIRS]
    other[...] = acc[PAIRS:].astype(other.dtype)


VM = pl.BlockSpec(memory_space=pltpu.VMEM)
SM = pl.BlockSpec(memory_space=pltpu.SMEM)
HB = pl.BlockSpec(memory_space=pl.ANY)


def params(mib):
    return pltpu.CompilerParams(vmem_limit_bytes=mib * 1024 * 1024)


BLOCK = jax.ShapeDtypeStruct((PAIRS, PNO, PNO), F32)


def shifted(value, axis, rel):
    return lax.ppermute(value, axis, [((i + rel) % 4, i) for i in range(4)])


def ring(value, axis):
    plus, minus = shifted(value, axis, 1), shifted(value, axis, 3)
    return [value, plus, shifted(value, axis, 2), minus]


def swap_core(value):
    return lax.ppermute(value, "core", [(0, 1), (1, 0)])


def to_class_plane(value):
    moves = []
    for z in range(4):
        for core in range(2):
            for y in range(4):
                moves.append(
                    ((z * 2 + core) * 4 + y, (y * 2 + core) * 4 + (z + 2 * core) % 4)
                )
    return lax.ppermute(value, ("z", "core", "grp"), moves)


def joined(held, got, extra=0):
    count, rows, columns = held.shape
    both = jnp.zeros((2 * count, rows + extra, columns), held.dtype)
    both = lax.optimization_barrier(lax.dynamic_update_slice(both, held, (0, 0, 0)))
    return lax.dynamic_update_slice(both, got, (count, 0, 0))


def plane_gather(half_a, half_b):
    a, b = lax.optimization_barrier(
        (jnp.stack(ring(half_a, "x")), jnp.stack(ring(half_b, "z")))
    )
    return ring(a, "z"), ring(b, "x")


def reduce_core_y(own, other, y, dtype):
    other = swap_core(other)
    pieces = []
    for d in range(4):
        first = 4 * ((y + d) % 4)
        pieces.append(
            lax.dynamic_slice_in_dim(own, first, 4, 0)
            + lax.dynamic_slice_in_dim(other, first, 4, 0)
        )
    result = pieces[0]
    for d in (1, 3, 2):
        arrived = shifted(pieces[d].astype(dtype), "grp", 4 - d)
        result = result + arrived.astype(F32)
    return result


def on_device(
    coefficients,
    domain,
    coupling_owner,
    coupling_slot,
    coupling_fock,
    exchange_integrals,
    pno_energy,
    pair_shift,
    amplitudes_start,
):
    z, x, core, y = [lax.axis_index(name) for name in ("z", "x", "core", "grp")]
    class_z = (y + 2 * core) % 4
    flat = coefficients.reshape(PAIRS * PNO, PNO)
    local = (domain - y * NB).astype(BF16)
    start = lax.dynamic_slice_in_dim(amplitudes_start, 4 * y, 4, 0).astype(BF16)
    start = start.reshape(4 * PNO, PNO)
    flat_in = to_class_plane(flat)
    start_in = to_class_plane(jnp.concatenate([start, local]))
    local_in = start_in[4 * PNO :]
    colours = []
    for k in range(4):
        rows = [
            flat_in[k * ORBITALS : (k + 1) * ORBITALS],
            start_in[k * PNO : (k + 1) * PNO],
        ]
        if k == 0:
            rows.append(local_in)
        colours.append(jnp.concatenate(rows)[None])

    table = jnp.stack(
        [(coupling_owner * PAIRS + coupling_slot).astype(F32), coupling_fock]
    ).reshape(2, -1)
    tables = jnp.stack([table, swap_core(table)])
    rest = jnp.concatenate([tables[1], jnp.zeros((PAIRS - 2, PNO), F32)]).astype(BF16)
    own_targets = jnp.concatenate([flat, local, flat_in[:PAIRS], start_in[:PAIRS], rest])
    targets = lax.all_gather(own_targets, ("core", "grp"))
    packed = pack_couplings(tables[:, 0].astype(jnp.int32), z, x, core, class_z)

    for step in range(3):
        got = [lax.ppermute(colours[k], *STEPS[k][step]) for k in range(4)]
        if step == 2:
            held_domains = joined(colours[0][:, COLOUR:], got[0][:, COLOUR:])
            got_domains = lax.ppermute(held_domains, *STEPS[0][3])
            last = joined(colours[3], got[3], extra=PAIRS)
            last = lax.dynamic_update_slice(last, got_domains, (0, COLOUR, 0))
        colours = [joined(colours[k], got[k]) for k in range(4)]
    colours[3] = last
    got = [lax.ppermute(colours[k], *STEPS[k][3]) for k in range(4)]
    lists = []
    for k in range(4):
        lists.append(colours[k].reshape(2, 2, 2, -1, PNO))
        lists.append(got[k].reshape(2, 2, 2, -1, PNO))

    lean = 1 - 2 * (z % 2)
    ranges = jnp.stack([z, z + lean, z - lean, z + 2]) % 4
    place = jnp.concatenate([4 * core + ranges, 4 * (1 - core) + ranges])
    info, fock, picked = pl.pallas_call(
        pick_kernel,
        out_shape=(
            jax.ShapeDtypeStruct((8, LINKS), jnp.int32),
            jax.ShapeDtypeStruct((1, LINKS + 1), F32),
            jax.ShapeDtypeStruct((LINKS, PNO, RANGES * PNO), BF16),
        ),
        in_specs=[SM, SM, SM, VM, VM, VM],
        out_specs=(SM, SM, VM),
        scratch_shapes=[
            pltpu.VMEM((2 * PAIRS, RANGES, PNO, NB), BF16),
            pltpu.VMEM((2 * RANGES, PAIRS, PNO), F32),
            pltpu.VMEM((2, 8, PAIRS, PNO), F32),
            pltpu.SMEM((LINKS + 1,), jnp.int32),
        ],
        compiler_params=params(22),
        name="pick_targets",
    )(place.astype(jnp.int32), packed, tables, targets, held_domains, got_domains)

    inter, own, other = pl.pallas_call(
        first_kernel,
        out_shape=(jax.ShapeDtypeStruct((LINKS, PNO, PNO), BF16), BLOCK, BLOCK),
        in_specs=[SM, SM] + [HB] * 8 + [VM],
        out_specs=(pl.BlockSpec(memory_space=pltpu.HBM), VM, VM),
        scratch_shapes=[
            pltpu.VMEM((LINKS, 2, 2, PNO, PNO), BF16),
            pltpu.VMEM((LINKS, PNO, PNO), BF16),
            pltpu.VMEM((2 * PAIRS, PNO, PNO), F32),
            pltpu.VMEM((LINKS, PNO, PNO), BF16),
            pltpu.SemaphoreType.DMA((LINKS,)),
            pltpu.SemaphoreType.DMA((LINKS,)),
            pltpu.SemaphoreType.DMA,
        ],
        compiler_params=params(19),
        name="intersect_and_project",
    )(info, fock, *lists, picked)

    energy = lax.dynamic_slice_in_dim(pno_energy, 4 * y, 4, 0)
    shift = lax.dynamic_slice_in_dim(pair_shift, 4 * y, 4, 0)
    exchange = lax.dynamic_slice_in_dim(exchange_integrals, 4 * y, 4, 0)
    denominator = energy[:, :, None] + energy[:, None, :] + shift[:, None, None]

    amplitudes = -(exchange + reduce_core_y(own, other, y, F32)) / denominator
    sent = to_class_plane(amplitudes.astype(BF16).reshape(4 * PNO, PNO))
    a_refs, b_refs = plane_gather(sent[: 2 * PNO], sent[2 * PNO :])
    own, other = pl.pallas_call(
        next_kernel,
        out_shape=(BLOCK, BLOCK),
        in_specs=[SM, SM] + [VM] * 9,
        out_specs=(VM, VM),
        scratch_shapes=[
            pltpu.VMEM((LINKS, PNO, PNO), BF16),
            pltpu.VMEM((2 * PAIRS, PNO, PNO), F32),
        ],
        compiler_params=params(12),
        name="project",
    )(info, fock, inter, *a_refs, *b_refs)
    amplitudes = -(exchange + reduce_core_y(own, other, y, BF16)) / denominator
    amplitudes = lax.reduce_precision(amplitudes, exponent_bits=8, mantissa_bits=7)
    gathered = ring(amplitudes.astype(BF16), "grp")
    result = jnp.zeros_like(exchange_integrals)
    for d in range(4):
        piece = gathered[d].astype(F32)
        result = lax.dynamic_update_slice_in_dim(result, piece, 4 * ((y + d) % 4), 0)
    return result


def solution(mesh):
    fine = Mesh(mesh.devices.reshape(4, 4, 2, 4), ("z", "x", "core", "grp"))
    placed = (
        P(SPLIT, "grp", None),
        P(SPLIT, "grp"),
        P(SPLIT, None),
        P(SPLIT, None),
        P(SPLIT, None),
        P(SPLIT, None, None),
        P(SPLIT, None),
        P(SPLIT),
        P(SPLIT, None, None),
    )
    return jax.shard_map(
        on_device, mesh=fine, in_specs=placed, out_specs=P(SPLIT, None, None), check_vma=False
    )
```

```python
import jax
import jax.numpy as jnp
from jax import lax
from jax.experimental import pallas as pl
from jax.experimental.pallas import tpu as pltpu
from jax.sharding import Mesh, PartitionSpec as P

NB = 192
RANGES = 4
PAIRS = 16
PNO = 128
LINKS = 40
UNROLL = 8
ORBITALS = 4 * PNO
COLOUR = ORBITALS + PNO
EVEN = [(0, 1), (1, 0), (2, 3), (3, 2)]
ODD = [(1, 2), (2, 1), (3, 0), (0, 3)]
STEPS = (
    (("x", EVEN), ("z", EVEN), ("x", ODD), ("z", ODD)),
    (("z", EVEN), ("x", EVEN), ("z", ODD), ("x", ODD)),
    (("x", ODD), ("z", ODD), ("x", EVEN), ("z", EVEN)),
    (("z", ODD), ("x", ODD), ("z", EVEN), ("x", EVEN)),
)
BF16 = jnp.bfloat16
F32 = jnp.float32
SPLIT = ("z", "x", "core")
TARGET, SLOT, REL_X, REL_Z, X_EVEN, X_ODD, AMP_LIST, AMP_AT = range(8)


def one_hot(row):
    functions = lax.broadcasted_iota(jnp.int32, (NB, PNO), 0).astype(F32)
    return jnp.where(functions == row, 1.0, 0.0).astype(BF16)


def ways(rel, here):
    lean = 1 + 2 * lax.rem(here, 2)
    even = (rel == 2) | (rel == lean)
    odd = (rel == 2) | (rel == 4 - lean)
    return even.astype(jnp.int32), odd.astype(jnp.int32)


FIELDS = (5, 4, 2, 2, 1, 1, 3, 3)


def pack_couplings(named, z, x, core, class_z):
    owner, slot = named // PAIRS, named % PAIRS
    mine = (owner % 2 == core) & (owner // 8 == class_z)
    rel_x, rel_z = ((owner // 2) % 4 - x) % 4, (slot // 4 - z) % 4
    x_even, x_odd = ways(rel_x, x)
    z_even, z_odd = ways(rel_z, z)
    colour = slot % 4
    x_first, even_first = colour % 2 == 0, colour < 2
    x_one, x_two = jnp.where(even_first, x_even, x_odd), jnp.where(even_first, x_odd, x_even)
    z_one, z_two = jnp.where(even_first, z_even, z_odd), jnp.where(even_first, z_odd, z_even)
    near = jnp.where(x_first, x_one + 2 * z_one, z_one + 2 * x_one)
    far, last = jnp.where(x_first, x_two, z_two), jnp.where(x_first, z_two, x_two)
    target = lax.broadcasted_iota(jnp.int32, named.shape, 0) * PAIRS
    target = target + lax.broadcasted_iota(jnp.int32, named.shape, 1) // 8
    values = (target, slot, rel_x, rel_z, x_even, x_odd, 2 * colour + last, near + 4 * far)
    code, place = 0, 1
    for bits, value in zip(FIELDS, values):
        code = code + value * place
        place *= 2**bits
    return jnp.where(mine, code, -1).astype(jnp.int32)


def list_couplings(packed, tables, info, fock, found):
    def clear(j, carry):
        found[j] = 0
        fock[0, j] = 0.0
        return carry

    lax.fori_loop(0, LINKS + 1, clear, 0)
    count = jnp.int32(0)
    for block in range(2):

        def look(step, count):
            for u in range(8):
                code = packed[block, step * 8 + u]
                fits = (code >= 0).astype(jnp.int32)
                spot = jnp.where(code >= 0, count, LINKS)
                found[spot] = code
                fock[0, spot] = tables[block, 1, step * 8 + u]
                count = count + fits
            return count

        count = lax.fori_loop(0, PAIRS, look, count)

    def unpack(j, carry):
        code = found[j]
        for row, bits in enumerate(FIELDS):
            info[row, j] = lax.rem(code, 2**bits)
            code = lax.div(code, 2**bits)
        return carry

    lax.fori_loop(0, LINKS, unpack, 0)


def pick_kernel(
    place, packed, tables, held, got, *refs
):
    targets = refs[: 2 * RANGES]
    info, fock, picked, expanded, dom, source_dom, found = refs[2 * RANGES :]
    list_couplings(packed, tables, info, fock, found)
    for i in range(2 * RANGES):
        dom[i] = targets[i][PAIRS * PNO : PAIRS * PNO + PAIRS, :].astype(F32)
    for i in range(8):
        source_dom[0, i] = held[i].astype(F32)
        source_dom[1, i] = got[i].astype(F32)

    def expand(i, carry):
        for block in range(2):
            for d in range(RANGES):
                rows = targets[RANGES * block + d]
                hot = one_hot(dom[RANGES * block + d, pl.ds(i, 1), :])
                rows = rows[pl.ds(pl.multiple_of(i * PNO, PNO), PNO), :]
                full = jnp.dot(hot, rows, preferred_element_type=F32)
                expanded[block * PAIRS + i, place[d]] = full.T.astype(BF16)
        return carry

    lax.fori_loop(0, PAIRS, expand, 0)

    def pick(step, carry):
        for u in range(4):
            j = step * 4 + u
            for r in range(RANGES):
                at = 4 * info[X_ODD, j] + 2 * (r % 2) + info[X_EVEN, j]
                row = source_dom[r // 2, at, pl.ds(info[SLOT, j], 1), :]
                part = jnp.dot(
                    expanded[info[TARGET, j], r], one_hot(row), preferred_element_type=F32
                )
                picked[j, :, r * PNO : (r + 1) * PNO] = part.astype(BF16)
        return carry

    lax.fori_loop(0, LINKS // 4, pick, 0)


def choose(which, low, high, act):
    if high - low == 1:
        act(low)
        return
    middle = (low + high) // 2

    @pl.when(which < middle)
    def _():
        choose(which, low, middle, act)

    @pl.when(which >= middle)
    def _():
        choose(which, middle, high, act)


def fetch_amplitudes(info, j, a_refs, b_refs, amp):
    rx, slot, rz = info[REL_X, j], info[SLOT, j], info[REL_Z, j]
    rows = pl.ds(pl.multiple_of(lax.rem(slot, 2) * PNO, PNO), PNO)

    def from_a(r):
        amp[j] = a_refs[r][rx, rows, :]

    def from_b(r):
        amp[j] = b_refs[r][rz, rows, :]

    @pl.when(lax.rem(slot, 4) < 2)
    def _():
        choose(rz, 0, 4, from_a)

    @pl.when(lax.rem(slot, 4) >= 2)
    def _():
        choose(rx, 0, 4, from_b)


def project_all(info, fock, inter, amp, acc):
    def first(step, carry):
        for u in range(UNROLL):
            j = step * UNROLL + u
            half = jnp.dot(inter[j], amp[j], preferred_element_type=F32)
            amp[j] = half.astype(BF16)
        return carry

    lax.fori_loop(0, LINKS // UNROLL, first, 0)

    def second(step, carry):
        for u in range(UNROLL):
            j = step * UNROLL + u
            target = info[TARGET, j]
            whole = lax.dot_general(
                amp[j], inter[j], (((1,), (1,)), ((), ())), preferred_element_type=F32
            )
            acc[target] = acc[target] + fock[0, j] * whole
        return carry

    lax.fori_loop(0, LINKS // UNROLL, second, 0)


def first_kernel(info, fock, *refs):
    lists, picked = refs[0:8], refs[8]
    inter_out, own, other = refs[9:12]
    source, amp, acc, inter, sem, amp_sem, out_sem = refs[12:]

    def fetch(j, carry):
        slot, even, odd = info[SLOT, j], info[X_EVEN, j], info[X_ODD, j]
        rows = pl.ds(pl.multiple_of(lax.rem(slot, 4) * PNO, PNO), PNO)

        def copy(src, dst):
            pltpu.make_async_copy(src, dst, sem.at[j]).start()

        def from_colour(colour):
            if colour == 0:
                for bit in range(2):
                    copy(lists[bit].at[odd, :, even, rows], source.at[j, bit])
            elif colour == 1:
                choose(odd, 0, 2, lambda last: copy(
                    lists[2 + last].at[:, even, :, rows], source.at[j]
                ))
            elif colour == 2:
                for bit in range(2):
                    copy(lists[4 + bit].at[even, :, odd, rows], source.at[j, :, bit])
            else:
                choose(even, 0, 2, lambda last: [
                    copy(lists[6 + last].at[bit, odd, :, rows], source.at[j, :, bit])
                    for bit in range(2)
                ])

        choose(lax.div(slot, 4), 0, 4, from_colour)
        at = info[AMP_AT, j]
        far, middle, near = lax.div(at, 4), lax.rem(lax.div(at, 2), 2), lax.rem(at, 2)
        choose(info[AMP_LIST, j], 0, 8, lambda i: pltpu.make_async_copy(
            lists[i].at[far, middle, near, pl.ds(ORBITALS, PNO)], amp.at[j], amp_sem.at[j]
        ).start())
        return carry

    lax.fori_loop(0, LINKS, fetch, 0)
    acc[...] = jnp.zeros_like(acc)

    def intersect(step, carry):
        for u in range(UNROLL):
            j = step * UNROLL + u
            pltpu.make_async_copy(source.at[j], source.at[j], sem.at[j]).wait()
            pltpu.make_async_copy(amp.at[j], amp.at[j], amp_sem.at[j]).wait()
        for u in range(UNROLL):
            j = step * UNROLL + u
            rows = source[j].reshape(RANGES * PNO, PNO)
            block = jnp.dot(picked[j], rows, preferred_element_type=F32)
            inter[j] = block.astype(BF16)
        return carry

    lax.fori_loop(0, LINKS // UNROLL, intersect, 0)
    out = pltpu.make_async_copy(inter, inter_out, out_sem)
    out.start()
    project_all(info, fock, inter, amp, acc)
    out.wait()
    own[...] = acc[0:PAIRS]
    other[...] = acc[PAIRS:].astype(other.dtype)


def next_kernel(info, fock, inter, *refs):
    a_refs, b_refs = refs[0:4], refs[4:8]
    own, other = refs[8:10]
    amp, acc = refs[10:]

    def fetch(j, carry):
        fetch_amplitudes(info, j, a_refs, b_refs, amp)
        return carry

    lax.fori_loop(0, LINKS, fetch, 0)
    acc[...] = jnp.zeros_like(acc)

    project_all(info, fock, inter, amp, acc)
    own[...] = acc[0:PAIRS]
    other[...] = acc[PAIRS:].astype(other.dtype)


VM = pl.BlockSpec(memory_space=pltpu.VMEM)
SM = pl.BlockSpec(memory_space=pltpu.SMEM)
HB = pl.BlockSpec(memory_space=pl.ANY)


def params(mib):
    return pltpu.CompilerParams(vmem_limit_bytes=mib * 1024 * 1024)


BLOCK = jax.ShapeDtypeStruct((PAIRS, PNO, PNO), F32)


def shifted(value, axis, rel):
    return lax.ppermute(value, axis, [((i + rel) % 4, i) for i in range(4)])


def ring(value, axis):
    plus, minus = shifted(value, axis, 1), shifted(value, axis, 3)
    return [value, plus, shifted(value, axis, 2), minus]


def swap_core(value):
    return lax.ppermute(value, "core", [(0, 1), (1, 0)])


def to_class_plane(value):
    moves = []
    for z in range(4):
        for core in range(2):
            for y in range(4):
                moves.append(
                    ((z * 2 + core) * 4 + y, (y * 2 + core) * 4 + (z + 2 * core) % 4)
                )
    return lax.ppermute(value, ("z", "core", "grp"), moves)


def joined(held, got, extra=0):
    count, rows, columns = held.shape
    both = jnp.zeros((2 * count, rows + extra, columns), held.dtype)
    both = lax.optimization_barrier(lax.dynamic_update_slice(both, held, (0, 0, 0)))
    return lax.dynamic_update_slice(both, got, (count, 0, 0))


def plane_gather(half_a, half_b):
    a, b = lax.optimization_barrier(
        (jnp.stack(ring(half_a, "x")), jnp.stack(ring(half_b, "z")))
    )
    return ring(a, "z"), ring(b, "x")


def reduce_core_y(own, other, y, dtype):
    other = swap_core(other)
    pieces = []
    for d in range(4):
        first = 4 * ((y + d) % 4)
        pieces.append(
            lax.dynamic_slice_in_dim(own, first, 4, 0)
            + lax.dynamic_slice_in_dim(other, first, 4, 0)
        )
    result = pieces[0]
    for d in (1, 3, 2):
        arrived = shifted(pieces[d].astype(dtype), "grp", 4 - d)
        result = result + arrived.astype(F32)
    return result


def on_device(
    coefficients,
    domain,
    coupling_owner,
    coupling_slot,
    coupling_fock,
    exchange_integrals,
    pno_energy,
    pair_shift,
    amplitudes_start,
):
    z, x, core, y = [lax.axis_index(name) for name in ("z", "x", "core", "grp")]
    class_z = (y + 2 * core) % 4
    flat = coefficients.reshape(PAIRS * PNO, PNO)
    local = (domain - y * NB).astype(BF16)
    start = lax.dynamic_slice_in_dim(amplitudes_start, 4 * y, 4, 0).astype(BF16)
    start = start.reshape(4 * PNO, PNO)
    flat_in = to_class_plane(flat)
    start_in = to_class_plane(jnp.concatenate([start, local]))
    local_in = start_in[4 * PNO :]
    colours = []
    for k in range(4):
        rows = [
            flat_in[k * ORBITALS : (k + 1) * ORBITALS],
            start_in[k * PNO : (k + 1) * PNO],
        ]
        if k == 0:
            rows.append(local_in)
        colours.append(jnp.concatenate(rows)[None])

    table = jnp.stack(
        [(coupling_owner * PAIRS + coupling_slot).astype(F32), coupling_fock]
    ).reshape(2, -1)
    tables = jnp.stack([table, swap_core(table)])
    rest = jnp.concatenate([tables[1], jnp.zeros((PAIRS - 2, PNO), F32)]).astype(BF16)
    plain_targets = jnp.concatenate([flat, local])
    other_plain = swap_core(plain_targets)
    arrived = [flat_in[:PAIRS], start_in[:PAIRS], rest, other_plain[:PAIRS]]
    own_targets = jnp.concatenate([plain_targets, *arrived])
    targets = [own_targets]
    for d in range(3):
        targets.append(shifted(targets[-1], "grp", 1))
    targets += [other_plain] + [swap_core(rows) for rows in targets[1:]]
    packed = pack_couplings(tables[:, 0].astype(jnp.int32), z, x, core, class_z)

    for step in range(3):
        got = [lax.ppermute(colours[k], *STEPS[k][step]) for k in range(4)]
        if step == 2:
            held_domains = joined(colours[0][:, COLOUR:], got[0][:, COLOUR:])
            got_domains = lax.ppermute(held_domains, *STEPS[0][3])
            last = joined(colours[3], got[3], extra=PAIRS)
            last = lax.dynamic_update_slice(last, got_domains, (0, COLOUR, 0))
        colours = [joined(colours[k], got[k]) for k in range(4)]
    colours[3] = last
    got = [lax.ppermute(colours[k], *STEPS[k][3]) for k in range(4)]
    lists = []
    for k in range(4):
        lists.append(colours[k].reshape(2, 2, 2, -1, PNO))
        lists.append(got[k].reshape(2, 2, 2, -1, PNO))

    even, odd = ways((y + jnp.arange(RANGES, dtype=jnp.int32) - z) % 4, z)
    place = even + 2 * odd
    info, fock, picked = pl.pallas_call(
        pick_kernel,
        out_shape=(
            jax.ShapeDtypeStruct((8, LINKS), jnp.int32),
            jax.ShapeDtypeStruct((1, LINKS + 1), F32),
            jax.ShapeDtypeStruct((LINKS, PNO, RANGES * PNO), BF16),
        ),
        in_specs=[SM, SM, SM] + [VM] * 10,
        out_specs=(SM, SM, VM),
        scratch_shapes=[
            pltpu.VMEM((2 * PAIRS, RANGES, PNO, NB), BF16),
            pltpu.VMEM((2 * RANGES, PAIRS, PNO), F32),
            pltpu.VMEM((2, 8, PAIRS, PNO), F32),
            pltpu.SMEM((LINKS + 1,), jnp.int32),
        ],
        compiler_params=params(22),
        name="pick_targets",
    )(place.astype(jnp.int32), packed, tables, held_domains, got_domains, *targets)

    inter, own, other = pl.pallas_call(
        first_kernel,
        out_shape=(jax.ShapeDtypeStruct((LINKS, PNO, PNO), BF16), BLOCK, BLOCK),
        in_specs=[SM, SM] + [HB] * 8 + [VM],
        out_specs=(pl.BlockSpec(memory_space=pltpu.HBM), VM, VM),
        scratch_shapes=[
            pltpu.VMEM((LINKS, 2, 2, PNO, PNO), BF16),
            pltpu.VMEM((LINKS, PNO, PNO), BF16),
            pltpu.VMEM((2 * PAIRS, PNO, PNO), F32),
            pltpu.VMEM((LINKS, PNO, PNO), BF16),
            pltpu.SemaphoreType.DMA((LINKS,)),
            pltpu.SemaphoreType.DMA((LINKS,)),
            pltpu.SemaphoreType.DMA,
        ],
        compiler_params=params(19),
        name="intersect_and_project",
    )(info, fock, *lists, picked)

    energy = lax.dynamic_slice_in_dim(pno_energy, 4 * y, 4, 0)
    shift = lax.dynamic_slice_in_dim(pair_shift, 4 * y, 4, 0)
    exchange = lax.dynamic_slice_in_dim(exchange_integrals, 4 * y, 4, 0)
    denominator = energy[:, :, None] + energy[:, None, :] + shift[:, None, None]

    amplitudes = -(exchange + reduce_core_y(own, other, y, F32)) / denominator
    sent = to_class_plane(amplitudes.astype(BF16).reshape(4 * PNO, PNO))
    a_refs, b_refs = plane_gather(sent[: 2 * PNO], sent[2 * PNO :])
    own, other = pl.pallas_call(
        next_kernel,
        out_shape=(BLOCK, BLOCK),
        in_specs=[SM, SM] + [VM] * 9,
        out_specs=(VM, VM),
        scratch_shapes=[
            pltpu.VMEM((LINKS, PNO, PNO), BF16),
            pltpu.VMEM((2 * PAIRS, PNO, PNO), F32),
        ],
        compiler_params=params(12),
        name="project",
    )(info, fock, inter, *a_refs, *b_refs)
    amplitudes = -(exchange + reduce_core_y(own, other, y, BF16)) / denominator
    amplitudes = lax.reduce_precision(amplitudes, exponent_bits=8, mantissa_bits=7)
    gathered = ring(amplitudes.astype(BF16), "grp")
    result = jnp.zeros_like(exchange_integrals)
    for d in range(4):
        piece = gathered[d].astype(F32)
        result = lax.dynamic_update_slice_in_dim(result, piece, 4 * ((y + d) % 4), 0)
    return result


def solution(mesh):
    fine = Mesh(mesh.devices.reshape(4, 4, 2, 4), ("z", "x", "core", "grp"))
    placed = (
        P(SPLIT, "grp", None),
        P(SPLIT, "grp"),
        P(SPLIT, None),
        P(SPLIT, None),
        P(SPLIT, None),
        P(SPLIT, None, None),
        P(SPLIT, None),
        P(SPLIT),
        P(SPLIT, None, None),
    )
    return jax.shard_map(
        on_device, mesh=fine, in_specs=placed, out_specs=P(SPLIT, None, None), check_vma=False
    )
```
